32 devices in a mesh: batch: 4 (over z), seq: 8 (over y, x, core).
Axes of the slice: x: 2, y: 2, z: 4, core: 2. Of those that a mesh axis runs over, the one named last changes fastest.
Arguments:
- tokens: bfloat16 [4, 2048, 512], P('batch', 'seq'), may hold values from -6 to 6
- cotangent: bfloat16 [4, 2048, 512], P('batch', 'seq'), may hold values from -6 to 6
- item_start: int32 [4, 2], P('batch'), may hold values from 0 to 1024, as said below
- first_gain: float32 [512], replicated, may hold values from 0.5 to 1.5
- first_shift: float32 [512], replicated, may hold values from -4 to 4
- query_weight: bfloat16 [512, 512], replicated, may hold values from -0.25 to 0.25
- query_bias: float32 [512], replicated, may hold values from -4 to 4
- key_weight: bfloat16 [512, 512], replicated, may hold values from -0.25 to 0.25
- value_weight: bfloat16 [512, 512], replicated, may hold values from -0.25 to 0.25
- value_bias: float32 [512], replicated, may hold values from -4 to 4
- out_weight: bfloat16 [512, 512], replicated, may hold values from -0.75 to 0.75
- out_bias: float32 [512], replicated, may hold values from -4 to 4
- second_gain: float32 [512], replicated, may hold values from 0.5 to 1.5
- second_shift: float32 [512], replicated, may hold values from -4 to 4
- up_weight: bfloat16 [512, 2048], replicated, may hold values from -0.25 to 0.25
- up_bias: float32 [2048], replicated, may hold values from -4 to 4
- down_weight: bfloat16 [2048, 512], replicated, may hold values from -0.125 to 0.125
- down_bias: float32 [512], replicated, may hold values from -4 to 4
Outputs:
- output: bfloat16 [4, 2048, 512], P('batch', 'seq')
- grad_tokens: float32 [4, 2048, 512], P('batch', 'seq')
- grad_query_weight: float32 [512, 512], replicated
- grad_key_weight: float32 [512, 512], replicated
- grad_value_weight: float32 [512, 512], replicated
- grad_out_weight: float32 [512, 512], replicated
- grad_up_weight: float32 [512, 2048], replicated
- grad_down_weight: float32 [2048, 512], replicated
- grad_query_bias: float32 [512], replicated
- grad_value_bias: float32 [512], replicated
- grad_out_bias: float32 [512], replicated
- grad_up_bias: float32 [2048], replicated
- grad_down_bias: float32 [512], replicated
- grad_first_gain: float32 [512], replicated
- grad_first_shift: float32 [512], replicated
- grad_second_gain: float32 [512], replicated
- grad_second_shift: float32 [512], replicated
The draws below stay inside these ranges and needn't reach their ends.
Inputs may be any that keep to these rules, and one draw needn't show every extreme that they name: `item_start`: A stream is either one item of 2048 tokens or items of 1024 tokens each; some stream of every draw is one item, and some other is made of short items.
All inputs are finite; a program needn't handle non-finite values.
Results may differ from the reference program's by a relative error of at most 0.012.
Values may be sent and summed in bfloat16 or wider, within the bound.
No kernel may reach another device: no remote copies, remote signals or barrier semaphores. Data moves between devices by JAX's collectives and lax.ppermute only.
A program may use at most 320 MiB of HBM per device.

```python
import math
import jax
import jax.numpy as jnp
from jax import lax

D = 512
HEADS = 8
FF = 2048
BLOCK = 16
UNIT = 1024
BATCH = 4
STREAM = 2048
MAXLEN = 2048
UNITS = 2
LEVELS = 5


def draw_item_start(key, part):
    key = jax.random.fold_in(key, 11)
    key_long, key_pick = jax.random.split(key)
    longs = jax.random.randint(key_long, (BATCH,), 0, 2)
    order = jax.random.permutation(key_pick, BATCH)
    longs = longs.at[order[0]].set(1)
    longs = longs.at[order[1]].set(0)
    unit_ids = jnp.arange(UNITS, dtype=jnp.int32)
    starts = jnp.where(longs[:, None] == 1, 0, unit_ids[None, :] * UNIT)
    return starts.astype(jnp.int32)


def levels(rng, dims, cuts, low, top_value):
    def one(axis_at, parts):
        heights = jax.random.uniform(jax.random.fold_in(jax.random.fold_in(rng, 6), axis_at), (parts,), jnp.float32, low / len(cuts), top_value / len(cuts))
        return jnp.repeat(jnp.exp(heights), dims[axis_at] // parts).reshape((-1,) + (1,) * (len(dims) - axis_at - 1))

    level = one(*cuts[0])
    for cut in cuts[1:]:
        level = level * one(*cut)
    return level


def bell_draw(rng, dims, width, reach, shards=(), held_as=jnp.bfloat16):
    values = jax.random.normal(rng, dims, jnp.float32) * width
    if len(shards) > 0:
        values = levels(rng, dims, shards, -0.22, 0.18) * values
    return jnp.clip(values, min=-reach, max=reach).astype(held_as)


def setup_inputs(seed: int = 0) -> dict:
    key_list = jax.random.split(jax.random.key(seed), 19)
    tokens = bell_draw(key_list[0], (BATCH, STREAM, D), 1.0, 6.0, ((0, 4), (1, 8)))
    cotangent = bell_draw(key_list[1], (BATCH, STREAM, D), 1.0, 6.0, ((0, 4), (1, 8)))
    item_start = draw_item_start(jax.random.fold_in(key_list[18], 71), 0)
    first_gain = jnp.clip(1.0 + 0.1 * jax.random.normal(key_list[3], (D,), jnp.float32), 0.5, 1.5)
    first_shift = bell_draw(key_list[4], (D,), 0.3, 4.0, (), jnp.float32)
    query_weight = bell_draw(key_list[5], (D, D), D ** -0.5, 0.25)
    query_bias = bell_draw(key_list[6], (D,), 0.3, 4.0, (), jnp.float32)
    key_weight = bell_draw(key_list[7], (D, D), D ** -0.5, 0.25)
    value_weight = bell_draw(key_list[8], (D, D), D ** -0.5, 0.25)
    value_bias = bell_draw(key_list[9], (D,), 0.3, 4.0, (), jnp.float32)
    out_weight = bell_draw(key_list[10], (D, D), (D // 8) ** -0.5, 0.75)
    out_bias = bell_draw(key_list[11], (D,), 0.3, 4.0, (), jnp.float32)
    second_gain = jnp.clip(1.0 + 0.1 * jax.random.normal(key_list[12], (D,), jnp.float32), 0.5, 1.5)
    second_shift = bell_draw(key_list[13], (D,), 0.3, 4.0, (), jnp.float32)
    up_weight = bell_draw(key_list[14], (D, FF), D ** -0.5, 0.25)
    up_bias = bell_draw(key_list[15], (FF,), 0.3, 4.0, (), jnp.float32)
    down_weight = bell_draw(key_list[16], (FF, D), FF ** -0.5, 0.125)
    down_bias = bell_draw(key_list[17], (D,), 0.3, 4.0, (), jnp.float32)
    return dict(tokens=tokens, cotangent=cotangent, item_start=item_start, first_gain=first_gain, first_shift=first_shift, query_weight=query_weight, query_bias=query_bias, key_weight=key_weight, value_weight=value_weight, value_bias=value_bias, out_weight=out_weight, out_bias=out_bias, second_gain=second_gain, second_shift=second_shift, up_weight=up_weight, up_bias=up_bias, down_weight=down_weight, down_bias=down_bias)


NORM_EPS = 1e-05
LOG_TWO = math.log(2.0)

@jax.custom_vjp
def low(v):
    return lax.optimization_barrier(v.astype(jnp.bfloat16)).astype(jnp.float32)

@jax.custom_vjp
def low_back(v):
    return v

def low_keep(v):
    return (low(v), None)

def low_pass(kept, grad):
    return (grad,)

def back_keep(v):
    return (v, None)

def back_low(kept, grad):
    return (low(grad),)
low.defvjp(low_keep, low_pass)
low_back.defvjp(back_keep, back_low)

def exact_product(left, right):
    return jnp.dot(left, right, precision=lax.Precision.HIGHEST)

def layer_norm(values, gain, shift):
    centre = lax.optimization_barrier(jnp.mean(values, axis=-1, keepdims=True))
    centred = values - centre
    spread = lax.optimization_barrier(jnp.mean(centred * centred, axis=-1, keepdims=True))
    return centred * lax.rsqrt(spread + NORM_EPS) * gain + shift

def banded(padded, row_count):
    blocks = row_count // BLOCK
    sections = [padded[offset * BLOCK:offset * BLOCK + row_count].reshape((blocks, BLOCK) + padded.shape[1:]) for offset in range(3)]
    return jnp.concatenate(sections, axis=1)

def stream_forward(stream_tokens, stream_starts, weights):
    first_gain, first_shift, query_weight, query_bias, key_weight, value_weight, value_bias, out_weight, out_bias, second_gain, second_shift, up_weight, up_bias, down_weight, down_bias = weights
    stream_len, model_width = stream_tokens.shape
    head_dim = model_width // HEADS
    score_scale = 1.0 / math.sqrt(head_dim)
    token_start = jnp.repeat(stream_starts, UNIT, total_repeat_length=stream_len)
    low_first = low(layer_norm(stream_tokens, first_gain, first_shift))
    query = low(low_back(exact_product(low_first, query_weight) + query_bias))
    key_rows = low(low_back(exact_product(low_first, key_weight)))
    value_rows = low(low_back(exact_product(low_first, value_weight) + value_bias))
    pooled_keys = []
    pooled_values = []
    for level_id in range(1, LEVELS + 1):
        pool_size = 2 ** level_id
        pool_rows = stream_len // pool_size
        pooled_keys.append(low(lax.optimization_barrier(jnp.mean(key_rows.reshape(pool_rows, pool_size, model_width), axis=1))))
        pooled_values.append(low(lax.optimization_barrier(jnp.mean(value_rows.reshape(pool_rows, pool_size, model_width), axis=1))))
    key_pad = jnp.pad(key_rows, ((BLOCK, BLOCK), (0, 0)))
    value_pad = jnp.pad(value_rows, ((BLOCK, BLOCK), (0, 0)))
    start_pad = jnp.pad(token_start, (BLOCK, BLOCK), constant_values=-1)
    blocks = UNIT // BLOCK

    def unit_attention(unit_id):
        row_low = unit_id * UNIT
        own_start = stream_starts[unit_id]
        query_rows = lax.dynamic_slice_in_dim(query, row_low, UNIT, 0).reshape(UNIT, HEADS, head_dim)
        key_band = banded(lax.dynamic_slice_in_dim(key_pad, row_low, UNIT + 2 * BLOCK, 0), UNIT).reshape(blocks, 3 * BLOCK, HEADS, head_dim)
        value_band = banded(lax.dynamic_slice_in_dim(value_pad, row_low, UNIT + 2 * BLOCK, 0), UNIT).reshape(blocks, 3 * BLOCK, HEADS, head_dim)
        near_mask = banded(lax.dynamic_slice_in_dim(start_pad, row_low, UNIT + 2 * BLOCK, 0), UNIT) == own_start
        query_blocks = query_rows.reshape(blocks, BLOCK, HEADS, head_dim)
        near_score = jnp.einsum('iahe,ibhe->hiab', query_blocks, key_band, precision=lax.Precision.HIGHEST) * score_scale
        near_score = jnp.where(near_mask[None, :, None, :], low_back(near_score), -jnp.inf)
        window_start = jnp.minimum(own_start, stream_len - MAXLEN)
        far_keys = []
        far_values = []
        far_places = []
        far_levels = []
        for level_id in range(1, LEVELS + 1):
            pool_size = 2 ** level_id
            pool_rows = MAXLEN // pool_size
            index_low = window_start // pool_size
            far_keys.append(lax.dynamic_slice_in_dim(pooled_keys[level_id - 1], index_low, pool_rows, 0))
            far_values.append(lax.dynamic_slice_in_dim(pooled_values[level_id - 1], index_low, pool_rows, 0))
            far_places.append((index_low + jnp.arange(pool_rows, dtype=jnp.int32)) * pool_size)
            far_levels.append(jnp.full((pool_rows,), level_id, jnp.int32))
        far_key = jnp.concatenate(far_keys, axis=0).reshape(-1, HEADS, head_dim)
        far_value = jnp.concatenate(far_values, axis=0).reshape(-1, HEADS, head_dim)
        far_pos = jnp.concatenate(far_places)
        far_level = jnp.concatenate(far_levels)
        far_span = BLOCK * jnp.left_shift(jnp.int32(1), far_level)
        query_pos = row_low + jnp.arange(UNIT, dtype=jnp.int32) - own_start
        query_block = query_pos[:, None] // far_span[None, :]
        far_block = (far_pos - own_start) // far_span
        parent_gap = far_block[None, :] // 2 - query_block // 2
        far_mask = (token_start[far_pos] == own_start)[None, :] & (jnp.abs(parent_gap) <= 1) & (jnp.abs(far_block[None, :] - query_block) >= 2)
        far_bias = far_level.astype(jnp.float32) * LOG_TWO
        far_score = jnp.einsum('the,rhe->htr', query_rows, far_key, precision=lax.Precision.HIGHEST) * score_scale + far_bias
        far_score = jnp.where(far_mask[None], low_back(far_score), -jnp.inf)
        near_rows = near_score.reshape(HEADS, UNIT, 3 * BLOCK)
        row_top = jnp.maximum(lax.optimization_barrier(jnp.max(near_rows, axis=2)), lax.optimization_barrier(jnp.max(far_score, axis=2)))
        row_total = lax.optimization_barrier(jnp.sum(jnp.exp(near_rows - row_top[:, :, None]), axis=2)) + lax.optimization_barrier(jnp.sum(jnp.exp(far_score - row_top[:, :, None]), axis=2))
        log_total = row_top + jnp.log(row_total)
        near_weight = low(jnp.exp(near_score - log_total.reshape(HEADS, blocks, BLOCK, 1)))
        far_weight = low(jnp.exp(far_score - log_total[:, :, None]))
        mixed = jnp.einsum('hiab,ibhe->iahe', near_weight, value_band, precision=lax.Precision.HIGHEST).reshape(UNIT, model_width)
        mixed = mixed + jnp.einsum('htr,rhe->the', far_weight, far_value, precision=lax.Precision.HIGHEST).reshape(UNIT, model_width)
        return low(low_back(mixed))
    unit_count = stream_len // UNIT
    attended = lax.map(jax.checkpoint(unit_attention), jnp.arange(unit_count, dtype=jnp.int32)).reshape(stream_len, model_width)
    mid = stream_tokens + low_back(exact_product(attended, out_weight) + out_bias)
    low_second = low(layer_norm(mid, second_gain, second_shift))
    upper = low_back(exact_product(low_second, up_weight) + up_bias)
    active = low(jax.nn.gelu(upper, approximate=False))
    return mid + low_back(exact_product(active, down_weight) + down_bias)

def reference(tokens, cotangent, item_start, first_gain, first_shift, query_weight, query_bias, key_weight, value_weight, value_bias, out_weight, out_bias, second_gain, second_shift, up_weight, up_bias, down_weight, down_bias):
    weights = (first_gain, first_shift, query_weight.astype(jnp.float32), query_bias, key_weight.astype(jnp.float32), value_weight.astype(jnp.float32), value_bias, out_weight.astype(jnp.float32), out_bias, second_gain, second_shift, up_weight.astype(jnp.float32), up_bias, down_weight.astype(jnp.float32), down_bias)

    def forward(all_tokens, *params):

        def one_stream(paired):
            return stream_forward(paired[0], paired[1], params)
        return lax.map(one_stream, (all_tokens, item_start))
    result, pullback = jax.vjp(forward, tokens.astype(jnp.float32), *weights)
    grads = pullback(cotangent.astype(jnp.float32))
    grad_input = grads[0]
    grad_params = grads[1:]
    return (result.astype(jnp.bfloat16), grad_input, grad_params[2], grad_params[4], grad_params[5], grad_params[7], grad_params[11], grad_params[13], grad_params[3], grad_params[6], grad_params[8], grad_params[12], grad_params[14], grad_params[0], grad_params[1], grad_params[9], grad_params[10])
```

```python
import functools
import math

import jax
import jax.numpy as jnp
import numpy as np
from jax import lax
from jax.experimental import pallas as pl
from jax.experimental.pallas import tpu as pltpu
from jax.sharding import PartitionSpec as P

HEADS = 8
BLOCK = 16
UNIT = 1024
ROWS = 256
SUB = 64
QUAD = 4
HALO = 112
LOCAL = 3
GATHER = 32
NEAR_COLS = 256
PIECES = 32
SMALL = 16

NORM_EPS = 1e-05
LOG_TWO = math.log(2.0)
NEVER = -1e30
F32 = jnp.float32
BF16 = jnp.bfloat16
VMEM_LIMIT = 56 * 1024 * 1024


def dot(left, right):
    return jnp.dot(left, right, preferred_element_type=F32)


def dot_rows(left, right):
    return lax.dot_general(left, right, (((0,), (0,)), ((), ())), preferred_element_type=F32)


def dot_cols(left, right):
    return lax.dot_general(left, right, (((1,), (1,)), ((), ())), preferred_element_type=F32)


def two_parts(values):
    high = values.astype(BF16)
    return high, (values - high.astype(F32)).astype(BF16)


def normalize(values):
    centred = values - jnp.mean(values, axis=-1, keepdims=True)
    spread = jnp.mean(centred * centred, axis=-1, keepdims=True)
    scale = lax.rsqrt(spread + NORM_EPS)
    return centred * scale, scale


def norm_back(grad, normed, scale):
    return scale * (
        grad
        - jnp.mean(grad, axis=-1, keepdims=True)
        - normed * jnp.mean(grad * normed, axis=-1, keepdims=True)
    )


def normal_parts(upper):
    far = jnp.abs(upper) * math.sqrt(0.5)
    t = 1.0 / (1.0 + 0.5 * far)
    series = (
        -1.26551223,
        1.00002368,
        0.37409196,
        0.09678418,
        -0.18628806,
        0.27886807,
        -1.13520398,
        1.48851587,
        -0.82215223,
        0.17087277,
    )
    power = jnp.full_like(t, series[-1])
    for term in series[-2::-1]:
        power = power * t + term
    square = far * far
    half_tail = 0.5 * t * jnp.exp(power - square)
    phi = jnp.exp(-square) * (1.0 / math.sqrt(2.0 * math.pi))
    return jnp.where(upper < 0.0, half_tail, 1.0 - half_tail), phi


def level_rows(level):
    return ROWS >> level


def pool_matrix(levels):
    matrix = np.zeros((ROWS, ROWS), np.float32)
    at = 0
    for level in range(1, levels + 1):
        size = 1 << level
        for row in range(level_rows(level)):
            matrix[at + row, row * size : (row + 1) * size] = 1.0 / size
        at += level_rows(level)
    return matrix


POOL_AT = {1: 0, 2: 128, 3: 192}
POOLED = 224
HALO_AT = {0: (0, 16), 1: (16, 32), 2: (48, 32), 3: (80, 32)}


def key_list(sub, levels):
    out = []

    def add(column, level, first, last):
        own = level_rows(level)
        base, width = HALO_AT[level]
        low = min(last, 0)
        if first < low:
            out.append((column, low - first, "halo", base + width + first, 1))
            column += low - first
            first = low
        mid = min(last, own)
        if first < mid:
            if level == 0:
                out.append((column, mid - first, "own", first, 0))
            else:
                out.append((column, mid - first, "pool", POOL_AT[level] + first, 0))
            column += mid - first
            first = mid
        if first < last:
            out.append((column, last - first, "halo", HALO + base + first - own, 2))

    start = SUB * sub
    add(0, 0, start - 16, start + SUB + 16)
    row = 32 * sub
    add(96, 1, row - 32, row)
    add(128, 1, row + 32, row + 64)
    row = 32 * (sub // 2)
    add(160, 2, row - 32, row - 16)
    third = row + 32 if sub % 2 == 0 else row - 16
    add(176, 2, third, third + 16)
    add(192, 2, row + 48, row + 64)
    add(208, 3, -32, -16)
    third = 32 if sub < 2 else -16
    add(224, 3, third, third + 16)
    add(240, 3, 48, 64)
    far = 48 * (levels - LOCAL)
    out.append((NEAR_COLS, far, "halo", 2 * HALO, 3))
    return out


def columns_of(levels):
    return -(-(NEAR_COLS + 48 * (levels - LOCAL)) // 128) * 128


def score_bias(levels):
    cols = columns_of(levels)
    bias = np.full((SUB, cols), NEVER, np.float32)
    block = np.arange(SUB) // BLOCK
    for col in range(96):
        bias[:, col] = np.where(np.abs(col // BLOCK - 1 - block) <= 1, 0.0, NEVER)
    bias[:, 96:160] = LOG_TWO
    bias[:32, 112:128] = NEVER
    bias[32:, 128:144] = NEVER
    bias[:, 160:208] = 2 * LOG_TWO
    bias[:, 208:256] = 3 * LOG_TWO
    for level in range(LOCAL + 1, levels + 1):
        at = NEAR_COLS + 48 * (level - LOCAL - 1)
        bias[:, at : at + 48] = level * LOG_TWO
    return bias


def column_codes(levels):
    codes = np.zeros((8, columns_of(levels)), np.int32)
    for sub in range(ROWS // SUB):
        for column, rows, _, _, code in key_list(sub, levels):
            if code == 3:
                codes[sub, column : column + rows] = 3 + np.arange(rows) // BLOCK
            else:
                codes[sub, column : column + rows] = code
    return codes


def gather_at(level):
    return sum(level_rows(other) for other in range(LOCAL + 1, level))


def item_bounds(starts, place):
    unit = place * ROWS // UNIT
    low = starts[0, unit]
    count = jnp.int32(0)
    for other in range(starts.shape[1]):
        count = count + jnp.where(starts[0, other] == low, 1, 0).astype(jnp.int32)
    return low, low + count * UNIT


def far_blocks(place, levels):
    out = []
    for level in range(LOCAL + 1, levels + 1):
        mine = place * ROWS // (BLOCK << level)
        parent = mine // 2
        odd = mine - 2 * parent
        third = jnp.where(odd == 1, 2 * parent - 1, 2 * parent + 2)
        out.append((level, (2 * parent - 2, third, 2 * parent + 3)))
    return out


def pick_matrix(place, levels, holders):
    rows = []
    column = lax.broadcasted_iota(jnp.int32, (48, holders * GATHER), 1)
    line = lax.broadcasted_iota(jnp.int32, (48, holders * GATHER), 0)
    for level, blocks in far_blocks(place, levels):
        part = line // BLOCK
        block = jnp.where(part == 0, blocks[0], jnp.where(part == 1, blocks[1], blocks[2]))
        row = block * BLOCK + (line - part * BLOCK)
        shift = 8 - level
        owner = lax.shift_right_arithmetic(row, jnp.int32(shift))
        inside = row - owner * (1 << shift)
        wanted = owner * GATHER + gather_at(level) + inside
        rows.append(jnp.where(column == wanted, 1.0, 0.0))
    return jnp.concatenate(rows, axis=0).astype(BF16)


def head_masks(quad_cols, rows):
    lane = lax.broadcasted_iota(jnp.int32, (rows, quad_cols), 1)
    width = quad_cols // QUAD
    return [(lane >= width * h) & (lane < width * (h + 1)) for h in range(QUAD)]


def stack_heads(block, masks):
    zero = jnp.zeros_like(block)
    return jnp.concatenate([jnp.where(mask, block, zero) for mask in masks], axis=0)


def unstack_heads(block, masks):
    total = None
    for h, mask in enumerate(masks):
        part = jnp.where(mask, block[SUB * h : SUB * (h + 1)], 0.0)
        total = part if total is None else total + part
    return total


def my_piece():
    return (
        (lax.axis_index("seq") % 2) * 16
        + ((lax.axis_index("seq") // 2) % 4) * 4
        + lax.axis_index("batch") % 4
    )


def first_kernel(tokens, gain, shift, pool, normed_out, next_out, prev_out, gather_out):
    normed, _ = normalize(tokens[0].astype(F32))
    normed_out[...] = (normed * gain[...] + shift[...]).astype(BF16)
    high, low = two_parts(normed)
    pooled = (dot(pool[...], high) + dot(pool[...], low)).astype(BF16)
    next_out[0:16] = high[ROWS - 16 :]
    prev_out[0:16] = high[:16]
    for level in range(1, LOCAL + 1):
        at, width = HALO_AT[level]
        base = POOL_AT[level]
        next_out[at : at + width] = pooled[base + level_rows(level) - width : base + level_rows(level)]
        prev_out[at : at + width] = pooled[base : base + width]
    gather_out[...] = pooled[POOLED:]


def project_kernel(
    normed, query_w, query_b, key_w, value_w, value_b, pool,
    query_out, key_out, value_out, key_pool, value_pool,
):
    rows = normed[...]
    query = (dot(rows, query_w[...]) + query_b[...]).astype(BF16)
    query_out[...] = query * jnp.asarray(0.125, BF16)
    key = dot(rows, key_w[...]).astype(BF16)
    value = (dot(rows, value_w[...]) + value_b[...]).astype(BF16)
    key_out[...] = key
    value_out[...] = value
    key_pool[...] = dot(pool[:POOLED], key).astype(BF16)
    value_pool[...] = dot(pool[:POOLED], value).astype(BF16)


def fill_keys(sub, levels, target, own, pool, halo):
    cols = columns_of(levels)
    used = NEAR_COLS + 48 * (levels - LOCAL)
    sources = {"own": own, "pool": pool, "halo": halo}
    for column, rows, source, row, _ in key_list(sub, levels):
        target[column : column + rows] = sources[source][row : row + rows]
    if cols > used:
        target[used:] = jnp.zeros((cols - used, target.shape[1]), BF16)


def middle_kernel(
    levels, holders,
    starts, tokens, cotangent, query, key, value, key_pool, value_pool, from_prev, from_next,
    window, gain, shift, key_w, value_w, value_b, out_w, out_b, gain2, shift2, up_w, up_b,
    down_w, down_b, bias_table, codes,
    output, attended_out, weights_out, halo_out, key_halo, value_halo, grad_mid_out, sums_out,
    key_cat, value_cat, attended, sums, small,
):
    width = tokens.shape[2]
    place = lax.axis_index("seq")
    low, high = item_bounds(starts, place)
    far = 48 * (levels - LOCAL)

    halo_out[0:HALO] = from_prev[...]
    halo_out[HALO : 2 * HALO] = from_next[...]
    halo_out[2 * HALO :] = dot(pick_matrix(place, levels, holders), window[...]).astype(BF16)
    scaled = (halo_out[...].astype(F32) * gain[...]).astype(BF16)
    shift_high, shift_low = two_parts(jnp.broadcast_to(shift[...], (16, width)))
    key_shift = (dot(shift_high, key_w[...]) + dot(shift_low, key_w[...]))[0:1]
    value_shift = (dot(shift_high, value_w[...]) + dot(shift_low, value_w[...]))[0:1]
    key_halo[...] = (dot(scaled, key_w[...]) + key_shift).astype(BF16)
    value_halo[...] = (dot(scaled, value_w[...]) + (value_shift + value_b[...])).astype(BF16)

    code = codes[...]
    allowed = [
        jnp.where(place * ROWS > low, 0.0, NEVER).astype(F32),
        jnp.where(place * ROWS + ROWS < high, 0.0, NEVER).astype(F32),
    ]
    for level, blocks in far_blocks(place, levels):
        span = BLOCK << level
        for block in blocks:
            inside = (block * span >= low) & (block * span + span <= high)
            allowed.append(jnp.where(inside, 0.0, NEVER).astype(F32))
    column_bias = jnp.zeros(code.shape, F32)
    for number, value_of in enumerate(allowed):
        column_bias = jnp.where(code == number + 1, value_of, column_bias)

    quad_cols = width * QUAD // HEADS
    masks = head_masks(quad_cols, SUB)
    for sub in range(ROWS // SUB):
        fill_keys(sub, levels, key_cat, key, key_pool, key_halo)
        fill_keys(sub, levels, value_cat, value, value_pool, value_halo)
        bias = bias_table[...] + column_bias[sub : sub + 1]
        bias = jnp.concatenate([bias] * QUAD, axis=0)
        for quad in range(HEADS // QUAD):
            lanes = slice(quad * quad_cols, (quad + 1) * quad_cols)
            stacked = stack_heads(query[SUB * sub : SUB * (sub + 1), lanes], masks)
            score = dot_cols(stacked, key_cat[:, lanes]) + bias
            score = jnp.exp(score - jnp.max(score, axis=1, keepdims=True))
            weight = score * (1.0 / jnp.sum(score, axis=1, keepdims=True))
            weight = weight.astype(BF16)
            weights_out[sub * (HEADS // QUAD) + quad] = weight
            mixed = unstack_heads(dot(weight, value_cat[:, lanes]), masks)
            attended[SUB * sub : SUB * (sub + 1), lanes] = mixed.astype(BF16)

    attended_out[...] = attended[...]
    mid = tokens[0].astype(F32) + dot(attended[...], out_w[...]) + out_b[...]
    normed, scale = normalize(mid)
    low_second = (normed * gain2[...] + shift2[...]).astype(BF16)
    cot = cotangent[0]
    hidden = up_w.shape[1]
    small[...] = jnp.zeros_like(small)

    def put(row, vector):
        for part in range(vector.shape[1] // 128):
            small[row + part : row + part + 1] = vector[:, 128 * part : 128 * (part + 1)]

    result = mid + down_b[...]
    grad_second = jnp.zeros((ROWS, width), F32)
    step = width
    for at in range(0, hidden, step):
        cols = slice(at, at + step)
        upper = dot(low_second, up_w[:, cols]) + up_b[:, cols]
        below, phi = normal_parts(upper)
        active = (upper * below).astype(BF16)
        result = result + dot(active, down_w[cols])
        grad_down = dot_rows(active, cot).astype(BF16)
        for piece in range(at // 64, (at + step) // 64):
            row = 64 * piece - at
            for part in range(width // 128):
                sums[piece, 64 * part : 64 * (part + 1)] = grad_down[
                    row : row + 64, 128 * part : 128 * (part + 1)
                ]
        grad_active = dot_cols(cot, down_w[cols])
        grad_upper = grad_active * (below + upper * phi)
        low_upper = grad_upper.astype(BF16)
        put(4 + at // 128, jnp.sum(low_upper.astype(F32), axis=0, keepdims=True))
        grad_up = dot_rows(low_second, low_upper).astype(BF16)
        for piece in range(PIECES):
            for part in range(step // 128):
                row = 256 + 16 * (at // 128 + part)
                sums[piece, row : row + 16] = grad_up[
                    16 * piece : 16 * (piece + 1), 128 * part : 128 * (part + 1)
                ]
        grad_second = grad_second + dot_cols(low_upper, up_w[:, cols])

    output[0] = result.astype(BF16)
    cot = cot.astype(F32)
    put(0, jnp.sum(cot, axis=0, keepdims=True))
    put(20, jnp.sum(grad_second * normed, axis=0, keepdims=True))
    put(24, jnp.sum(grad_second, axis=0, keepdims=True))
    grad_mid_out[...] = cot + norm_back(grad_second * gain2[...], normed, scale)
    spread_small(sums, 512, small)
    me = my_piece()
    for piece in range(PIECES):
        sums_out[jnp.bitwise_xor(me, piece)] = sums[piece]


def spread_small(sums, row, small):
    for piece in range(PIECES):
        if piece < 2:
            part = small[SMALL * piece : SMALL * (piece + 1)].astype(BF16)
        else:
            part = jnp.zeros((SMALL, 128), BF16)
        sums[piece, row : row + SMALL] = part


def back_kernel(
    levels, holders,
    tokens, normed_low, query, key, value, key_pool, value_pool, halo, key_halo, value_halo,
    weights, attended, grad_mid, gain, shift, query_w, key_w, value_w, out_w, pool,
    grad_normed_out, to_prev, to_next, to_owners, sums_out,
    key_cat, value_cat, grad_query, key_own, key_pooled, key_lent, value_own, value_pooled,
    value_lent, sums, small,
):
    width = tokens.shape[2]
    place = lax.axis_index("seq")
    far = 48 * (levels - LOCAL)
    branch = grad_mid[...].astype(BF16)
    grad_attended = dot_cols(branch, out_w[...]).astype(BF16)
    for ref in (key_own, key_pooled, key_lent, value_own, value_pooled, value_lent):
        ref[...] = jnp.zeros_like(ref)
    key_sums = {"own": key_own, "pool": key_pooled, "halo": key_lent}
    value_sums = {"own": value_own, "pool": value_pooled, "halo": value_lent}

    quad_cols = width * QUAD // HEADS
    masks = head_masks(quad_cols, SUB)
    for sub in range(ROWS // SUB):
        fill_keys(sub, levels, key_cat, key, key_pool, key_halo)
        fill_keys(sub, levels, value_cat, value, value_pool, value_halo)
        rows = slice(SUB * sub, SUB * (sub + 1))
        for quad in range(HEADS // QUAD):
            lanes = slice(quad * quad_cols, (quad + 1) * quad_cols)
            stacked = stack_heads(query[rows, lanes], masks)
            grads = stack_heads(grad_attended[rows, lanes], masks)
            weight = weights[sub * (HEADS // QUAD) + quad]
            prob = weight.astype(F32)
            dprob = dot_cols(grads, value_cat[:, lanes])
            delta = jnp.sum(prob * dprob, axis=1, keepdims=True)
            dscore = (prob * (dprob - delta)).astype(BF16)
            mixed = unstack_heads(dot(dscore, key_cat[:, lanes]), masks)
            grad_query[rows, lanes] = (mixed * 0.125).astype(BF16)
            grad_keys = dot_rows(dscore, stacked)
            grad_values = dot_rows(weight, grads)
            for column, count, source, row, _ in key_list(sub, levels):
                key_sums[source][row : row + count, lanes] += grad_keys[column : column + count]
                value_sums[source][row : row + count, lanes] += grad_values[
                    column : column + count
                ]

    low_query = grad_query[...]
    low_key = (key_own[...] + dot_rows(pool[:POOLED], key_pooled[...].astype(BF16))).astype(BF16)
    low_value = (value_own[...] + dot_rows(pool[:POOLED], value_pooled[...].astype(BF16))).astype(
        BF16
    )
    lent_key = key_lent[...].astype(BF16)
    lent_value = value_lent[...].astype(BF16)
    lent_normed = halo[...].astype(F32)
    lent_low = (lent_normed * gain[...] + shift[...]).astype(BF16)
    rows = normed_low[...]

    def pieces(base, grad):
        grad = grad.astype(BF16)
        for piece in range(PIECES):
            for part in range(width // 128):
                row = base + 16 * part
                sums[piece, row : row + 16] = grad[
                    16 * piece : 16 * (piece + 1), 128 * part : 128 * (part + 1)
                ]

    pieces(0, dot_rows(attended[...], branch))
    pieces(64, dot_rows(rows, low_query))
    pieces(128, dot_rows(rows, low_key) + dot_rows(lent_low, lent_key))
    pieces(192, dot_rows(rows, low_value) + dot_rows(lent_low, lent_value))

    small[...] = jnp.zeros_like(small)

    def put(row, vector):
        for part in range(vector.shape[1] // 128):
            small[row + part : row + part + 1] = vector[:, 128 * part : 128 * (part + 1)]

    def total(values):
        return jnp.sum(values.astype(F32), axis=0, keepdims=True)

    normed, _ = normalize(tokens[0].astype(F32))
    grad_normed = (
        dot_cols(low_query, query_w[...])
        + dot_cols(low_key, key_w[...])
        + dot_cols(low_value, value_w[...])
    )
    lent_grad = dot_cols(lent_key, key_w[...]) + dot_cols(lent_value, value_w[...])
    grad_normed_out[...] = grad_normed
    put(0, total(low_query))
    put(4, total(low_value) + total(lent_value))
    put(8, total(branch))
    put(12, total(grad_normed * normed) + total(lent_grad * lent_normed))
    put(16, total(grad_normed) + total(lent_grad))
    lent_grad = lent_grad.astype(BF16)
    to_prev[...] = lent_grad[:HALO]
    to_next[...] = lent_grad[HALO : 2 * HALO]
    to_owners[...] = dot_rows(pick_matrix(place, levels, holders), lent_grad[2 * HALO :]).astype(
        BF16
    )
    spread_small(sums, 256, small)
    me = my_piece()
    for piece in range(PIECES):
        sums_out[jnp.bitwise_xor(me, piece)] = sums[piece]


def last_kernel(
    tokens, gain, grad_mid, grad_normed, from_prev, from_next, from_users, pool, grad_tokens, pooled
):
    for level in range(1, LOCAL + 1):
        at, width = HALO_AT[level]
        base, own = POOL_AT[level], level_rows(level)
        pooled[base : base + own] = jnp.zeros((own, pooled.shape[1]), F32)
        pooled[base : base + width] += from_prev[at : at + width].astype(F32)
        pooled[base + own - width : base + own] += from_next[at : at + width].astype(F32)
    users = from_users[0].astype(F32)
    for other in range(1, from_users.shape[0]):
        users = users + from_users[other].astype(F32)
    pooled[POOLED:] = users
    high, low = two_parts(pooled[...])
    grad = grad_normed[...] + dot_rows(pool[...], high) + dot_rows(pool[...], low)
    first = from_prev[:16].astype(F32)
    last = from_next[:16].astype(F32)
    gap = jnp.zeros((ROWS - 32, first.shape[1]), F32)
    grad = grad + jnp.concatenate([first, gap, last], axis=0)
    normed, scale = normalize(tokens[0].astype(F32))
    grad_tokens[0] = grad_mid[...] + norm_back(grad * gain[...], normed, scale)


def collect_kernel(kind, *refs):
    blocks, refs = refs[:8], refs[8:]
    me = my_piece()
    if kind == 1:
        down, up, down_b, up_b, gain, shift, small = refs
        small_row = 512
    else:
        out, query, key, value, query_b, value_b, out_b, gain, shift, small = refs
        small_row = 256
    small[...] = jnp.zeros_like(small)
    for core in range(2):
        for quad in range(4):
            for depth in range(4):
                piece = jnp.bitwise_xor(me, core * 16 + quad * 4 + depth)
                block = blocks[core * 4 + quad]
                lines = pl.ds(pl.multiple_of(piece * 16, 16), 16)
                if kind == 1:
                    rows = pl.ds(pl.multiple_of(piece * 64, 64), 64)
                    for part in range(down.shape[1] // 128):
                        down[rows, 128 * part : 128 * (part + 1)] = block[
                            depth, 64 * part : 64 * (part + 1)
                        ].astype(F32)
                    for part in range(up.shape[1] // 128):
                        row = 256 + 16 * part
                        up[lines, 128 * part : 128 * (part + 1)] = block[
                            depth, row : row + 16
                        ].astype(F32)
                else:
                    for number, grad in enumerate((out, query, key, value)):
                        for part in range(grad.shape[1] // 128):
                            row = 64 * number + 16 * part
                            grad[lines, 128 * part : 128 * (part + 1)] = block[
                                depth, row : row + 16
                            ].astype(F32)

                @pl.when(piece < 2)
                def _(block=block, depth=depth, lines=lines):
                    small[lines] = block[depth, small_row : small_row + SMALL].astype(F32)

    if kind == 1:
        order = (down_b, up_b, gain, shift)
    else:
        order = (query_b, value_b, out_b, gain, shift)
    at = 0
    for ref in order:
        ref[...] = small[at : at + ref.shape[0]]
        at += ref.shape[0]


def call(kernel, inputs, outputs, scratch=(), smem=0, flops=0):
    space = [pltpu.SMEM] * smem + [pltpu.VMEM] * (len(inputs) - smem)
    size = sum(math.prod(s) * jnp.dtype(d).itemsize for s, d in outputs)
    size += sum(math.prod(a.shape) * a.dtype.itemsize for a in inputs)
    return pl.pallas_call(
        kernel,
        out_shape=[jax.ShapeDtypeStruct(s, d) for s, d in outputs],
        in_specs=[pl.BlockSpec(memory_space=s) for s in space],
        out_specs=[pl.BlockSpec(memory_space=pltpu.VMEM) for _ in outputs],
        scratch_shapes=[pltpu.VMEM(s, d) for s, d in scratch],
        compiler_params=pltpu.CompilerParams(vmem_limit_bytes=VMEM_LIMIT),
        cost_estimate=pl.CostEstimate(flops=flops, bytes_accessed=size, transcendentals=0),
    )(*inputs)


def swap(array, axis, distance):
    count = lax.axis_size(axis)
    return lax.ppermute(array, axis, [(i, i ^ distance) for i in range(count)])


def shifted(array, axis, by):
    count = lax.axis_size(axis)
    return lax.ppermute(array, axis, [(i, i + by) for i in range(count) if 0 <= i + by < count])


def add(*arrays):
    total = arrays[0].astype(F32)
    for array in arrays[1:]:
        total = total + array.astype(F32)
    return total.astype(BF16)


def sum_pieces(slots):
    rows = slots.shape[1]
    slots = slots.reshape(2, 4, 4, rows, 128)
    other = swap(slots[1], "seq", 1)
    parts = [add(slots[0, quad], other[quad]) for quad in range(4)]
    came = [swap(parts[quad], "seq", 2 * quad) for quad in range(1, 4)]
    depths = [add(*[part[depth] for part in [parts[0]] + came]) for depth in range(4)]
    came = [swap(depths[depth], "batch", depth) for depth in range(1, 4)]
    whole = add(depths[0], *came)
    distance = 8
    while distance < lax.axis_size("seq"):
        whole = add(whole, swap(whole, "seq", distance))
        distance *= 2
    column = jnp.stack([whole] + [swap(whole, "batch", depth) for depth in range(1, 4)])
    plane = [column] + [swap(column, "seq", 2 * quad) for quad in range(1, 4)]
    return plane + [swap(block, "seq", 1) for block in plane]


def on_device(
    tokens, cotangent, item_start, first_gain, first_shift, query_weight, query_bias, key_weight,
    value_weight, value_bias, out_weight, out_bias, second_gain, second_shift, up_weight, up_bias,
    down_weight, down_bias,
):
    width = tokens.shape[2]
    hidden = up_weight.shape[1]
    holders = lax.axis_size("seq")
    levels = (ROWS * holders // (4 * BLOCK)).bit_length() - 1
    far = 48 * (levels - LOCAL)
    lent = 2 * HALO + far
    cols = columns_of(levels)
    groups = (ROWS // SUB) * (HEADS // QUAD)
    pool = jnp.asarray(pool_matrix(levels), BF16)
    bias_table = jnp.asarray(score_bias(levels))
    codes = jnp.asarray(column_codes(levels))

    def row(vector):
        return vector.reshape(1, -1)

    gain, shift = row(first_gain), row(first_shift)
    normed_low, for_next, for_prev, for_all = call(
        first_kernel,
        (tokens, gain, shift, pool),
        [((ROWS, width), BF16), ((HALO, width), BF16), ((HALO, width), BF16)]
        + [((GATHER, width), BF16)],
        flops=4 * ROWS * ROWS * width,
    )
    from_prev = shifted(for_next, "seq", 1)
    from_next = shifted(for_prev, "seq", -1)
    window = lax.all_gather(for_all, "seq", axis=0, tiled=True)
    query, key, value, key_pool, value_pool = call(
        project_kernel,
        (normed_low, query_weight, row(query_bias), key_weight, value_weight, row(value_bias), pool),
        [((ROWS, width), BF16)] * 3 + [((POOLED, width), BF16)] * 2,
        flops=8 * ROWS * width * width,
    )
    (
        output, attended, weights, halo, key_halo, value_halo, grad_mid, sums,
    ) = call(
        functools.partial(middle_kernel, levels, holders),
        (
            item_start, tokens, cotangent, query, key, value, key_pool, value_pool, from_prev,
            from_next, window, gain, shift, key_weight, value_weight, row(value_bias), out_weight,
            row(out_bias), row(second_gain), row(second_shift), up_weight, row(up_bias),
            down_weight, row(down_bias), bias_table, codes,
        ),
        [
            ((1, ROWS, width), BF16),
            ((ROWS, width), BF16),
            ((groups, QUAD * SUB, cols), BF16),
            ((lent, width), BF16),
            ((lent, width), BF16),
            ((lent, width), BF16),
            ((ROWS, width), F32),
            ((PIECES, 512 + SMALL, 128), BF16),
        ],
        scratch=[
            ((cols, width), BF16),
            ((cols, width), BF16),
            ((ROWS, width), BF16),
            ((PIECES, 512 + SMALL, 128), BF16),
            ((2 * SMALL, 128), F32),
        ],
        smem=1,
        flops=12 * ROWS * width * hidden,
    )
    first_sums = sum_pieces(sums)
    grad_normed, to_prev, to_next, to_owners, sums = call(
        functools.partial(back_kernel, levels, holders),
        (
            tokens, normed_low, query, key, value, key_pool, value_pool, halo, key_halo,
            value_halo, weights, attended, grad_mid, gain, shift, query_weight, key_weight,
            value_weight, out_weight, pool,
        ),
        [
            ((ROWS, width), F32),
            ((HALO, width), BF16),
            ((HALO, width), BF16),
            ((holders * GATHER, width), BF16),
            ((PIECES, 256 + SMALL, 128), BF16),
        ],
        scratch=[
            ((cols, width), BF16),
            ((cols, width), BF16),
            ((ROWS, width), BF16),
            ((ROWS, width), F32),
            ((POOLED, width), F32),
            ((lent, width), F32),
            ((ROWS, width), F32),
            ((POOLED, width), F32),
            ((lent, width), F32),
            ((PIECES, 256 + SMALL, 128), BF16),
            ((2 * SMALL, 128), F32),
        ],
        flops=20 * ROWS * width * width,
    )
    second_sums = sum_pieces(sums)
    back_next = shifted(to_prev, "seq", -1)
    back_prev = shifted(to_next, "seq", 1)
    users = lax.all_to_all(
        to_owners.reshape(holders, GATHER, width), "seq", split_axis=0, concat_axis=0, tiled=True
    )
    (grad_tokens,) = call(
        last_kernel,
        (tokens, gain, grad_mid, grad_normed, back_prev, back_next, users, pool),
        [((1, ROWS, width), F32)],
        scratch=[((ROWS, width), F32)],
        flops=4 * ROWS * ROWS * width,
    )
    lines = width // 128
    small = ((lines, 128), F32)
    scratch = [((PIECES * SMALL, 128), F32)]
    down, up, down_b, up_b, gain2, shift2 = call(
        functools.partial(collect_kernel, 1),
        first_sums,
        [((hidden, width), F32), ((width, hidden), F32), small, ((hidden // 128, 128), F32)]
        + [small] * 2,
        scratch=scratch,
    )
    square = ((width, width), F32)
    out_w, query_w, key_w, value_w, query_b, value_b, out_b, gain1, shift1 = call(
        functools.partial(collect_kernel, 2),
        second_sums,
        [square] * 4 + [small] * 5,
        scratch=scratch,
    )
    vectors = [query_b, value_b, out_b, up_b, down_b, gain1, shift1, gain2, shift2]
    return (output, grad_tokens, query_w, key_w, value_w, out_w, up, down) + tuple(
        vector.reshape(-1) for vector in vectors
    )


def solution(mesh):
    cut = P("batch", "seq", None)
    in_specs = (cut, cut, P("batch", None)) + (P(),) * 15
    out_specs = (cut, cut) + (P(),) * 15
    return jax.shard_map(
        on_device, mesh=mesh, in_specs=in_specs, out_specs=out_specs, check_vma=False
    )
```

```python
import functools
import math

import jax
import jax.numpy as jnp
import numpy as np
from jax import lax
from jax.experimental import pallas as pl
from jax.experimental.pallas import tpu as pltpu
from jax.sharding import PartitionSpec as P

HEADS = 8
BLOCK = 16
UNIT = 1024
ROWS = 256
SUB = 64
QUAD = 4
HALO = 112
LOCAL = 3
GATHER = 32
NEAR_COLS = 256
PIECES = 32
SMALL = 16

NORM_EPS = 1e-05
LOG_TWO = math.log(2.0)
NEVER = -1e30
F32 = jnp.float32
BF16 = jnp.bfloat16


def dot(left, right):
    return jnp.dot(left, right, preferred_element_type=F32)


def dot_rows(left, right):
    return lax.dot_general(left, right, (((0,), (0,)), ((), ())), preferred_element_type=F32)


def dot_cols(left, right):
    return lax.dot_general(left, right, (((1,), (1,)), ((), ())), preferred_element_type=F32)


def two_parts(values):
    high = values.astype(BF16)
    return high, (values - high.astype(F32)).astype(BF16)


def normalize(values):
    centred = values - jnp.mean(values, axis=-1, keepdims=True)
    spread = jnp.mean(centred * centred, axis=-1, keepdims=True)
    scale = lax.rsqrt(spread + NORM_EPS)
    return centred * scale, scale


def norm_back(grad, normed, scale):
    return scale * (
        grad
        - jnp.mean(grad, axis=-1, keepdims=True)
        - normed * jnp.mean(grad * normed, axis=-1, keepdims=True)
    )


def normal_parts(upper):
    far = jnp.abs(upper) * math.sqrt(0.5)
    t = 1.0 / (1.0 + 0.5 * far)
    series = (
        -1.26551223,
        1.00002368,
        0.37409196,
        0.09678418,
        -0.18628806,
        0.27886807,
        -1.13520398,
        1.48851587,
        -0.82215223,
        0.17087277,
    )
    power = jnp.full_like(t, series[-1])
    for term in series[-2::-1]:
        power = power * t + term
    square = far * far
    half_tail = 0.5 * t * jnp.exp(power - square)
    phi = jnp.exp(-square) * (1.0 / math.sqrt(2.0 * math.pi))
    return jnp.where(upper < 0.0, half_tail, 1.0 - half_tail), phi


def level_rows(level):
    return ROWS >> level


def pool_matrix(levels, rows=ROWS):
    line = lax.broadcasted_iota(jnp.int32, (rows, ROWS), 0)
    token = lax.broadcasted_iota(jnp.int32, (rows, ROWS), 1)
    matrix = jnp.zeros((rows, ROWS), F32)
    at = 0
    for level in range(1, levels + 1):
        if at < rows:
            mine = lax.shift_right_arithmetic(token, jnp.int32(level)) == line - at
            matrix = jnp.where(mine, 1.0 / (1 << level), matrix)
        at += level_rows(level)
    return matrix.astype(BF16)


POOL_AT = {1: 0, 2: 128, 3: 192}
POOLED = 224
HALO_AT = {0: (0, 16), 1: (16, 32), 2: (48, 32), 3: (80, 32)}


def key_list(sub, levels):
    out = []

    def add(column, level, first, last):
        own = level_rows(level)
        base, width = HALO_AT[level]
        low = min(last, 0)
        if first < low:
            out.append((column, low - first, "halo", base + width + first, 1))
            column += low - first
            first = low
        mid = min(last, own)
        if first < mid:
            if level == 0:
                out.append((column, mid - first, "own", first, 0))
            else:
                out.append((column, mid - first, "pool", POOL_AT[level] + first, 0))
            column += mid - first
            first = mid
        if first < last:
            out.append((column, last - first, "halo", HALO + base + first - own, 2))

    start = SUB * sub
    add(0, 0, start - 16, start + SUB + 16)
    row = 32 * sub
    add(96, 1, row - 32, row)
    add(128, 1, row + 32, row + 64)
    row = 32 * (sub // 2)
    add(160, 2, row - 32, row - 16)
    third = row + 32 if sub % 2 == 0 else row - 16
    add(176, 2, third, third + 16)
    add(192, 2, row + 48, row + 64)
    add(208, 3, -32, -16)
    third = 32 if sub < 2 else -16
    add(224, 3, third, third + 16)
    add(240, 3, 48, 64)
    far = 48 * (levels - LOCAL)
    out.append((NEAR_COLS, far, "halo", 2 * HALO, 3))
    return out


def columns_of(levels):
    return -(-(NEAR_COLS + 48 * (levels - LOCAL)) // 128) * 128


def score_bias(levels):
    cols = columns_of(levels)
    bias = np.full((SUB, cols), NEVER, np.float32)
    block = np.arange(SUB) // BLOCK
    for col in range(96):
        bias[:, col] = np.where(np.abs(col // BLOCK - 1 - block) <= 1, 0.0, NEVER)
    bias[:, 96:160] = LOG_TWO
    bias[:32, 112:128] = NEVER
    bias[32:, 128:144] = NEVER
    bias[:, 160:208] = 2 * LOG_TWO
    bias[:, 208:256] = 3 * LOG_TWO
    for level in range(LOCAL + 1, levels + 1):
        at = NEAR_COLS + 48 * (level - LOCAL - 1)
        bias[:, at : at + 48] = level * LOG_TWO
    return bias


def column_codes(levels):
    codes = np.zeros((8, columns_of(levels)), np.int32)
    for sub in range(ROWS // SUB):
        for column, rows, _, _, code in key_list(sub, levels):
            if code == 3:
                codes[sub, column : column + rows] = 3 + np.arange(rows) // BLOCK
            else:
                codes[sub, column : column + rows] = code
    return codes


def gather_at(level):
    return sum(level_rows(other) for other in range(LOCAL + 1, level))


def item_bounds(starts, place):
    unit = place * ROWS // UNIT
    low = starts[0, unit]
    count = jnp.int32(0)
    for other in range(starts.shape[1]):
        count = count + jnp.where(starts[0, other] == low, 1, 0).astype(jnp.int32)
    return low, low + count * UNIT


def extra_rows(holders):
    return GATHER if direct(holders) else 0


def far_blocks(place, levels):
    out = []
    for level in range(LOCAL + 1, levels + 1):
        mine = place * ROWS // (BLOCK << level)
        parent = mine // 2
        odd = mine - 2 * parent
        third = jnp.where(odd == 1, 2 * parent - 1, 2 * parent + 2)
        out.append((level, (2 * parent - 2, third, 2 * parent + 3)))
    return out


def direct(holders):
    return holders == 8


def pick_matrix(place, levels, holders):
    rows = []
    column = lax.broadcasted_iota(jnp.int32, (48, holders * GATHER), 1)
    line = lax.broadcasted_iota(jnp.int32, (48, holders * GATHER), 0)
    for level, blocks in far_blocks(place, levels):
        part = line // BLOCK
        block = jnp.where(part == 0, blocks[0], jnp.where(part == 1, blocks[1], blocks[2]))
        row = block * BLOCK + (line - part * BLOCK)
        shift = 8 - level
        owner = lax.shift_right_arithmetic(row, jnp.int32(shift))
        inside = row - owner * (1 << shift)
        if direct(holders):
            owner = jnp.where(owner < 0, -1, jnp.bitwise_xor(owner, place))
        wanted = owner * GATHER + gather_at(level) + inside
        rows.append(jnp.where(column == wanted, 1.0, 0.0))
    return jnp.concatenate(rows, axis=0).astype(BF16)


def head_masks(quad_cols, rows):
    lane = lax.broadcasted_iota(jnp.int32, (rows, quad_cols), 1)
    width = quad_cols // QUAD
    return [(lane >= width * h) & (lane < width * (h + 1)) for h in range(QUAD)]


def stack_heads(block, masks):
    zero = jnp.zeros_like(block)
    return jnp.concatenate([jnp.where(mask, block, zero) for mask in masks], axis=0)


def unstack_heads(block, masks):
    total = None
    for h, mask in enumerate(masks):
        part = jnp.where(mask, block[SUB * h : SUB * (h + 1)], 0.0)
        total = part if total is None else total + part
    return total


def my_piece():
    return (
        (lax.axis_index("seq") % 2) * 16
        + ((lax.axis_index("seq") // 2) % 4) * 4
        + lax.axis_index("batch") % 4
    )


def first_kernel(levels, tokens, inner, outer):
    normed, _ = normalize(tokens[0].astype(F32))
    high, low = two_parts(normed)
    pool = pool_matrix(levels)
    pooled = (dot(pool, high) + dot(pool, low)).astype(BF16)
    even = lax.axis_index("seq") % 2 == 0

    def put(at, first, last):
        rows = first.shape[0]
        inner[at : at + rows] = jnp.where(even, last, first)
        outer[at : at + rows] = jnp.where(even, first, last)

    put(0, high[:16], high[ROWS - 16 :])
    for level in range(1, LOCAL + 1):
        at, width = HALO_AT[level]
        base, own = POOL_AT[level], level_rows(level)
        put(at, pooled[base : base + width], pooled[base + own - width : base + own])
    inner[HALO:] = pooled[POOLED:]


def project_kernel(
    levels,
    tokens, gain, shift, query_w, query_b, key_w, value_w, value_b, out_w, up_w, down_w, cotangent,
    normed_out, query_out, key_out, value_out, key_pool, value_pool, out_copy, up_copy, down_copy,
    cot_copy, sem,
):
    pairs = ((out_w, out_copy), (up_w, up_copy), (down_w, down_copy), (cotangent, cot_copy))
    copies = [pltpu.make_async_copy(*pair, sem.at[n]) for n, pair in enumerate(pairs)]
    for copy in copies:
        copy.start()
    normed, _ = normalize(tokens[0].astype(F32))
    rows = (normed * gain[...] + shift[...]).astype(BF16)
    normed_out[...] = rows
    pool = pool_matrix(levels, POOLED)
    query = (dot(rows, query_w[...]) + query_b[...]).astype(BF16)
    query_out[...] = query * jnp.asarray(0.125, BF16)
    key = dot(rows, key_w[...]).astype(BF16)
    key_out[...] = key
    key_pool[...] = dot(pool, key).astype(BF16)
    value = (dot(rows, value_w[...]) + value_b[...]).astype(BF16)
    value_out[...] = value
    value_pool[...] = dot(pool, value).astype(BF16)
    for copy in copies:
        copy.wait()


def fill_keys(sub, levels, target, own, pool, halo):
    cols = columns_of(levels)
    used = NEAR_COLS + 48 * (levels - LOCAL)
    sources = {"own": own, "pool": pool, "halo": halo}
    for column, rows, source, row, _ in key_list(sub, levels):
        target[column : column + rows] = sources[source][row : row + rows]
    if cols > used:
        target[used:] = jnp.zeros((cols - used, target.shape[1]), BF16)


def middle_kernel(
    levels, holders, parts,
    starts, tokens, cotangent, query, key, value, key_pool, value_pool, inner, outer,
    gain, shift, key_w, value_w, value_b, out_w, out_b, gain2, shift2, up_w, up_b,
    down_w, down_b, bias_table, codes, *refs,
):
    windows, refs = refs[:parts], refs[parts:]
    (
    output, attended_out, weights_out, halo_out, key_halo, value_halo, mid_out, grad_second_out,
    late_out, keep, send,
    key_cat, value_cat, attended, sums, small, sem,
    ) = refs
    width = tokens.shape[2]
    place = lax.axis_index("seq")
    low, high = item_bounds(starts, place)
    far = 48 * (levels - LOCAL)

    even = place % 2 == 0
    halo_out[0:HALO] = jnp.where(even, outer[...], inner[0:HALO])
    halo_out[HALO : 2 * HALO] = jnp.where(even, inner[0:HALO], outer[...])
    window = jnp.concatenate([ref[...] for ref in windows], axis=0)
    halo_out[2 * HALO :] = dot(pick_matrix(place, levels, holders), window).astype(BF16)
    scaled = (halo_out[...].astype(F32) * gain[...]).astype(BF16)
    shift_high, shift_low = two_parts(jnp.broadcast_to(shift[...], (16, width)))
    key_shift = (dot(shift_high, key_w[...]) + dot(shift_low, key_w[...]))[0:1]
    value_shift = (dot(shift_high, value_w[...]) + dot(shift_low, value_w[...]))[0:1]
    key_halo[...] = (dot(scaled, key_w[...]) + key_shift).astype(BF16)
    value_halo[...] = (dot(scaled, value_w[...]) + (value_shift + value_b[...])).astype(BF16)

    code = codes[...]
    allowed = [
        jnp.where(place * ROWS > low, 0.0, NEVER).astype(F32),
        jnp.where(place * ROWS + ROWS < high, 0.0, NEVER).astype(F32),
    ]
    for level, blocks in far_blocks(place, levels):
        span = BLOCK << level
        for block in blocks:
            inside = (block * span >= low) & (block * span + span <= high)
            allowed.append(jnp.where(inside, 0.0, NEVER).astype(F32))
    column_bias = jnp.zeros(code.shape, F32)
    for number, value_of in enumerate(allowed):
        column_bias = jnp.where(code == number + 1, value_of, column_bias)

    quad_cols = width * QUAD // HEADS
    masks = head_masks(quad_cols, SUB)
    for sub in range(ROWS // SUB):
        fill_keys(sub, levels, key_cat, key, key_pool, key_halo)
        fill_keys(sub, levels, value_cat, value, value_pool, value_halo)
        bias = bias_table[...] + column_bias[sub : sub + 1]
        bias = jnp.concatenate([bias] * QUAD, axis=0)
        for quad in range(HEADS // QUAD):
            lanes = slice(quad * quad_cols, (quad + 1) * quad_cols)
            stacked = stack_heads(query[SUB * sub : SUB * (sub + 1), lanes], masks)
            score = dot_cols(stacked, key_cat[:, lanes]) + bias
            score = jnp.exp(score - jnp.max(score, axis=1, keepdims=True))
            weight = score * (1.0 / jnp.sum(score, axis=1, keepdims=True))
            weight = weight.astype(BF16)
            weights_out[sub * (HEADS // QUAD) + quad] = weight
            mixed = unstack_heads(dot(weight, value_cat[:, lanes]), masks)
            attended[SUB * sub : SUB * (sub + 1), lanes] = mixed.astype(BF16)

    attended_out[...] = attended[...]
    mid = tokens[0].astype(F32) + dot(attended[...], out_w[...]) + out_b[...]
    normed, scale = normalize(mid)
    low_second = (normed * gain2[...] + shift2[...]).astype(BF16)
    cot = cotangent[0]
    hidden = up_w.shape[1]
    small[...] = jnp.zeros_like(small)

    def put(row, vector):
        for part in range(vector.shape[1] // 128):
            small[row + part : row + part + 1] = vector[:, 128 * part : 128 * (part + 1)]

    result = mid + down_b[...]
    grad_second = jnp.zeros((ROWS, width), F32)
    step = width
    for at in range(0, hidden, step):
        cols = slice(at, at + step)
        upper = dot(low_second, up_w[:, cols]) + up_b[:, cols]
        below, phi = normal_parts(upper)
        active = (upper * below).astype(BF16)
        result = result + dot(active, down_w[cols])
        grad_down = dot_rows(active, cot).astype(BF16)
        for piece in range(at // 64, (at + step) // 64):
            row = 64 * piece - at
            for part in range(width // 128):
                sums[slot_of(piece), 64 * part : 64 * (part + 1)] = grad_down[
                    row : row + 64, 128 * part : 128 * (part + 1)
                ]
        grad_active = dot_cols(cot, down_w[cols])
        grad_upper = grad_active * (below + upper * phi)
        low_upper = grad_upper.astype(BF16)
        put(4 + at // 128, jnp.sum(low_upper.astype(F32), axis=0, keepdims=True))
        grad_up = dot_rows(low_second, low_upper).astype(BF16)
        if at >= EARLY_UP:
            late_out[:, at - EARLY_UP : at - EARLY_UP + step] = grad_up
        else:
            put_lines(sums, 256 + 16 * (at // 128), grad_up)
        grad_second = grad_second + dot_cols(low_upper, up_w[:, cols])

    output[0] = result.astype(BF16)
    put(0, jnp.sum(cot.astype(F32), axis=0, keepdims=True))
    mid_out[...] = mid
    grad_second_out[...] = grad_second
    put_small(sums, FIRST_ROWS - SMALL, small)
    hand_out(sums, keep, send, sem)


def branch_kernel(
    cotangent, mid, grad_second, gain2, attended, out_w,
    grad_mid_out, grad_attended, grad_out, vectors,
):
    normed, scale = normalize(mid[...])
    grad = grad_second[...]
    grad_mid = cotangent[0].astype(F32) + norm_back(grad * gain2[...], normed, scale)
    grad_mid_out[...] = grad_mid
    branch = grad_mid.astype(BF16)
    grad_attended[...] = dot_cols(branch, out_w[...]).astype(BF16)
    grad_out[...] = dot_rows(attended[...], branch).astype(BF16)
    vectors[0:1] = jnp.sum(branch.astype(F32), axis=0, keepdims=True)
    vectors[1:2] = jnp.sum(grad * normed, axis=0, keepdims=True)
    vectors[2:3] = jnp.sum(grad, axis=0, keepdims=True)


EARLY_UP = 1536
FIRST_ROWS = 256 + 192 + SMALL
SECOND_ROWS = 5 * 64 + SMALL
FIRST_CUT, SECOND_CUT = 256, 176


def slot_of(piece):
    return (piece // 16) * 16 + jnp.bitwise_xor(my_piece() % 16, piece % 16)


def put_lines(sums, base, grad):
    for piece in range(PIECES):
        slot = slot_of(piece)
        for part in range(grad.shape[1] // 128):
            row = base + 16 * part
            sums[slot, row : row + 16] = grad[
                16 * piece : 16 * (piece + 1), 128 * part : 128 * (part + 1)
            ]


def put_small(sums, row, small):
    for piece in range(PIECES):
        if piece < 2:
            part = small[SMALL * piece : SMALL * (piece + 1)].astype(BF16)
        else:
            part = jnp.zeros((SMALL, 128), BF16)
        sums[slot_of(piece), row : row + SMALL] = part


def hand_out(sums, keep, send, sem):
    mine = my_piece() // 16
    half = PIECES // 2
    copies = [
        pltpu.make_async_copy(sums.at[pl.ds(mine * half, half)], keep, sem.at[0]),
        pltpu.make_async_copy(sums.at[pl.ds((1 - mine) * half, half)], send, sem.at[1]),
    ]
    for copy in copies:
        copy.start()
    for copy in copies:
        copy.wait()


def back_kernel(
    levels, holders,
    tokens, normed_low, query, key, value, key_pool, value_pool, halo, key_halo, value_halo,
    weights, grad_attended, grad_out, late, vectors, gain, shift, query_w, key_w, value_w,
    grad_normed_out, inner, outer, keep, send, *refs,
):
    owners, refs = refs[:-12], refs[-12:]
    (
    key_cat, value_cat, grad_query, key_own, key_pooled, key_lent, value_own, value_pooled,
    value_lent, sums, small, sem,
    ) = refs
    width = tokens.shape[2]
    place = lax.axis_index("seq")
    far = 48 * (levels - LOCAL)
    for ref in (key_own, key_pooled, key_lent, value_own, value_pooled, value_lent):
        ref[...] = jnp.zeros_like(ref)
    key_sums = {"own": key_own, "pool": key_pooled, "halo": key_lent}
    value_sums = {"own": value_own, "pool": value_pooled, "halo": value_lent}

    quad_cols = width * QUAD // HEADS
    masks = head_masks(quad_cols, SUB)
    for sub in range(ROWS // SUB):
        fill_keys(sub, levels, key_cat, key, key_pool, key_halo)
        fill_keys(sub, levels, value_cat, value, value_pool, value_halo)
        rows = slice(SUB * sub, SUB * (sub + 1))
        for quad in range(HEADS // QUAD):
            lanes = slice(quad * quad_cols, (quad + 1) * quad_cols)
            stacked = stack_heads(query[rows, lanes], masks)
            grads = stack_heads(grad_attended[rows, lanes], masks)
            weight = weights[sub * (HEADS // QUAD) + quad]
            prob = weight.astype(F32)
            dprob = dot_cols(grads, value_cat[:, lanes])
            delta = jnp.sum(prob * dprob, axis=1, keepdims=True)
            dscore = (prob * (dprob - delta)).astype(BF16)
            mixed = unstack_heads(dot(dscore, key_cat[:, lanes]), masks)
            grad_query[rows, lanes] = (mixed * 0.125).astype(BF16)
            grad_keys = dot_rows(dscore, stacked)
            grad_values = dot_rows(weight, grads)
            for column, count, source, row, _ in key_list(sub, levels):
                key_sums[source][row : row + count, lanes] += grad_keys[column : column + count]
                value_sums[source][row : row + count, lanes] += grad_values[
                    column : column + count
                ]

    low_query = grad_query[...]
    pool = pool_matrix(levels, POOLED)
    low_key = (key_own[...] + dot_rows(pool, key_pooled[...].astype(BF16))).astype(BF16)
    low_value = (value_own[...] + dot_rows(pool, value_pooled[...].astype(BF16))).astype(BF16)
    lent_key = key_lent[...].astype(BF16)
    lent_value = value_lent[...].astype(BF16)
    lent_normed = halo[...].astype(F32)
    lent_low = (lent_normed * gain[...] + shift[...]).astype(BF16)
    rows = normed_low[...]

    put_lines(sums, 0, late[...])
    put_lines(sums, 64, grad_out[...])
    put_lines(sums, 128, dot_rows(rows, low_query).astype(BF16))
    grad_key = dot_rows(rows, low_key) + dot_rows(lent_low, lent_key)
    put_lines(sums, 192, grad_key.astype(BF16))
    grad_value = dot_rows(rows, low_value) + dot_rows(lent_low, lent_value)
    put_lines(sums, 256, grad_value.astype(BF16))

    small[...] = jnp.zeros_like(small)

    def put(row, vector):
        for part in range(vector.shape[1] // 128):
            small[row + part : row + part + 1] = vector[:, 128 * part : 128 * (part + 1)]

    def total(values):
        return jnp.sum(values.astype(F32), axis=0, keepdims=True)

    normed, _ = normalize(tokens[0].astype(F32))
    grad_normed = (
        dot_cols(low_query, query_w[...])
        + dot_cols(low_key, key_w[...])
        + dot_cols(low_value, value_w[...])
    )
    lent_grad = dot_cols(lent_key, key_w[...]) + dot_cols(lent_value, value_w[...])
    grad_normed_out[...] = grad_normed
    put(0, total(low_query))
    put(4, total(low_value) + total(lent_value))
    put(8, vectors[0:1])
    put(20, vectors[1:2])
    put(24, vectors[2:3])
    put(12, total(grad_normed * normed) + total(lent_grad * lent_normed))
    put(16, total(grad_normed) + total(lent_grad))
    lent_grad = lent_grad.astype(BF16)
    even = place % 2 == 0
    inner[...] = jnp.where(even, lent_grad[HALO : 2 * HALO], lent_grad[:HALO])
    outer[...] = jnp.where(even, lent_grad[:HALO], lent_grad[HALO : 2 * HALO])
    pick = pick_matrix(place, levels, holders)
    returned = dot_rows(pick, lent_grad[2 * HALO :]).astype(BF16)
    if owners:
        owners[0][...] = returned
    else:
        for plane in range(4):
            for other in range(2):
                core = (place + other) % 2
                rows = returned[GATHER * (2 * plane + other) :][:GATHER]
                for part in range(4):
                    slot = core * 16 + plane * 4 + part
                    sums[slot, SECOND_ROWS:] = rows[:, 128 * part : 128 * (part + 1)]
    put_small(sums, SECOND_ROWS - SMALL, small)
    hand_out(sums, keep, send, sem)


def last_kernel(levels, tokens, gain, grad_mid, grad_normed, inner, outer, *refs):
    from_users, (grad_tokens, pooled) = refs[:-2], refs[-2:]
    even = lax.axis_index("seq") % 2 == 0
    first = jnp.where(even, outer[...], inner[0:HALO]).astype(F32)
    last = jnp.where(even, inner[0:HALO], outer[...]).astype(F32)
    for level in range(1, LOCAL + 1):
        at, width = HALO_AT[level]
        base, own = POOL_AT[level], level_rows(level)
        pooled[base : base + own] = jnp.zeros((own, pooled.shape[1]), F32)
        pooled[base : base + width] += first[at : at + width]
        pooled[base + own - width : base + own] += last[at : at + width]
    if len(from_users) > 1:
        pooled[POOLED:] = functools.reduce(jnp.add, [ref[...].astype(F32) for ref in from_users])
    else:
        for part in range(4):
            pooled[POOLED:, 128 * part : 128 * (part + 1)] = from_users[0][part].astype(F32)
    high, low = two_parts(pooled[...])
    pool = pool_matrix(levels)
    gap = jnp.zeros((ROWS - 32, first.shape[1]), F32)
    grad = grad_normed[...] + dot_rows(pool, high) + dot_rows(pool, low)
    grad = grad + jnp.concatenate([first[:16], gap, last[:16]], axis=0)
    normed, scale = normalize(tokens[0].astype(F32))
    grad_tokens[0] = grad_mid[...] + norm_back(grad * gain[...], normed, scale)


def collect_kernel(kind, *refs):
    blocks, refs = refs[:8], refs[8:]
    small = refs[-1]
    me = my_piece()
    if kind == 1:
        down, up, *order = refs[:-1]
        lined = [(up, 256, 12)]
        small_row = FIRST_ROWS - SMALL
    else:
        whole_up, out, query, key, value, *order, up, sem = refs[1:-1]
        lined = [(up, 0, 4), (out, 64, 4), (query, 128, 4), (key, 192, 4), (value, 256, 4)]
        small_row = SECOND_ROWS - SMALL
    for core in range(2):
        for plane in range(4):
            for depth in range(4):
                piece = jnp.bitwise_xor(me, core * 16 + plane * 4 + depth)
                block = blocks[core * 4 + plane]
                if kind == 1:
                    rows = pl.ds(pl.multiple_of(piece * 64, 64), 64)
                    for part in range(down.shape[1] // 128):
                        down[rows, 128 * part : 128 * (part + 1)] = block[
                            depth, 64 * part : 64 * (part + 1)
                        ].astype(F32)
                lines = pl.ds(pl.multiple_of(piece * 16, 16), 16)
                for grad, base, parts in lined:
                    for part in range(parts):
                        row = base + 16 * part
                        grad[lines, 128 * part : 128 * (part + 1)] = block[
                            depth, row : row + 16
                        ].astype(F32)

                @pl.when(piece < 2)
                def _(block=block, depth=depth, lines=lines):
                    small[lines] = block[depth, small_row : small_row + SMALL].astype(F32)

    if kind == 2:
        late = whole_up.shape[1] - up.shape[1]
        copy = pltpu.make_async_copy(up, whole_up.at[:, pl.ds(late, up.shape[1])], sem)
        copy.start()
    at = 0
    for ref in order:
        ref[...] = small[at : at + ref.shape[0]]
        at += ref.shape[0]
    if kind == 2:
        copy.wait()


class Fetched:
    def __init__(self, ref, copy):
        self.ref = ref
        self.copy = copy
        self.shape = ref.shape

    def wait(self):
        if self.copy is not None:
            self.copy.wait()
            self.copy = None

    def __getitem__(self, at):
        self.wait()
        return self.ref[at]


def call(
    kernel, inputs, outputs, scratch=(), smem=0, flops=0, room=16, fetch=(), far_in=(), far_out=(),
    alias=None, pinned=(),
):
    count_in, count_out = len(inputs), len(outputs)
    inputs = list(inputs)
    for at in (*fetch, *pinned):
        inputs[at] = pltpu.with_memory_space_constraint(inputs[at], pltpu.HBM)
    in_space = [pltpu.SMEM] * smem + [pltpu.VMEM] * (count_in - smem)
    out_space = [pltpu.VMEM] * count_out
    for at in fetch:
        in_space[at] = pltpu.HBM
    for at in far_in:
        in_space[at] = pl.ANY
    for at in far_out:
        out_space[at] = pl.ANY
    size = sum(math.prod(s) * jnp.dtype(d).itemsize for s, d in outputs)
    size += sum(math.prod(a.shape) * a.dtype.itemsize for a in inputs)
    buffers = [pltpu.VMEM(inputs[at].shape, inputs[at].dtype) for at in fetch]
    if fetch:
        buffers.append(pltpu.SemaphoreType.DMA((len(fetch),)))

    def with_copies(*refs):
        refs = list(refs)
        if fetch:
            held, sem = refs[-len(fetch) - 1 : -1], refs[-1]
            refs = refs[: -len(fetch) - 1]
            for number, at in enumerate(fetch):
                copy = pltpu.make_async_copy(refs[at], held[number], sem.at[number])
                copy.start()
                refs[at] = Fetched(held[number], copy)
        kernel(*refs)
        for at in fetch:
            refs[at].wait()

    return pl.pallas_call(
        with_copies,
        out_shape=[jax.ShapeDtypeStruct(s, d) for s, d in outputs],
        in_specs=[pl.BlockSpec(memory_space=s) for s in in_space],
        out_specs=[pl.BlockSpec(memory_space=s) for s in out_space],
        scratch_shapes=[pltpu.VMEM(*s) if isinstance(s, tuple) else s for s in scratch] + buffers,
        input_output_aliases=alias or {},
        compiler_params=pltpu.CompilerParams(vmem_limit_bytes=room * 1024 * 1024),
        cost_estimate=pl.CostEstimate(flops=flops, bytes_accessed=size, transcendentals=0),
    )(*inputs)


def swap(array, axis, distance):
    count = lax.axis_size(axis)
    return lax.ppermute(array, axis, [(i, i ^ distance) for i in range(count)])


def swap_outer(array, axis):
    count = lax.axis_size(axis)
    pairs = [(i, i + 1) for i in range(1, count - 1, 2)]
    return lax.ppermute(array, axis, pairs + [(j, i) for i, j in pairs])


def after(value, *others):
    return lax.optimization_barrier((value, others))[0]


def planes(parts):
    if not isinstance(parts, (list, tuple)):
        parts = [parts] * 4
    return [swap(parts[plane], "seq", 2 * plane) for plane in (3, 1, 2)]


def sum_of(*values):
    total = values[0].astype(F32)
    for value in values[1:]:
        total = total + value.astype(F32)
    return total.astype(BF16)


def cores_kernel(cut, keep, other, *outs):
    ways = ((slice(cut), ((1, 3), (0, 2))), (slice(cut, None), ((2, 3), (0, 1))))
    for way, (rows, groups) in enumerate(ways):
        for number, group in enumerate(groups):
            for at, plane in enumerate(group):
                for depth in range(4):
                    slot = 4 * plane + depth
                    outs[2 * way + number][at, depth] = sum_of(keep[slot, rows], other[slot, rows])


def add_cores(keep, other, cut):
    rows = keep.shape[1]
    shapes = [(2, 4, cut, 128)] * 2 + [(2, 4, rows - cut, 128)] * 2
    kernel = functools.partial(cores_kernel, cut)
    return call(kernel, (keep, other), [(s, BF16) for s in shapes], room=12)


def step_one(parts):
    return [swap(parts[0], "seq", 2), swap(parts[2], "seq", 4)]


def step_two(parts):
    return [swap(parts[0], "seq", 4), swap(parts[2], "seq", 2)]


def step_one_kernel(first, first_came, last, last_came, *outs):
    for way, (kept, came) in enumerate(((first, first_came), (last, last_came))):
        for number, plane in enumerate((1, 0)):
            for depth in range(4):
                outs[2 * way + number][depth] = sum_of(kept[plane, depth], came[plane, depth])


def add_step_one(parts, came):
    inputs = (parts[1], came[0], parts[3], came[1])
    shapes = [(parts[0].shape[1:], BF16)] * 2 + [(parts[2].shape[1:], BF16)] * 2
    return call(step_one_kernel, inputs, shapes, room=8)


def step_two_kernel(first, first_came, last, last_came, *outs):
    cut, rows = first.shape[1], outs[0].shape[1]
    for depth in range(4):
        out = outs[1 - depth % 2]
        out[depth // 2, 0:cut] = sum_of(first[depth], first_came[depth])
        out[depth // 2, cut:] = sum_of(last[depth, : rows - cut], last_came[depth, : rows - cut])
        if len(outs) > 2:
            outs[2][depth] = sum_of(last[depth, rows - cut :], last_came[depth, rows - cut :])


def add_step_two(parts, came, extra=0):
    rows = parts[0].shape[1] + parts[2].shape[1] - extra
    inputs = (parts[1], came[0], parts[3], came[1])
    outputs = [((2, rows, 128), BF16)] * 2
    if extra:
        outputs.append(((4, extra, 128), BF16))
    return call(step_two_kernel, inputs, outputs, room=8)


def near_kernel(kept, came, sent, mine):
    mine[...] = sum_of(kept[0], came[0])
    sent[...] = sum_of(kept[1], came[1])


def add_near(kept, came):
    return call(near_kernel, (kept, came), [(kept.shape[1:], BF16)] * 2, room=8)


def far_kernel(mine, came, whole):
    whole[...] = sum_of(mine[...], came[...])


def add_far(mine, came):
    (whole,) = call(far_kernel, (mine, came), [(mine.shape, BF16)], room=8)
    distance = 8
    while distance < lax.axis_size("seq"):
        other = swap(whole, "seq", distance)
        (whole,) = call(far_kernel, (whole, other), [(mine.shape, BF16)], room=8)
        distance *= 2
    return whole


def pair_kernel(one, two, out):
    out[0] = one[...]
    out[1] = two[...]


def pair_of(one, two):
    (pair,) = call(pair_kernel, (one, two), [((2, *one.shape), BF16)], room=8)
    return pair


def column_kernel(pair, came, out):
    for far in range(2):
        out[2 * far] = pair[far]
        out[2 * far + 1] = came[far]


def column_of(pair, came):
    (column,) = call(column_kernel, (pair, came), [((4, *pair.shape[1:]), BF16)], room=8)
    return column


def plane_of(column, came):
    return [column, came[1], came[2], came[0]]


def chip_kernel(inner, came, chip):
    chip[0:GATHER] = inner[HALO:]
    chip[GATHER:] = came[HALO:]


def share(inner, came):
    if not direct(lax.axis_size("seq")):
        return [lax.all_gather(inner[HALO:], "seq", axis=0, tiled=True)]
    (chip,) = call(chip_kernel, (inner, came), [((2 * GATHER, inner.shape[1]), BF16)], room=8)
    return plane_of(chip, planes(chip))


def on_device(
    tokens, cotangent, item_start, first_gain, first_shift, query_weight, query_bias, key_weight,
    value_weight, value_bias, out_weight, out_bias, second_gain, second_shift, up_weight, up_bias,
    down_weight, down_bias,
):
    width = tokens.shape[2]
    hidden = up_weight.shape[1]
    holders = lax.axis_size("seq")
    levels = (ROWS * holders // (4 * BLOCK)).bit_length() - 1
    far = 48 * (levels - LOCAL)
    lent = 2 * HALO + far
    cols = columns_of(levels)
    groups = (ROWS // SUB) * (HEADS // QUAD)
    bias_table = jnp.asarray(score_bias(levels))
    codes = jnp.asarray(column_codes(levels))

    def row(vector):
        return vector.reshape(1, -1)

    gain, shift = row(first_gain), row(first_shift)
    inner, outer = call(
        functools.partial(first_kernel, levels),
        (tokens,),
        [((HALO + GATHER, width), BF16), ((HALO, width), BF16)],
        flops=4 * ROWS * ROWS * width,
        room=8,
    )
    inner_came = swap(inner, "seq", 1)
    outer_came = swap_outer(outer, "seq")
    windows = share(inner, inner_came)
    (
        normed_low, query, key, value, key_pool, value_pool, out_weight, up_weight, down_weight,
        cotangent,
    ) = call(
        functools.partial(project_kernel, levels),
        (
            tokens, gain, shift, query_weight, row(query_bias), key_weight, value_weight,
            row(value_bias), out_weight, up_weight, down_weight, cotangent,
        ),
        [((ROWS, width), BF16)] * 4
        + [((POOLED, width), BF16)] * 2
        + [(a.shape, a.dtype) for a in (out_weight, up_weight, down_weight, cotangent)],
        scratch=[pltpu.SemaphoreType.DMA((4,))],
        fetch=(0, 1, 2, 3, 4, 5, 6, 7),
        far_in=(8, 9, 10, 11),
        pinned=(8, 9, 10, 11),
        flops=8 * ROWS * width * width,
        room=24,
    )
    extra = extra_rows(holders)
    owner_shapes = [] if extra else [((holders * GATHER, width), BF16)]
    half = PIECES // 2
    dma_pair = pltpu.SemaphoreType.DMA((2,))
    (
        output, attended, weights, halo, key_halo, value_halo, mid, grad_second, late, keep, send,
    ) = call(
        functools.partial(middle_kernel, levels, holders, len(windows)),
        (
            item_start, tokens, cotangent, query, key, value, key_pool, value_pool, inner_came,
            outer_came, gain, shift, key_weight, value_weight, row(value_bias), out_weight,
            row(out_bias), row(second_gain), row(second_shift), up_weight, row(up_bias),
            down_weight, row(down_bias), bias_table, codes, *windows,
        ),
        [
            ((1, ROWS, width), BF16),
            ((ROWS, width), BF16),
            ((groups, QUAD * SUB, cols), BF16),
            ((lent, width), BF16),
            ((lent, width), BF16),
            ((lent, width), BF16),
            ((ROWS, width), F32),
            ((ROWS, width), F32),
            ((width, hidden - EARLY_UP), BF16),
            ((half, FIRST_ROWS, 128), BF16),
            ((half, FIRST_ROWS, 128), BF16),
        ],
        scratch=[
            ((cols, width), BF16),
            ((cols, width), BF16),
            ((ROWS, width), BF16),
            ((PIECES, FIRST_ROWS, 128), BF16),
            ((2 * SMALL, 128), F32),
            dma_pair,
        ],
        smem=1,
        fetch=(12, 13, 10, 11, 14, 23, 24, 16, 1, 17, 18, 20, 22),
        far_out=(9, 10),
        flops=12 * ROWS * width * hidden,
        room=32,
    )
    other = swap(send, "seq", 1)
    grad_mid, grad_attended, grad_out, vectors = call(
        branch_kernel,
        (cotangent, mid, grad_second, row(second_gain), attended, out_weight),
        [((ROWS, width), F32), ((ROWS, width), BF16), ((width, width), BF16), ((8, width), F32)],
        fetch=(3,),
        flops=4 * ROWS * width * width,
        room=8,
    )
    first = add_cores(keep, after(other, grad_attended), FIRST_CUT)
    first_came = step_one(first)
    grad_attended, grad_out, vectors = after((grad_attended, grad_out, vectors), first)
    grad_normed, inner, outer, keep, send, *owners = call(
        functools.partial(back_kernel, levels, holders),
        (
            tokens, normed_low, query, key, value, key_pool, value_pool, halo, key_halo,
            value_halo, weights, grad_attended, grad_out, late, vectors, gain, shift, query_weight,
            key_weight, value_weight,
        ),
        [
            ((ROWS, width), F32),
            ((HALO, width), BF16),
            ((HALO, width), BF16),
            ((half, SECOND_ROWS + extra, 128), BF16),
            ((half, SECOND_ROWS + extra, 128), BF16),
        ]
        + owner_shapes,
        scratch=[
            ((cols, width), BF16),
            ((cols, width), BF16),
            ((ROWS, width), BF16),
            ((ROWS, width), F32),
            ((POOLED, width), F32),
            ((lent, width), F32),
            ((ROWS, width), F32),
            ((POOLED, width), F32),
            ((lent, width), F32),
            ((PIECES, SECOND_ROWS + extra, 128), BF16),
            ((2 * SMALL, 128), F32),
            dma_pair,
        ],
        fetch=(15, 16, 0, 17, 18, 19),
        far_out=(3, 4),
        flops=20 * ROWS * width * width,
        room=28,
    )
    other = swap(after(send, first_came), "seq", 1)
    inner_came = swap(inner, "seq", 1)
    outer_came = swap_outer(outer, "seq")
    first = add_step_one(first, first_came)
    first_came = step_two(first)
    second = add_cores(keep, other, SECOND_CUT)
    second_came = step_one(second)
    sent, kept = add_step_two(first, after(first_came, second))
    sent, kept = add_near(kept, swap(sent, "batch", 1))
    second = add_step_one(second, after(second_came, kept))
    second_came = step_two(second)
    first = add_far(kept, after(swap(sent, "batch", 2), second))
    pair = pair_of(first, swap(first, "batch", 2))
    sent, kept, *users = add_step_two(second, after(second_came, pair), extra)
    column = column_of(pair, after(swap(pair, "batch", 1), kept))
    first_came = planes(column)
    sent, kept = add_near(kept, after(swap(sent, "batch", 1), column))
    second = add_far(kept, swap(sent, "batch", 2))
    pair = pair_of(second, swap(second, "batch", 2))
    second_column = column_of(pair, swap(pair, "batch", 1))
    second_came = planes(second_column)
    if not users:
        rows = owners[0].reshape(holders, GATHER, width)
        users = list(lax.all_to_all(rows, "seq", split_axis=0, concat_axis=0, tiled=True))
    users, inner_came, outer_came = after((users, inner_came, outer_came), second_column)
    (grad_tokens,) = call(
        functools.partial(last_kernel, levels),
        (tokens, gain, grad_mid, grad_normed, inner_came, outer_came, *users),
        [((1, ROWS, width), F32)],
        scratch=[((ROWS, width), F32)],
        fetch=(0, 1),
        flops=4 * ROWS * ROWS * width,
        room=8,
    )
    first_sums = plane_of(column, after(first_came, grad_tokens))
    first_sums += [swap(block, "seq", 1) for block in first_sums]
    lines = width // 128
    small = ((lines, 128), F32)
    square = ((width, width), F32)
    small_rows = ((PIECES * SMALL, 128), F32)
    down, up, down_b, up_b = call(
        functools.partial(collect_kernel, 1),
        first_sums,
        [((hidden, width), F32), ((width, hidden), F32), small, ((hidden // 128, 128), F32)],
        scratch=[small_rows],
        room=24,
    )
    second_sums = plane_of(second_column, after(second_came, down_b))
    second_sums += [swap(block, "seq", 1) for block in second_sums]
    up, out_w, query_w, key_w, value_w, query_b, value_b, out_b, gain1, shift1, gain2, shift2 = call(
        functools.partial(collect_kernel, 2),
        [*second_sums, up],
        [((width, hidden), F32)] + [square] * 4 + [small] * 7,
        scratch=[((width, hidden - EARLY_UP), F32), pltpu.SemaphoreType.DMA, small_rows],
        far_in=(8,),
        far_out=(0,),
        alias={8: 0},
        room=20,
    )
    vectors = [query_b, value_b, out_b, up_b, down_b, gain1, shift1, gain2, shift2]
    return (output, grad_tokens, query_w, key_w, value_w, out_w, up, down) + tuple(
        vector.reshape(-1) for vector in vectors
    )


def solution(mesh):
    cut = P("batch", "seq", None)
    in_specs = (cut, cut, P("batch", None)) + (P(),) * 15
    out_specs = (cut, cut) + (P(),) * 15
    return jax.shard_map(
        on_device, mesh=mesh, in_specs=in_specs, out_specs=out_specs, check_vma=False
    )
```

```python
import functools
import math

import jax
import jax.numpy as jnp
import numpy as np
from jax import lax
from jax.experimental import pallas as pl
from jax.experimental.pallas import tpu as pltpu
from jax.sharding import PartitionSpec as P

HEADS = 8
BLOCK = 16
UNIT = 1024
ROWS = 256
SUB = 64
QUAD = 4
HALO = 112
LOCAL = 3
GATHER = 32
NEAR_COLS = 256
PIECES = 32
SMALL = 16

NORM_EPS = 1e-05
LOG_TWO = math.log(2.0)
NEVER = -1e30
F32 = jnp.float32
BF16 = jnp.bfloat16


def dot(left, right):
    return jnp.dot(left, right, preferred_element_type=F32)


def dot_rows(left, right):
    return lax.dot_general(left, right, (((0,), (0,)), ((), ())), preferred_element_type=F32)


def dot_cols(left, right):
    return lax.dot_general(left, right, (((1,), (1,)), ((), ())), preferred_element_type=F32)


def two_parts(values):
    high = values.astype(BF16)
    return high, (values - high.astype(F32)).astype(BF16)


def normalize(values):
    centred = values - jnp.mean(values, axis=-1, keepdims=True)
    spread = jnp.mean(centred * centred, axis=-1, keepdims=True)
    scale = lax.rsqrt(spread + NORM_EPS)
    return centred * scale, scale


def norm_back(grad, normed, scale):
    return scale * (
        grad
        - jnp.mean(grad, axis=-1, keepdims=True)
        - normed * jnp.mean(grad * normed, axis=-1, keepdims=True)
    )


def normal_parts(upper):
    far = jnp.abs(upper) * math.sqrt(0.5)
    t = 1.0 / (1.0 + 0.5 * far)
    series = (
        -1.26551223,
        1.00002368,
        0.37409196,
        0.09678418,
        -0.18628806,
        0.27886807,
        -1.13520398,
        1.48851587,
        -0.82215223,
        0.17087277,
    )
    power = jnp.full_like(t, series[-1])
    for term in series[-2::-1]:
        power = power * t + term
    square = far * far
    half_tail = 0.5 * t * jnp.exp(power - square)
    phi = jnp.exp(-square) * (1.0 / math.sqrt(2.0 * math.pi))
    return jnp.where(upper < 0.0, half_tail, 1.0 - half_tail), phi


def level_rows(level):
    return ROWS >> level


def pool_matrix(levels, rows=ROWS):
    line = lax.broadcasted_iota(jnp.int32, (rows, ROWS), 0)
    token = lax.broadcasted_iota(jnp.int32, (rows, ROWS), 1)
    matrix = jnp.zeros((rows, ROWS), F32)
    at = 0
    for level in range(1, levels + 1):
        if at < rows:
            mine = lax.shift_right_arithmetic(token, jnp.int32(level)) == line - at
            matrix = jnp.where(mine, 1.0 / (1 << level), matrix)
        at += level_rows(level)
    return matrix.astype(BF16)


POOL_AT = {1: 0, 2: 128, 3: 192}
POOLED = 224
HALO_AT = {0: (0, 16), 1: (16, 32), 2: (48, 32), 3: (80, 32)}


def key_list(sub, levels):
    out = []

    def add(column, level, first, last):
        own = level_rows(level)
        base, width = HALO_AT[level]
        low = min(last, 0)
        if first < low:
            out.append((column, low - first, "halo", base + width + first, 1))
            column += low - first
            first = low
        mid = min(last, own)
        if first < mid:
            if level == 0:
                out.append((column, mid - first, "own", first, 0))
            else:
                out.append((column, mid - first, "pool", POOL_AT[level] + first, 0))
            column += mid - first
            first = mid
        if first < last:
            out.append((column, last - first, "halo", HALO + base + first - own, 2))

    start = SUB * sub
    add(0, 0, start - 16, start + SUB + 16)
    row = 32 * sub
    add(96, 1, row - 32, row)
    add(128, 1, row + 32, row + 64)
    row = 32 * (sub // 2)
    add(160, 2, row - 32, row - 16)
    third = row + 32 if sub % 2 == 0 else row - 16
    add(176, 2, third, third + 16)
    add(192, 2, row + 48, row + 64)
    add(208, 3, -32, -16)
    third = 32 if sub < 2 else -16
    add(224, 3, third, third + 16)
    add(240, 3, 48, 64)
    far = 48 * (levels - LOCAL)
    out.append((NEAR_COLS, far, "halo", 2 * HALO, 3))
    return out


def columns_of(levels):
    return -(-(NEAR_COLS + 48 * (levels - LOCAL)) // 128) * 128


def score_bias(levels):
    cols = columns_of(levels)
    bias = np.full((SUB, cols), NEVER, np.float32)
    block = np.arange(SUB) // BLOCK
    for col in range(96):
        bias[:, col] = np.where(np.abs(col // BLOCK - 1 - block) <= 1, 0.0, NEVER)
    bias[:, 96:160] = LOG_TWO
    bias[:32, 112:128] = NEVER
    bias[32:, 128:144] = NEVER
    bias[:, 160:208] = 2 * LOG_TWO
    bias[:, 208:256] = 3 * LOG_TWO
    for level in range(LOCAL + 1, levels + 1):
        at = NEAR_COLS + 48 * (level - LOCAL - 1)
        bias[:, at : at + 48] = level * LOG_TWO
    return bias


def column_codes(levels):
    codes = np.zeros((8, columns_of(levels)), np.int32)
    for sub in range(ROWS // SUB):
        for column, rows, _, _, code in key_list(sub, levels):
            if code == 3:
                codes[sub, column : column + rows] = 3 + np.arange(rows) // BLOCK
            else:
                codes[sub, column : column + rows] = code
    return codes


def gather_at(level):
    return sum(level_rows(other) for other in range(LOCAL + 1, level))


def item_bounds(starts, place):
    unit = place * ROWS // UNIT
    low = starts[0, unit]
    count = jnp.int32(0)
    for other in range(starts.shape[1]):
        count = count + jnp.where(starts[0, other] == low, 1, 0).astype(jnp.int32)
    return low, low + count * UNIT


def extra_rows(holders):
    return GATHER if direct(holders) else 0


def far_blocks(place, levels):
    out = []
    for level in range(LOCAL + 1, levels + 1):
        mine = place * ROWS // (BLOCK << level)
        parent = mine // 2
        odd = mine - 2 * parent
        third = jnp.where(odd == 1, 2 * parent - 1, 2 * parent + 2)
        out.append((level, (2 * parent - 2, third, 2 * parent + 3)))
    return out


def direct(holders):
    return holders == 8


def pick_matrix(place, levels, holders):
    rows = []
    column = lax.broadcasted_iota(jnp.int32, (48, holders * GATHER), 1)
    line = lax.broadcasted_iota(jnp.int32, (48, holders * GATHER), 0)
    for level, blocks in far_blocks(place, levels):
        part = line // BLOCK
        block = jnp.where(part == 0, blocks[0], jnp.where(part == 1, blocks[1], blocks[2]))
        row = block * BLOCK + (line - part * BLOCK)
        shift = 8 - level
        owner = lax.shift_right_arithmetic(row, jnp.int32(shift))
        inside = row - owner * (1 << shift)
        if direct(holders):
            owner = jnp.where(owner < 0, -1, jnp.bitwise_xor(owner, place))
        wanted = owner * GATHER + gather_at(level) + inside
        rows.append(jnp.where(column == wanted, 1.0, 0.0))
    return jnp.concatenate(rows, axis=0).astype(BF16)


def head_masks(quad_cols, rows):
    lane = lax.broadcasted_iota(jnp.int32, (rows, quad_cols), 1)
    width = quad_cols // QUAD
    return [(lane >= width * h) & (lane < width * (h + 1)) for h in range(QUAD)]


def stack_heads(block, masks):
    zero = jnp.zeros_like(block)
    return jnp.concatenate([jnp.where(mask, block, zero) for mask in masks], axis=0)


def unstack_heads(block, masks):
    total = None
    for h, mask in enumerate(masks):
        part = jnp.where(mask, block[SUB * h : SUB * (h + 1)], 0.0)
        total = part if total is None else total + part
    return total


def my_piece():
    return (
        (lax.axis_index("seq") % 2) * 16
        + ((lax.axis_index("seq") // 2) % 4) * 4
        + lax.axis_index("batch") % 4
    )


def first_kernel(levels, tokens, inner, outer):
    normed, _ = normalize(tokens[0].astype(F32))
    high, low = two_parts(normed)
    pool = pool_matrix(levels)
    pooled = (dot(pool, high) + dot(pool, low)).astype(BF16)
    even = lax.axis_index("seq") % 2 == 0

    def put(at, first, last):
        rows = first.shape[0]
        inner[at : at + rows] = jnp.where(even, last, first)
        outer[at : at + rows] = jnp.where(even, first, last)

    put(0, high[:16], high[ROWS - 16 :])
    for level in range(1, LOCAL + 1):
        at, width = HALO_AT[level]
        base, own = POOL_AT[level], level_rows(level)
        put(at, pooled[base : base + width], pooled[base + own - width : base + own])
    inner[HALO:] = pooled[POOLED:]


def project_kernel(levels, count, *refs):
    sources, refs = refs[:count], refs[count:]
    held, (normed_out, query_out, key_out, value_out, key_pool, value_pool, sem) = (
        refs[:count],
        refs[count:],
    )
    copies = [pltpu.make_async_copy(*pair, sem.at[n]) for n, pair in enumerate(zip(sources, held))]
    for copy in copies:
        copy.start()
    tokens, gain, shift, query_w, query_b, key_w, value_w, value_b = [
        Fetched(ref, copy) for ref, copy in zip(held[:8], copies[:8])
    ]
    normed, _ = normalize(tokens[0].astype(F32))
    rows = (normed * gain[...] + shift[...]).astype(BF16)
    normed_out[...] = rows
    pool = pool_matrix(levels, POOLED)
    query = (dot(rows, query_w[...]) + query_b[...]).astype(BF16)
    query_out[...] = query * jnp.asarray(0.125, BF16)
    key = dot(rows, key_w[...]).astype(BF16)
    key_out[...] = key
    key_pool[...] = dot(pool, key).astype(BF16)
    value = (dot(rows, value_w[...]) + value_b[...]).astype(BF16)
    value_out[...] = value
    value_pool[...] = dot(pool, value).astype(BF16)
    for copy in copies[8:]:
        copy.wait()


def fill_keys(sub, levels, target, own, pool, halo):
    cols = columns_of(levels)
    used = NEAR_COLS + 48 * (levels - LOCAL)
    sources = {"own": own, "pool": pool, "halo": halo}
    for column, rows, source, row, _ in key_list(sub, levels):
        target[column : column + rows] = sources[source][row : row + rows]
    if cols > used:
        target[used:] = jnp.zeros((cols - used, target.shape[1]), BF16)


def middle_kernel(
    levels, holders, parts,
    starts, tokens, query, key, value, key_pool, value_pool, inner, outer,
    gain, shift, key_w, value_w, value_b, out_b, gain2, shift2, up_b, bias_table, codes,
    out_source, up_source, cot_source, down_source, *refs,
):
    windows, refs = refs[:parts], refs[parts:]
    (
    attended_out, weights_out, halo_out, key_halo, value_halo, mid_out, second_out, active_out,
    slope_out, keep, send, out_held, up_held, cot_held, down_held,
    key_cat, value_cat, attended, sums, small, sem, sources_sem,
    ) = refs
    pairs = (
        (out_source, out_held), (up_source, up_held), (cot_source, cot_held),
        (down_source, down_held),
    )
    brought = []
    for number, pair in enumerate(pairs):
        copy = pltpu.make_async_copy(*pair, sources_sem.at[number])
        copy.start()
        brought.append(Fetched(pair[1], copy))
    out_w, up_w, cotangent, down_w = brought
    width = tokens.shape[2]
    place = lax.axis_index("seq")
    low, high = item_bounds(starts, place)
    far = 48 * (levels - LOCAL)

    even = place % 2 == 0
    halo_out[0:HALO] = jnp.where(even, outer[...], inner[0:HALO])
    halo_out[HALO : 2 * HALO] = jnp.where(even, inner[0:HALO], outer[...])
    window = jnp.concatenate([ref[...] for ref in windows], axis=0)
    halo_out[2 * HALO :] = dot(pick_matrix(place, levels, holders), window).astype(BF16)
    scaled = (halo_out[...].astype(F32) * gain[...]).astype(BF16)
    shift_high, shift_low = two_parts(jnp.broadcast_to(shift[...], (16, width)))
    key_shift = (dot(shift_high, key_w[...]) + dot(shift_low, key_w[...]))[0:1]
    value_shift = (dot(shift_high, value_w[...]) + dot(shift_low, value_w[...]))[0:1]
    key_halo[...] = (dot(scaled, key_w[...]) + key_shift).astype(BF16)
    value_halo[...] = (dot(scaled, value_w[...]) + (value_shift + value_b[...])).astype(BF16)

    code = codes[...]
    allowed = [
        jnp.where(place * ROWS > low, 0.0, NEVER).astype(F32),
        jnp.where(place * ROWS + ROWS < high, 0.0, NEVER).astype(F32),
    ]
    for level, blocks in far_blocks(place, levels):
        span = BLOCK << level
        for block in blocks:
            inside = (block * span >= low) & (block * span + span <= high)
            allowed.append(jnp.where(inside, 0.0, NEVER).astype(F32))
    column_bias = jnp.zeros(code.shape, F32)
    for number, value_of in enumerate(allowed):
        column_bias = jnp.where(code == number + 1, value_of, column_bias)

    quad_cols = width * QUAD // HEADS
    masks = head_masks(quad_cols, SUB)
    for sub in range(ROWS // SUB):
        fill_keys(sub, levels, key_cat, key, key_pool, key_halo)
        fill_keys(sub, levels, value_cat, value, value_pool, value_halo)
        bias = bias_table[...] + column_bias[sub : sub + 1]
        bias = jnp.concatenate([bias] * QUAD, axis=0)
        for quad in range(HEADS // QUAD):
            lanes = slice(quad * quad_cols, (quad + 1) * quad_cols)
            stacked = stack_heads(query[SUB * sub : SUB * (sub + 1), lanes], masks)
            score = dot_cols(stacked, key_cat[:, lanes]) + bias
            score = jnp.exp(score - jnp.max(score, axis=1, keepdims=True))
            weight = score * (1.0 / jnp.sum(score, axis=1, keepdims=True))
            weight = weight.astype(BF16)
            weights_out[sub * (HEADS // QUAD) + quad] = weight
            mixed = unstack_heads(dot(weight, value_cat[:, lanes]), masks)
            attended[SUB * sub : SUB * (sub + 1), lanes] = mixed.astype(BF16)

    attended_out[...] = attended[...]
    mid = tokens[0].astype(F32) + dot(attended[...], out_w[...]) + out_b[...]
    normed, scale = normalize(mid)
    low_second = (normed * gain2[...] + shift2[...]).astype(BF16)
    cot = cotangent[0]
    hidden = up_w.shape[1]
    mid_out[...] = mid
    second_out[...] = low_second
    for at in range(0, hidden, width):
        cols = slice(at, at + width)
        upper = dot(low_second, up_w[:, cols]) + up_b[:, cols]
        below, phi = normal_parts(upper)
        slope_out[:, cols] = below + upper * phi
        active = (upper * below).astype(BF16)
        active_out[:, cols] = active
        grad_down = dot_rows(active, cot).astype(BF16)
        for piece in range(at // 64, (at + width) // 64):
            row = 64 * piece - at
            for part in range(width // 128):
                sums[slot_of(piece), 64 * part : 64 * (part + 1)] = grad_down[
                    row : row + 64, 128 * part : 128 * (part + 1)
                ]
    small[...] = jnp.zeros_like(small)
    put_vector(small, 0, jnp.sum(cot.astype(F32), axis=0, keepdims=True))
    put_small(sums, 256, small)
    down_w.wait()
    hand_out(sums, keep, [send], sem)


def feed_kernel(
    cotangent, mid, low_second, active, slope, gain2, up_w, down_w, down_b, out_w, attended,
    output, grad_mid_out, grad_attended, grad_out, out_b_sum, keep, *refs,
):
    sends, (sums, small, sem) = refs[:-3], refs[-3:]
    cot = cotangent[0]
    hidden, width = down_w.shape
    result = mid[...] + down_b[...]
    grad_second = jnp.zeros((ROWS, width), F32)
    small[...] = jnp.zeros_like(small)
    for at in range(0, hidden, width):
        cols = slice(at, at + width)
        result = result + dot(active[:, cols], down_w[cols])
        grad_upper = (dot_cols(cot, down_w[cols]) * slope[:, cols]).astype(BF16)
        put_vector(small, at // 128, jnp.sum(grad_upper.astype(F32), axis=0, keepdims=True))
        put_lines(sums, at // 8, dot_rows(low_second[...], grad_upper).astype(BF16))
        grad_second = grad_second + dot_cols(grad_upper, up_w[:, cols])
    output[0] = result.astype(BF16)
    normed, scale = normalize(mid[...])
    put_vector(small, 16, jnp.sum(grad_second * normed, axis=0, keepdims=True))
    put_vector(small, 20, jnp.sum(grad_second, axis=0, keepdims=True))
    put_small(sums, 256, small)
    grad_mid = cot.astype(F32) + norm_back(grad_second * gain2[...], normed, scale)
    grad_mid_out[...] = grad_mid
    branch = grad_mid.astype(BF16)
    grad_attended[...] = dot_cols(branch, out_w[...]).astype(BF16)
    grad_out[...] = dot_rows(attended[...], branch).astype(BF16)
    out_b_sum[...] = jnp.sum(branch.astype(F32), axis=0, keepdims=True)
    hand_out(sums, keep, sends, sem)


FEED, BACK, BORROWED, LAST = "feed", "back", "borrowed", "last"
ORDER = (FEED, 1, 2, BACK, 1, 2, 3, 1, BORROWED, 2, 1, 3, 2, 1, 3, 2, 1, 3, 2, 1, 3, 2, 3, LAST, 2, 1, 3, 3)
Z_DIRECT = True
GROUP_ROWS = 256 + SMALL
MID_PARTS, LATE_PARTS = 2, 4


def put_vector(small, row, vector):
    for part in range(vector.shape[1] // 128):
        small[row + part : row + part + 1] = vector[:, 128 * part : 128 * (part + 1)]


def turned(place):
    return (place & 4) * 2 + (place // 2 & 4) + (place & 3)


def slot_of(piece):
    mine, place = my_piece() % 16, piece % 16
    if piece // 16 == 1:
        mine, place = turned(mine), turned(place)
    return (piece // 16) * 16 + jnp.bitwise_xor(mine, place)


def put_lines(sums, base, grad):
    for piece in range(PIECES):
        slot = slot_of(piece)
        for part in range(grad.shape[1] // 128):
            row = base + 16 * part
            sums[slot, row : row + 16] = grad[
                16 * piece : 16 * (piece + 1), 128 * part : 128 * (part + 1)
            ]


def put_small(sums, row, small):
    for piece in range(PIECES):
        if piece < 2:
            part = small[SMALL * piece : SMALL * (piece + 1)].astype(BF16)
        else:
            part = jnp.zeros((SMALL, 128), BF16)
        sums[slot_of(piece), row : row + SMALL] = part


def hand_out(sums, keep, sends, sem):
    mine = my_piece() // 16
    half = PIECES // 2
    count = half // len(sends)
    copies = [pltpu.make_async_copy(sums.at[pl.ds(mine * half, half)], keep, sem.at[0])]
    for number, send in enumerate(sends):
        rows = pl.ds((1 - mine) * half + number * count, count)
        copies.append(pltpu.make_async_copy(sums.at[rows], send, sem.at[1 + number]))
    for copy in copies:
        copy.start()
    for copy in copies:
        copy.wait()


def back_kernel(
    levels, holders,
    tokens, normed_low, query, key, value, key_pool, value_pool, halo, key_halo, value_halo,
    weights, grad_attended, grad_out, out_b_sum, gain, shift, query_w, key_w, value_w,
    grad_normed_out, inner, outer, keep, *refs,
):
    sends, owners, refs = refs[:LATE_PARTS], refs[LATE_PARTS:-12], refs[-12:]
    (
    key_cat, value_cat, grad_query, key_own, key_pooled, key_lent, value_own, value_pooled,
    value_lent, sums, small, sem,
    ) = refs
    width = tokens.shape[2]
    place = lax.axis_index("seq")
    far = 48 * (levels - LOCAL)
    for ref in (key_own, key_pooled, key_lent, value_own, value_pooled, value_lent):
        ref[...] = jnp.zeros_like(ref)
    key_sums = {"own": key_own, "pool": key_pooled, "halo": key_lent}
    value_sums = {"own": value_own, "pool": value_pooled, "halo": value_lent}

    quad_cols = width * QUAD // HEADS
    masks = head_masks(quad_cols, SUB)
    for sub in range(ROWS // SUB):
        fill_keys(sub, levels, key_cat, key, key_pool, key_halo)
        fill_keys(sub, levels, value_cat, value, value_pool, value_halo)
        rows = slice(SUB * sub, SUB * (sub + 1))
        for quad in range(HEADS // QUAD):
            lanes = slice(quad * quad_cols, (quad + 1) * quad_cols)
            stacked = stack_heads(query[rows, lanes], masks)
            grads = stack_heads(grad_attended[rows, lanes], masks)
            weight = weights[sub * (HEADS // QUAD) + quad]
            prob = weight.astype(F32)
            dprob = dot_cols(grads, value_cat[:, lanes])
            delta = jnp.sum(prob * dprob, axis=1, keepdims=True)
            dscore = (prob * (dprob - delta)).astype(BF16)
            mixed = unstack_heads(dot(dscore, key_cat[:, lanes]), masks)
            grad_query[rows, lanes] = (mixed * 0.125).astype(BF16)
            grad_keys = dot_rows(dscore, stacked)
            grad_values = dot_rows(weight, grads)
            for column, count, source, row, _ in key_list(sub, levels):
                key_sums[source][row : row + count, lanes] += grad_keys[column : column + count]
                value_sums[source][row : row + count, lanes] += grad_values[
                    column : column + count
                ]

    low_query = grad_query[...]
    pool = pool_matrix(levels, POOLED)
    low_key = (key_own[...] + dot_rows(pool, key_pooled[...].astype(BF16))).astype(BF16)
    low_value = (value_own[...] + dot_rows(pool, value_pooled[...].astype(BF16))).astype(BF16)
    lent_key = key_lent[...].astype(BF16)
    lent_value = value_lent[...].astype(BF16)
    lent_normed = halo[...].astype(F32)
    lent_low = (lent_normed * gain[...] + shift[...]).astype(BF16)
    rows = normed_low[...]

    put_lines(sums, 0, grad_out[...])
    put_lines(sums, 64, dot_rows(rows, low_query).astype(BF16))
    grad_key = dot_rows(rows, low_key) + dot_rows(lent_low, lent_key)
    put_lines(sums, 128, grad_key.astype(BF16))
    grad_value = dot_rows(rows, low_value) + dot_rows(lent_low, lent_value)
    put_lines(sums, 192, grad_value.astype(BF16))
    small[...] = jnp.zeros_like(small)

    def total(values):
        return jnp.sum(values.astype(F32), axis=0, keepdims=True)

    normed, _ = normalize(tokens[0].astype(F32))
    grad_normed = (
        dot_cols(low_query, query_w[...])
        + dot_cols(low_key, key_w[...])
        + dot_cols(low_value, value_w[...])
    )
    lent_grad = dot_cols(lent_key, key_w[...]) + dot_cols(lent_value, value_w[...])
    grad_normed_out[...] = grad_normed
    put_vector(small, 0, total(low_query))
    put_vector(small, 4, total(low_value) + total(lent_value))
    put_vector(small, 8, out_b_sum[...])
    put_vector(small, 12, total(grad_normed * normed) + total(lent_grad * lent_normed))
    put_vector(small, 16, total(grad_normed) + total(lent_grad))
    lent_grad = lent_grad.astype(BF16)
    even = place % 2 == 0
    inner[...] = jnp.where(even, lent_grad[HALO : 2 * HALO], lent_grad[:HALO])
    outer[...] = jnp.where(even, lent_grad[:HALO], lent_grad[HALO : 2 * HALO])
    pick = pick_matrix(place, levels, holders)
    returned = dot_rows(pick, lent_grad[2 * HALO :]).astype(BF16)
    if owners:
        owners[0][...] = returned
    else:
        for plane in range(4):
            for other in range(2):
                core = (place + other) % 2
                at = jnp.where(core == 1, turned(4 * plane), 4 * plane)
                rows = returned[GATHER * (2 * plane + other) :][:GATHER]
                for part in range(4):
                    slot = core * 16 + at + part
                    sums[slot, GROUP_ROWS:] = rows[:, 128 * part : 128 * (part + 1)]
    put_small(sums, 256, small)
    hand_out(sums, keep, sends, sem)


def last_kernel(levels, tokens, gain, grad_mid, grad_normed, inner, outer, *refs):
    from_users, (grad_tokens, pooled) = refs[:-2], refs[-2:]
    even = lax.axis_index("seq") % 2 == 0
    first = jnp.where(even, outer[...], inner[0:HALO]).astype(F32)
    last = jnp.where(even, inner[0:HALO], outer[...]).astype(F32)
    for level in range(1, LOCAL + 1):
        at, width = HALO_AT[level]
        base, own = POOL_AT[level], level_rows(level)
        pooled[base : base + own] = jnp.zeros((own, pooled.shape[1]), F32)
        pooled[base : base + width] += first[at : at + width]
        pooled[base + own - width : base + own] += last[at : at + width]
    if len(from_users) > 1:
        pooled[POOLED:] = functools.reduce(jnp.add, [ref[...].astype(F32) for ref in from_users])
    else:
        for part in range(4):
            pooled[POOLED:, 128 * part : 128 * (part + 1)] = from_users[0][part].astype(F32)
    high, low = two_parts(pooled[...])
    pool = pool_matrix(levels)
    gap = jnp.zeros((ROWS - 32, first.shape[1]), F32)
    grad = grad_normed[...] + dot_rows(pool, high) + dot_rows(pool, low)
    grad = grad + jnp.concatenate([first[:16], gap, last[:16]], axis=0)
    normed, scale = normalize(tokens[0].astype(F32))
    grad_tokens[0] = grad_mid[...] + norm_back(grad * gain[...], normed, scale)


def collect_kernel(kind, *refs):
    blocks, refs, small = refs[:4], refs[4:-1], refs[-1]
    me = my_piece()
    squares = 4 if kind == 2 else 1
    grads, order = refs[:squares], refs[squares:]

    for core in range(2):
        odd = (me // 16 + core) % 2 == 1
        for plane in range(4):
            for depth in range(4):
                place = 4 * plane + depth
                place = jnp.where(odd, turned(place), place)
                piece = jnp.bitwise_xor(me, core * 16 + place)
                block = blocks[2 * core + plane % 2]

                def held(row, rows, block=block, plane=plane, depth=depth):
                    return block[plane // 2, depth, row : row + rows].astype(F32)

                lines = pl.ds(pl.multiple_of(piece * 16, 16), 16)
                if kind == 0:
                    (down,) = grads
                    rows = pl.ds(pl.multiple_of(piece * 64, 64), 64)
                    for part in range(down.shape[1] // 128):
                        down[rows, 128 * part : 128 * (part + 1)] = held(64 * part, 64)
                else:
                    base = 0
                    for grad in grads:
                        for part in range(grad.shape[1] // 128):
                            grad[lines, 128 * part : 128 * (part + 1)] = held(base, 16)
                            base += 16

                @pl.when(piece < 2)
                def _(held=held, lines=lines):
                    small[lines] = held(256, SMALL)

    at = 0
    for ref in order:
        ref[...] = small[at : at + ref.shape[0]]
        at += ref.shape[0]


class Fetched:
    def __init__(self, ref, copy):
        self.ref = ref
        self.copy = copy
        self.shape = ref.shape

    def wait(self):
        if self.copy is not None:
            self.copy.wait()
            self.copy = None

    def __getitem__(self, at):
        self.wait()
        return self.ref[at]


def call(
    kernel, inputs, outputs, scratch=(), smem=0, room=16, far_in=(), far_out=(), alias=None, pinned=()
):
    inputs = list(inputs)
    in_space = [pltpu.SMEM] * smem + [pltpu.VMEM] * (len(inputs) - smem)
    out_space = [pltpu.VMEM] * len(outputs)
    for at in far_in:
        in_space[at] = pl.ANY
    for at in pinned:
        inputs[at] = pltpu.with_memory_space_constraint(inputs[at], pltpu.HBM)
        in_space[at] = pltpu.HBM
    for at in far_out:
        out_space[at] = pl.ANY
    return pl.pallas_call(
        kernel,
        out_shape=[jax.ShapeDtypeStruct(s, d) for s, d in outputs],
        in_specs=[pl.BlockSpec(memory_space=s) for s in in_space],
        out_specs=[pl.BlockSpec(memory_space=s) for s in out_space],
        scratch_shapes=[pltpu.VMEM(*s) if isinstance(s, tuple) else s for s in scratch],
        input_output_aliases=alias or {},
        compiler_params=pltpu.CompilerParams(vmem_limit_bytes=room * 1024 * 1024),
        cost_estimate=pl.CostEstimate(flops=0, bytes_accessed=0, transcendentals=0),
    )(*inputs)


def swap(array, axis, distance):
    count = lax.axis_size(axis)
    return lax.ppermute(array, axis, [(i, i ^ distance) for i in range(count)])


def swap_outer(array, axis):
    count = lax.axis_size(axis)
    pairs = [(i, i + 1) for i in range(1, count - 1, 2)]
    return lax.ppermute(array, axis, pairs + [(j, i) for i, j in pairs])


def after(value, *others):
    return lax.optimization_barrier((value, others))[0]


def planes(array):
    return [swap(array, "seq", 2 * plane) for plane in (3, 1, 2)]


def hop(array, step):
    pairs = []
    for place in range(lax.axis_size("seq")):
        bit = 2 << (step if place % 2 == 0 else 1 - step)
        pairs.append((place, place ^ bit))
    return lax.ppermute(array, "seq", pairs)


def sum_of(*values):
    total = values[0].astype(F32)
    for value in values[1:]:
        total = total + value.astype(F32)
    return total.astype(BF16)


def halves_kernel(kept, *refs):
    came, (sent_out, kept_out) = refs[:-2], refs[-2:]
    each = kept.shape[0] // len(came)
    for slot in range(kept.shape[0]):
        out = (kept_out, sent_out)[slot % 2]
        out[slot // 2] = sum_of(kept[slot], came[slot // each][slot % each])


def add_halves(kept, *came):
    shape = (kept.shape[0] // 2, *kept.shape[1:])
    return call(halves_kernel, (kept, *came), [(shape, BF16)] * 2, room=12)


def plane_kernel(extra, kept, came, sent_out, kept_out, *complete):
    rows = kept.shape[1] - extra
    for depth in range(4):
        total = sum_of(kept[depth], came[depth])
        (kept_out, sent_out)[depth % 2][depth // 2] = total[:rows]
        if extra:
            complete[0][depth] = total[rows:]


def add_plane(kept, came, extra):
    rows = kept.shape[1] - extra
    outputs = [((2, rows, 128), BF16)] * 2
    if extra:
        outputs.append(((4, extra, 128), BF16))
    return call(functools.partial(plane_kernel, extra), (kept, came), outputs, room=8)


def plane_direct_kernel(extra, kept, came, *outs):
    rows = kept.shape[1] - extra
    for depth in range(4):
        total = sum_of(kept[depth], came[depth])
        outs[depth][...] = total[:rows]
        if extra:
            outs[4][depth] = total[rows:]


def add_plane_direct(kept, came, extra):
    rows = kept.shape[1] - extra
    outputs = [((rows, 128), BF16)] * 4
    if extra:
        outputs.append(((4, extra, 128), BF16))
    outs = call(functools.partial(plane_direct_kernel, extra), (kept, came), outputs, room=8)
    return [*outs[:4], list(outs[4:])]


def column_kernel(whole, two, three, one, out):
    for depth, ref in enumerate((whole, one, two, three)):
        out[0, depth] = ref[...]


def column_of(whole, came):
    (column,) = call(column_kernel, (whole, *came), [((1, 4, *whole.shape), BF16)], room=8)
    return column


def whole_kernel(*refs):
    refs[-1][...] = sum_of(*[ref[...] for ref in refs[:-1]])


def add_whole(mine, *came):
    (whole,) = call(whole_kernel, (mine, *came), [(mine.shape, BF16)], room=8)
    distance = 8
    while distance < lax.axis_size("seq"):
        other = swap(whole, "seq", distance)
        (whole,) = call(whole_kernel, (whole, other), [(mine.shape, BF16)], room=8)
        distance *= 2
    return whole


def joined_kernel(mine, came, out):
    for slot in range(mine.shape[0]):
        out[2 * slot] = mine[slot]
        out[2 * slot + 1] = came[slot]


def join(mine, came):
    (out,) = call(joined_kernel, (mine, came), [((2 * mine.shape[0], *mine.shape[1:]), BF16)], room=8)
    return out


class Group:
    def __init__(self, keep, sends):
        self.kept = slots(keep)
        self.came = [slots(swap(send, "seq", 1)) for send in sends]
        self.stage = 0
        self.users = []

    def step(self, last, extra):
        stage, kept = self.stage, self.kept
        came = after(self.came, last)
        self.stage += 1
        if stage == 0:
            sent, self.kept = add_halves(kept, *came)
            self.came = hop(sent, 0)
        elif stage == 1:
            sent, kept = add_halves(kept, came)
            self.kept = kept[0]
            self.came = hop(sent[0], 1)
        elif stage == 2 and Z_DIRECT:
            *self.kept, self.users = add_plane_direct(kept, came, extra)
            self.came = [swap(self.kept[depth], "batch", depth) for depth in (2, 3, 1)]
            self.stage = 4
        elif stage == 4 and Z_DIRECT:
            self.kept = add_whole(kept[0], *came)
            self.came = [swap(self.kept, "batch", depth) for depth in (2, 3, 1)]
            self.stage = 6
        elif stage == 6 and Z_DIRECT:
            self.kept = column_of(kept, came)
            self.came = hop(self.kept, 1)
        elif stage == 2:
            sent, self.kept, *self.users = add_plane(kept, came, extra)
            self.came = swap(sent, "batch", 1)
        elif stage == 3:
            sent, kept = add_halves(kept, came)
            self.kept = kept[0]
            self.came = swap(sent[0], "batch", 2)
        elif stage == 4:
            self.kept = add_whole(kept, came)[None]
            self.came = swap(self.kept, "batch", 2)
        elif stage == 5:
            self.kept = join(kept, came)
            self.came = swap(self.kept, "batch", 1)
        elif stage == 6:
            self.kept = join(kept, came)[None]
            self.came = hop(self.kept, 1)
        elif stage == 7:
            self.kept = join(kept, came)
            self.came = hop(self.kept, 0)
        else:
            self.sums = [kept, came]
            self.sums += [swap(block, "seq", 1) for block in self.sums]
            return came
        return self.kept[0] if isinstance(self.kept, list) else self.kept


def slots(array):
    return array.reshape(-1, 4, *array.shape[1:])


def plane_of(column, came):
    return [column, came[1], came[2], came[0]]


def chip_kernel(inner, came, chip):
    chip[0:GATHER] = inner[HALO:]
    chip[GATHER:] = came[HALO:]


def share(inner, came):
    if not direct(lax.axis_size("seq")):
        return [lax.all_gather(inner[HALO:], "seq", axis=0, tiled=True)]
    (chip,) = call(chip_kernel, (inner, came), [((2 * GATHER, inner.shape[1]), BF16)], room=8)
    return plane_of(chip, planes(chip))


def on_device(
    tokens, cotangent, item_start, first_gain, first_shift, query_weight, query_bias, key_weight,
    value_weight, value_bias, out_weight, out_bias, second_gain, second_shift, up_weight, up_bias,
    down_weight, down_bias,
):
    width = tokens.shape[2]
    hidden = up_weight.shape[1]
    holders = lax.axis_size("seq")
    levels = (ROWS * holders // (4 * BLOCK)).bit_length() - 1
    far = 48 * (levels - LOCAL)
    lent = 2 * HALO + far

    cols = columns_of(levels)
    groups = (ROWS // SUB) * (HEADS // QUAD)
    bias_table = jnp.asarray(score_bias(levels))
    codes = jnp.asarray(column_codes(levels))

    def row(vector):
        return vector.reshape(1, -1)

    gain, shift = row(first_gain), row(first_shift)
    inner, outer = call(
        functools.partial(first_kernel, levels),
        (tokens,),
        [((HALO + GATHER, width), BF16), ((HALO, width), BF16)],
        room=8,
    )
    inner_came = swap(inner, "seq", 1)
    outer_came = swap_outer(outer, "seq")
    windows = share(inner, inner_came)
    carried = (
        tokens, gain, shift, query_weight, row(query_bias), key_weight, value_weight,
        row(value_bias), row(out_bias), row(second_gain), row(second_shift), row(up_bias),
        row(down_bias), bias_table, codes,
    )
    count = len(carried)
    *carried, normed_low, query, key, value, key_pool, value_pool = call(
        functools.partial(project_kernel, levels, count),
        carried,
        [(a.shape, a.dtype) for a in carried]
        + [((ROWS, width), BF16)] * 4
        + [((POOLED, width), BF16)] * 2,
        scratch=[pltpu.SemaphoreType.DMA((count,))],
        pinned=range(count),
        room=24,
    )
    (
        tokens, gain, shift, query_weight, _, key_weight, value_weight, value_bias, out_bias,
        second_gain, second_shift, up_bias, down_bias, bias_table, codes,
    ) = carried
    extra = extra_rows(holders)
    owner_shapes = [] if extra else [((holders * GATHER, width), BF16)]
    half = PIECES // 2
    copies = pltpu.SemaphoreType.DMA((1 + max(MID_PARTS, LATE_PARTS),))

    def piece_sums(parts, rows=GROUP_ROWS):
        sends = [((half // parts, rows, 128), BF16)] * parts
        return [((half, rows, 128), BF16)] + sends

    sums_scratch = ((PIECES, GROUP_ROWS, 128), BF16)
    small_scratch = ((2 * SMALL, 128), F32)
    (
        attended, weights, halo, key_halo, value_halo, mid, low_second, active, slope, keep, send,
        out_weight, up_weight, cotangent, down_weight,
    ) = call(
        functools.partial(middle_kernel, levels, holders, len(windows)),
        (
            item_start, tokens, query, key, value, key_pool, value_pool, inner_came, outer_came,
            gain, shift, key_weight, value_weight, value_bias, out_bias, second_gain, second_shift,
            up_bias, bias_table, codes, out_weight, up_weight, cotangent, down_weight, *windows,
        ),
        [
            ((ROWS, width), BF16),
            ((groups, QUAD * SUB, cols), BF16),
            ((lent, width), BF16),
            ((lent, width), BF16),
            ((lent, width), BF16),
            ((ROWS, width), F32),
            ((ROWS, width), BF16),
            ((ROWS, hidden), BF16),
            ((ROWS, hidden), F32),
        ]
        + piece_sums(1)
        + [(a.shape, a.dtype) for a in (out_weight, up_weight, cotangent, down_weight)],
        scratch=[
            ((cols, width), BF16),
            ((cols, width), BF16),
            ((ROWS, width), BF16),
            sums_scratch,
            small_scratch,
            copies,
            pltpu.SemaphoreType.DMA((4,)),
        ],
        smem=1,
        far_in=(20, 21, 22, 23),
        pinned=(20, 21, 22, 23),
        far_out=(9, 10),
        room=24,
    )
    lines = width // 128
    small = ((lines, 128), F32)
    square = ((width, width), F32)
    collected = {
        1: [((hidden, width), F32), small],
        2: [((width, hidden), F32), ((hidden // 128, 128), F32), small, small],
        3: [square] * 4 + [small] * 5,
    }
    sums = {1: Group(keep, [send])}
    done = {}
    last = ()
    for what in ORDER:
        if what == FEED:
            output, grad_mid, grad_attended, grad_out, out_b_sum, keep, *sends = call(
                feed_kernel,
                (
                    cotangent, after(mid, last), low_second, active, slope, second_gain, up_weight, down_weight,
                    down_bias, out_weight, attended,
                ),
                [
                    ((1, ROWS, width), BF16),
                    ((ROWS, width), F32),
                    ((ROWS, width), BF16),
                    ((width, width), BF16),
                    ((1, width), F32),
                ]
                + piece_sums(MID_PARTS),
                scratch=[sums_scratch, small_scratch, copies],
                far_out=range(5, 6 + MID_PARTS),
                room=24,
            )
            sums[2] = Group(keep, sends)
            last = grad_attended
        elif what == BACK:
            grad_normed, inner, outer, keep, *sends = call(
                functools.partial(back_kernel, levels, holders),
                (
                    tokens, normed_low, after(query, last), key, value, key_pool, value_pool, halo, key_halo,
                    value_halo, weights, grad_attended, grad_out, out_b_sum, gain, shift, query_weight,
                    key_weight, value_weight,
                ),
                [
                    ((ROWS, width), F32),
                    ((HALO, width), BF16),
                    ((HALO, width), BF16),
                ]
                + piece_sums(LATE_PARTS, GROUP_ROWS + extra)
                + owner_shapes,
                scratch=[
                    ((cols, width), BF16),
                    ((cols, width), BF16),
                    ((ROWS, width), BF16),
                    ((ROWS, width), F32),
                    ((POOLED, width), F32),
                    ((lent, width), F32),
                    ((ROWS, width), F32),
                    ((POOLED, width), F32),
                    ((lent, width), F32),
                    ((PIECES, GROUP_ROWS + extra, 128), BF16),
                    small_scratch,
                    copies,
                ],
                far_out=range(3, 4 + LATE_PARTS),
                room=28,
            )
            sends, owners = sends[:LATE_PARTS], sends[LATE_PARTS:]
            sums[3] = Group(keep, sends)
            inner_came = swap(inner, "seq", 1)
            outer_came = swap_outer(outer, "seq")
            last = grad_normed
        elif what == LAST:
            users = sums[3].users
            if not extra:
                rows = owners[0].reshape(holders, GATHER, width)
                users = list(lax.all_to_all(rows, "seq", split_axis=0, concat_axis=0, tiled=True))
            (grad_tokens,) = call(
                functools.partial(last_kernel, levels),
                (tokens, gain, grad_mid, after(grad_normed, last), inner_came, outer_came, *users),
                [((1, ROWS, width), F32)],
                scratch=[((ROWS, width), F32)],
                room=8,
            )
            last = grad_tokens
        elif what == BORROWED:
            inner_came, outer_came = after((inner_came, outer_came), last)
            last = (inner_came, outer_came)
        elif sums[what].stage < 9:
            last = sums[what].step(last, extra if what == 3 else 0)
        else:
            done[what] = call(
                functools.partial(collect_kernel, what - 1),
                after(sums[what].sums, last),
                collected[what],
                scratch=[((PIECES * SMALL, 128), F32)],
                room=16,
            )
            last = done[what][-1]
    down, down_b = done[1]
    up, up_b, gain2, shift2 = done[2]
    out_w, query_w, key_w, value_w, query_b, value_b, out_b, gain1, shift1 = done[3]
    vectors = [query_b, value_b, out_b, up_b, down_b, gain1, shift1, gain2, shift2]
    return (output, grad_tokens, query_w, key_w, value_w, out_w, up, down) + tuple(
        vector.reshape(-1) for vector in vectors
    )


def solution(mesh):
    cut = P("batch", "seq", None)
    in_specs = (cut, cut, P("batch", None)) + (P(),) * 15
    out_specs = (cut, cut) + (P(),) * 15
    return jax.shard_map(
        on_device, mesh=mesh, in_specs=in_specs, out_specs=out_specs, check_vma=False
    )
```

```python
import functools
import math

import jax
import jax.numpy as jnp
import numpy as np
from jax import lax
from jax.experimental import pallas as pl
from jax.experimental.pallas import tpu as pltpu
from jax.sharding import PartitionSpec as P

HEADS = 8
BLOCK = 16
UNIT = 1024
ROWS = 256
SUB = 64
QUAD = 4
HALO = 112
LOCAL = 3
GATHER = 32
NEAR_COLS = 256
PIECES = 32
SMALL = 16

NORM_EPS = 1e-05
LOG_TWO = math.log(2.0)
NEVER = -1e30
F32 = jnp.float32
BF16 = jnp.bfloat16


def dot(left, right):
    return jnp.dot(left, right, preferred_element_type=F32)


def dot_rows(left, right):
    return lax.dot_general(left, right, (((0,), (0,)), ((), ())), preferred_element_type=F32)


def dot_cols(left, right):
    return lax.dot_general(left, right, (((1,), (1,)), ((), ())), preferred_element_type=F32)


def two_parts(values):
    high = values.astype(BF16)
    return high, (values - high.astype(F32)).astype(BF16)


def normalize(values):
    centred = values - jnp.mean(values, axis=-1, keepdims=True)
    spread = jnp.mean(centred * centred, axis=-1, keepdims=True)
    scale = lax.rsqrt(spread + NORM_EPS)
    return centred * scale, scale


def norm_back(grad, normed, scale):
    return scale * (
        grad
        - jnp.mean(grad, axis=-1, keepdims=True)
        - normed * jnp.mean(grad * normed, axis=-1, keepdims=True)
    )


def normal_parts(upper):
    below = 0.5 + 0.5 * lax.erf(upper * math.sqrt(0.5))
    return below, jnp.exp(-0.5 * upper * upper) * (1.0 / math.sqrt(2.0 * math.pi))


def level_rows(level):
    return ROWS >> level


def pool_matrix(levels, rows=ROWS):
    line = lax.broadcasted_iota(jnp.int32, (rows, ROWS), 0)
    token = lax.broadcasted_iota(jnp.int32, (rows, ROWS), 1)
    matrix = jnp.zeros((rows, ROWS), F32)
    at = 0
    for level in range(1, levels + 1):
        if at < rows:
            mine = lax.shift_right_arithmetic(token, jnp.int32(level)) == line - at
            matrix = jnp.where(mine, 1.0 / (1 << level), matrix)
        at += level_rows(level)
    return matrix.astype(BF16)


POOL_AT = {1: 0, 2: 128, 3: 192}
POOLED = 224
HALO_AT = {0: (0, 16), 1: (16, 32), 2: (48, 32), 3: (80, 32)}


def key_list(sub, levels):
    out = []

    def add(column, level, first, last):
        own = level_rows(level)
        base, width = HALO_AT[level]
        low = min(last, 0)
        if first < low:
            out.append((column, low - first, "halo", base + width + first, 1))
            column += low - first
            first = low
        mid = min(last, own)
        if first < mid:
            if level == 0:
                out.append((column, mid - first, "own", first, 0))
            else:
                out.append((column, mid - first, "pool", POOL_AT[level] + first, 0))
            column += mid - first
            first = mid
        if first < last:
            out.append((column, last - first, "halo", HALO + base + first - own, 2))

    start = SUB * sub
    add(0, 0, start - 16, start + SUB + 16)
    row = 32 * sub
    add(96, 1, row - 32, row)
    add(128, 1, row + 32, row + 64)
    row = 32 * (sub // 2)
    add(160, 2, row - 32, row - 16)
    third = row + 32 if sub % 2 == 0 else row - 16
    add(176, 2, third, third + 16)
    add(192, 2, row + 48, row + 64)
    add(208, 3, -32, -16)
    third = 32 if sub < 2 else -16
    add(224, 3, third, third + 16)
    add(240, 3, 48, 64)
    far = 48 * (levels - LOCAL)
    out.append((NEAR_COLS, far, "halo", 2 * HALO, 3))
    return out


def columns_of(levels):
    return -(-(NEAR_COLS + 48 * (levels - LOCAL)) // 128) * 128


def score_bias(levels):
    cols = columns_of(levels)
    bias = np.full((SUB, cols), NEVER, np.float32)
    block = np.arange(SUB) // BLOCK
    for col in range(96):
        bias[:, col] = np.where(np.abs(col // BLOCK - 1 - block) <= 1, 0.0, NEVER)
    bias[:, 96:160] = LOG_TWO
    bias[:32, 112:128] = NEVER
    bias[32:, 128:144] = NEVER
    bias[:, 160:208] = 2 * LOG_TWO
    bias[:, 208:256] = 3 * LOG_TWO
    for level in range(LOCAL + 1, levels + 1):
        at = NEAR_COLS + 48 * (level - LOCAL - 1)
        bias[:, at : at + 48] = level * LOG_TWO
    return bias


def column_codes(levels):
    codes = np.zeros((8, columns_of(levels)), np.int32)
    for sub in range(ROWS // SUB):
        for column, rows, _, _, code in key_list(sub, levels):
            if code == 3:
                codes[sub, column : column + rows] = 3 + np.arange(rows) // BLOCK
            else:
                codes[sub, column : column + rows] = code
    return codes


def gather_at(level):
    return sum(level_rows(other) for other in range(LOCAL + 1, level))


def item_bounds(starts, place):
    unit = place * ROWS // UNIT
    low = starts[0, unit]
    count = jnp.int32(0)
    for other in range(starts.shape[1]):
        count = count + jnp.where(starts[0, other] == low, 1, 0).astype(jnp.int32)
    return low, low + count * UNIT


def extra_rows(holders):
    return GATHER if direct(holders) else 0


def far_blocks(place, levels):
    out = []
    for level in range(LOCAL + 1, levels + 1):
        mine = place * ROWS // (BLOCK << level)
        parent = mine // 2
        odd = mine - 2 * parent
        third = jnp.where(odd == 1, 2 * parent - 1, 2 * parent + 2)
        out.append((level, (2 * parent - 2, third, 2 * parent + 3)))
    return out


def direct(holders):
    return holders == 8


def pick_matrix(place, levels, holders):
    rows = []
    column = lax.broadcasted_iota(jnp.int32, (48, holders * GATHER), 1)
    line = lax.broadcasted_iota(jnp.int32, (48, holders * GATHER), 0)
    for level, blocks in far_blocks(place, levels):
        part = line // BLOCK
        block = jnp.where(part == 0, blocks[0], jnp.where(part == 1, blocks[1], blocks[2]))
        row = block * BLOCK + (line - part * BLOCK)
        shift = 8 - level
        owner = lax.shift_right_arithmetic(row, jnp.int32(shift))
        inside = row - owner * (1 << shift)
        if direct(holders):
            owner = jnp.where(owner < 0, -1, jnp.bitwise_xor(owner, place))
        wanted = owner * GATHER + gather_at(level) + inside
        rows.append(jnp.where(column == wanted, 1.0, 0.0))
    return jnp.concatenate(rows, axis=0).astype(BF16)


def head_masks(quad_cols, rows):
    lane = lax.broadcasted_iota(jnp.int32, (rows, quad_cols), 1)
    width = quad_cols // QUAD
    return [(lane >= width * h) & (lane < width * (h + 1)) for h in range(QUAD)]


def stack_heads(block, masks):
    zero = jnp.zeros_like(block)
    return jnp.concatenate([jnp.where(mask, block, zero) for mask in masks], axis=0)


def unstack_heads(block, masks):
    total = None
    for h, mask in enumerate(masks):
        part = jnp.where(mask, block[SUB * h : SUB * (h + 1)], 0.0)
        total = part if total is None else total + part
    return total


def my_piece():
    return (
        (lax.axis_index("seq") % 2) * 16
        + ((lax.axis_index("seq") // 2) % 4) * 4
        + lax.axis_index("batch") % 4
    )


def first_kernel(levels, tokens, inner, outer):
    normed, _ = normalize(tokens[0].astype(F32))
    high, low = two_parts(normed)
    pool = pool_matrix(levels)
    pooled = (dot(pool, high) + dot(pool, low)).astype(BF16)
    even = lax.axis_index("seq") % 2 == 0

    def put(at, first, last):
        rows = first.shape[0]
        inner[at : at + rows] = jnp.where(even, last, first)
        outer[at : at + rows] = jnp.where(even, first, last)

    put(0, high[:16], high[ROWS - 16 :])
    for level in range(1, LOCAL + 1):
        at, width = HALO_AT[level]
        base, own = POOL_AT[level], level_rows(level)
        put(at, pooled[base : base + width], pooled[base + own - width : base + own])
    inner[HALO:] = pooled[POOLED:]


def project_kernel(levels, count, *refs):
    sources, refs = refs[:count], refs[count:]
    held, (normed_out, query_out, key_out, value_out, key_pool, value_pool, sem) = (
        refs[:count],
        refs[count:],
    )
    copies = [pltpu.make_async_copy(*pair, sem.at[n]) for n, pair in enumerate(zip(sources, held))]
    for copy in copies:
        copy.start()
    tokens, gain, shift, query_w, query_b, key_w, value_w, value_b = [
        Fetched(ref, copy) for ref, copy in zip(held[:8], copies[:8])
    ]
    normed, _ = normalize(tokens[0].astype(F32))
    rows = (normed * gain[...] + shift[...]).astype(BF16)
    normed_out[...] = rows
    pool = pool_matrix(levels, POOLED)
    query = (dot(rows, query_w[...]) + query_b[...]).astype(BF16)
    query_out[...] = query * jnp.asarray(0.125, BF16)
    key = dot(rows, key_w[...]).astype(BF16)
    key_out[...] = key
    key_pool[...] = dot(pool, key).astype(BF16)
    value = (dot(rows, value_w[...]) + value_b[...]).astype(BF16)
    value_out[...] = value
    value_pool[...] = dot(pool, value).astype(BF16)
    for copy in copies[8:]:
        copy.wait()


def fill_keys(sub, levels, target, own, pool, halo):
    cols = columns_of(levels)
    used = NEAR_COLS + 48 * (levels - LOCAL)
    sources = {"own": own, "pool": pool, "halo": halo}
    for column, rows, source, row, _ in key_list(sub, levels):
        target[column : column + rows] = sources[source][row : row + rows]
    if cols > used:
        target[used:] = jnp.zeros((cols - used, target.shape[1]), BF16)


def middle_kernel(
    levels, holders, parts,
    starts, tokens, query, key, value, key_pool, value_pool, inner, outer,
    gain, shift, key_w, value_w, value_b, out_b, gain2, shift2, up_b, bias_table, codes,
    out_source, up_source, cot_source, down_source, *refs,
):
    windows, refs = refs[:parts], refs[parts:]
    (
    attended_out, weights_out, halo_out, key_halo, value_halo, mid_out, second_out, active_out,
    slope_out, keep, send, out_held, up_held, cot_held, down_held,
    key_cat, value_cat, attended, sums, small, sem, sources_sem,
    ) = refs
    pairs = (
        (out_source, out_held), (up_source, up_held), (cot_source, cot_held),
        (down_source, down_held),
    )
    brought = []
    for number, pair in enumerate(pairs):
        copy = pltpu.make_async_copy(*pair, sources_sem.at[number])
        copy.start()
        brought.append(Fetched(pair[1], copy))
    out_w, up_w, cotangent, down_w = brought
    width = tokens.shape[2]
    place = lax.axis_index("seq")
    low, high = item_bounds(starts, place)
    far = 48 * (levels - LOCAL)

    even = place % 2 == 0
    halo_out[0:HALO] = jnp.where(even, outer[...], inner[0:HALO])
    halo_out[HALO : 2 * HALO] = jnp.where(even, inner[0:HALO], outer[...])
    window = jnp.concatenate([ref[...] for ref in windows], axis=0)
    halo_out[2 * HALO :] = dot(pick_matrix(place, levels, holders), window).astype(BF16)
    scaled = (halo_out[...].astype(F32) * gain[...]).astype(BF16)
    shift_high, shift_low = two_parts(jnp.broadcast_to(shift[...], (16, width)))
    key_shift = (dot(shift_high, key_w[...]) + dot(shift_low, key_w[...]))[0:1]
    value_shift = (dot(shift_high, value_w[...]) + dot(shift_low, value_w[...]))[0:1]
    key_halo[...] = (dot(scaled, key_w[...]) + key_shift).astype(BF16)
    value_halo[...] = (dot(scaled, value_w[...]) + (value_shift + value_b[...])).astype(BF16)

    code = codes[...]
    allowed = [
        jnp.where(place * ROWS > low, 0.0, NEVER).astype(F32),
        jnp.where(place * ROWS + ROWS < high, 0.0, NEVER).astype(F32),
    ]
    for level, blocks in far_blocks(place, levels):
        span = BLOCK << level
        for block in blocks:
            inside = (block * span >= low) & (block * span + span <= high)
            allowed.append(jnp.where(inside, 0.0, NEVER).astype(F32))
    column_bias = jnp.zeros(code.shape, F32)
    for number, value_of in enumerate(allowed):
        column_bias = jnp.where(code == number + 1, value_of, column_bias)

    quad_cols = width * QUAD // HEADS
    masks = head_masks(quad_cols, SUB)
    for sub in range(ROWS // SUB):
        fill_keys(sub, levels, key_cat, key, key_pool, key_halo)
        fill_keys(sub, levels, value_cat, value, value_pool, value_halo)
        bias = bias_table[...] + column_bias[sub : sub + 1]
        bias = jnp.concatenate([bias] * QUAD, axis=0)
        for quad in range(HEADS // QUAD):
            lanes = slice(quad * quad_cols, (quad + 1) * quad_cols)
            stacked = stack_heads(query[SUB * sub : SUB * (sub + 1), lanes], masks)
            score = dot_cols(stacked, key_cat[:, lanes]) + bias
            score = jnp.exp(score - jnp.max(score, axis=1, keepdims=True))
            weight = score * (1.0 / jnp.sum(score, axis=1, keepdims=True))
            weight = weight.astype(BF16)
            weights_out[sub * (HEADS // QUAD) + quad] = weight
            mixed = unstack_heads(dot(weight, value_cat[:, lanes]), masks)
            attended[SUB * sub : SUB * (sub + 1), lanes] = mixed.astype(BF16)

    attended_out[...] = attended[...]
    mid = tokens[0].astype(F32) + dot(attended[...], out_w[...]) + out_b[...]
    normed, scale = normalize(mid)
    low_second = (normed * gain2[...] + shift2[...]).astype(BF16)
    cot = cotangent[0]
    hidden = up_w.shape[1]
    mid_out[...] = mid
    second_out[...] = low_second
    for at in range(0, hidden, width):
        cols = slice(at, at + width)
        upper = dot(low_second, up_w[:, cols]) + up_b[:, cols]
        below, phi = normal_parts(upper)
        slope_out[:, cols] = below + upper * phi
        active = (upper * below).astype(BF16)
        active_out[:, cols] = active
        grad_down = dot_rows(active, cot).astype(BF16)
        for piece in range(at // 64, (at + width) // 64):
            row = 64 * piece - at
            for part in range(width // 128):
                sums[slot_of(piece), 64 * part : 64 * (part + 1)] = grad_down[
                    row : row + 64, 128 * part : 128 * (part + 1)
                ]
    small[...] = jnp.zeros_like(small)
    put_vector(small, 0, jnp.sum(cot.astype(F32), axis=0, keepdims=True))
    put_small(sums, 256, small)
    copies = hand_out(sums, keep, [send], sem)
    down_w.wait()
    for copy in copies:
        copy.wait()


def feed_kernel(
    cotangent, mid, low_second, slope, gain2, up_w, down_w, out_w, attended,
    grad_mid_out, grad_attended, grad_out, out_b_sum, keep, *refs,
):
    sends, (sums, small, sem) = refs[:-3], refs[-3:]
    cot = cotangent[0]
    hidden, width = down_w.shape
    grad_second = jnp.zeros((ROWS, width), F32)
    small[...] = jnp.zeros_like(small)
    for at in range(0, hidden, width):
        cols = slice(at, at + width)
        grad_upper = (dot_cols(cot, down_w[cols]) * slope[:, cols]).astype(BF16)
        put_vector(small, at // 128, jnp.sum(grad_upper.astype(F32), axis=0, keepdims=True))
        put_lines(sums, at // 8, dot_rows(low_second[...], grad_upper).astype(BF16))
        grad_second = grad_second + dot_cols(grad_upper, up_w[:, cols])
    normed, scale = normalize(mid[...])
    put_vector(small, 16, jnp.sum(grad_second * normed, axis=0, keepdims=True))
    put_vector(small, 20, jnp.sum(grad_second, axis=0, keepdims=True))
    put_small(sums, 256, small)
    copies = hand_out(sums, keep, sends, sem)
    grad_mid = cot.astype(F32) + norm_back(grad_second * gain2[...], normed, scale)
    grad_mid_out[...] = grad_mid
    branch = grad_mid.astype(BF16)
    grad_attended[...] = dot_cols(branch, out_w[...]).astype(BF16)
    grad_out[...] = dot_rows(attended[...], branch).astype(BF16)
    out_b_sum[...] = jnp.sum(branch.astype(F32), axis=0, keepdims=True)
    for copy in copies:
        copy.wait()


FEED, BACK, BORROWED, LAST = "feed", "back", "borrowed", "last"
ORDER = (FEED, 1, 2, BACK, 1, 2, 1, 3, 2, 1, 3, BORROWED, 2, 1, 3, 2, 1, 3, 2, 3, 1, 2, 3, LAST, 2, 1, 3, 3)
STEP_PARTS = 1
Z_DIRECT = True
GROUP_ROWS = 256 + SMALL
MID_PARTS, LATE_PARTS = 2, 3


def put_vector(small, row, vector):
    for part in range(vector.shape[1] // 128):
        small[row + part : row + part + 1] = vector[:, 128 * part : 128 * (part + 1)]


def turned(place):
    return (place & 4) * 2 + (place // 2 & 4) + (place & 3)


def slot_of(piece):
    mine, place = my_piece() % 16, piece % 16
    if piece // 16 == 1:
        mine, place = turned(mine), turned(place)
    return (piece // 16) * 16 + jnp.bitwise_xor(mine, place)


def put_lines(sums, base, grad):
    for piece in range(PIECES):
        slot = slot_of(piece)
        for part in range(grad.shape[1] // 128):
            row = base + 16 * part
            sums[slot, row : row + 16] = grad[
                16 * piece : 16 * (piece + 1), 128 * part : 128 * (part + 1)
            ]


def put_small(sums, row, small):
    for piece in range(PIECES):
        if piece < 2:
            part = small[SMALL * piece : SMALL * (piece + 1)].astype(BF16)
        else:
            part = jnp.zeros((SMALL, 128), BF16)
        sums[slot_of(piece), row : row + SMALL] = part


def row_bounds(rows, parts):
    return [16 * (rows // 16 * part // parts) for part in range(parts)] + [rows]


def hand_out(sums, keep, sends, sem, first=0, last=None):
    mine = my_piece() // 16
    half = PIECES // 2
    last = keep.shape[1] if last is None else last
    bounds = row_bounds(keep.shape[1], len(sends))
    copies = []
    for ref, core, low, high in [(keep, mine, 0, keep.shape[1])] + [
        (send, 1 - mine, low, high) for send, low, high in zip(sends, bounds, bounds[1:])
    ]:
        start, end = max(first, low), min(last, high)
        if start < end:
            copies.append(
                pltpu.make_async_copy(
                    sums.at[pl.ds(core * half, half), pl.ds(start, end - start)],
                    ref.at[:, pl.ds(start - low, end - start)],
                    sem.at[len(copies)],
                )
            )
    for copy in copies:
        copy.start()
    return copies


def back_kernel(
    levels, holders,
    tokens, normed_low, query, key, value, key_pool, value_pool, halo, key_halo, value_halo,
    weights, grad_attended, grad_out, out_b_sum, gain, shift, query_w, key_w, value_w,
    grad_normed_out, inner, outer, keep, *refs,
):
    sends, owners, refs = refs[:LATE_PARTS], refs[LATE_PARTS:-13], refs[-13:]
    (
    key_cat, value_cat, grad_query, key_own, key_pooled, key_lent, value_own, value_pooled,
    value_lent, sums, small, sem, rest_sem,
    ) = refs
    width = tokens.shape[2]
    place = lax.axis_index("seq")
    far = 48 * (levels - LOCAL)
    for ref in (key_own, key_pooled, key_lent, value_own, value_pooled, value_lent):
        ref[...] = jnp.zeros_like(ref)
    key_sums = {"own": key_own, "pool": key_pooled, "halo": key_lent}
    value_sums = {"own": value_own, "pool": value_pooled, "halo": value_lent}

    quad_cols = width * QUAD // HEADS
    masks = head_masks(quad_cols, SUB)
    for sub in range(ROWS // SUB):
        fill_keys(sub, levels, key_cat, key, key_pool, key_halo)
        fill_keys(sub, levels, value_cat, value, value_pool, value_halo)
        rows = slice(SUB * sub, SUB * (sub + 1))
        for quad in range(HEADS // QUAD):
            lanes = slice(quad * quad_cols, (quad + 1) * quad_cols)
            stacked = stack_heads(query[rows, lanes], masks)
            grads = stack_heads(grad_attended[rows, lanes], masks)
            weight = weights[sub * (HEADS // QUAD) + quad]
            prob = weight.astype(F32)
            dprob = dot_cols(grads, value_cat[:, lanes])
            delta = jnp.sum(prob * dprob, axis=1, keepdims=True)
            dscore = (prob * (dprob - delta)).astype(BF16)
            mixed = unstack_heads(dot(dscore, key_cat[:, lanes]), masks)
            grad_query[rows, lanes] = (mixed * 0.125).astype(BF16)
            grad_keys = dot_rows(dscore, stacked)
            grad_values = dot_rows(weight, grads)
            for column, count, source, row, _ in key_list(sub, levels):
                key_sums[source][row : row + count, lanes] += grad_keys[column : column + count]
                value_sums[source][row : row + count, lanes] += grad_values[
                    column : column + count
                ]

    low_query = grad_query[...]
    pool = pool_matrix(levels, POOLED)
    low_key = (key_own[...] + dot_rows(pool, key_pooled[...].astype(BF16))).astype(BF16)
    low_value = (value_own[...] + dot_rows(pool, value_pooled[...].astype(BF16))).astype(BF16)
    lent_key = key_lent[...].astype(BF16)
    lent_value = value_lent[...].astype(BF16)
    lent_normed = halo[...].astype(F32)
    lent_low = (lent_normed * gain[...] + shift[...]).astype(BF16)
    rows = normed_low[...]

    put_lines(sums, 0, grad_out[...])
    put_lines(sums, 64, dot_rows(rows, low_query).astype(BF16))
    grad_key = dot_rows(rows, low_key) + dot_rows(lent_low, lent_key)
    put_lines(sums, 128, grad_key.astype(BF16))
    grad_value = dot_rows(rows, low_value) + dot_rows(lent_low, lent_value)
    put_lines(sums, 192, grad_value.astype(BF16))
    copies = hand_out(sums, keep, sends, sem, last=256)
    small[...] = jnp.zeros_like(small)

    def total(values):
        return jnp.sum(values.astype(F32), axis=0, keepdims=True)

    normed, _ = normalize(tokens[0].astype(F32))
    grad_normed = (
        dot_cols(low_query, query_w[...])
        + dot_cols(low_key, key_w[...])
        + dot_cols(low_value, value_w[...])
    )
    lent_grad = dot_cols(lent_key, key_w[...]) + dot_cols(lent_value, value_w[...])
    grad_normed_out[...] = grad_normed
    put_vector(small, 0, total(low_query))
    put_vector(small, 4, total(low_value) + total(lent_value))
    put_vector(small, 8, out_b_sum[...])
    put_vector(small, 12, total(grad_normed * normed) + total(lent_grad * lent_normed))
    put_vector(small, 16, total(grad_normed) + total(lent_grad))
    lent_grad = lent_grad.astype(BF16)
    even = place % 2 == 0
    inner[...] = jnp.where(even, lent_grad[HALO : 2 * HALO], lent_grad[:HALO])
    outer[...] = jnp.where(even, lent_grad[:HALO], lent_grad[HALO : 2 * HALO])
    pick = pick_matrix(place, levels, holders)
    returned = dot_rows(pick, lent_grad[2 * HALO :]).astype(BF16)
    if owners:
        owners[0][...] = returned
    else:
        for plane in range(4):
            for other in range(2):
                core = (place + other) % 2
                at = jnp.where(core == 1, turned(4 * plane), 4 * plane)
                rows = returned[GATHER * (2 * plane + other) :][:GATHER]
                for part in range(4):
                    slot = core * 16 + at + part
                    sums[slot, GROUP_ROWS:] = rows[:, 128 * part : 128 * (part + 1)]
    put_small(sums, 256, small)
    copies += hand_out(sums, keep, sends, rest_sem, first=256)
    for copy in copies:
        copy.wait()


def last_kernel(
    levels, tokens, gain, grad_mid, grad_normed, inner, outer, mid, active, down_w, down_b, *refs
):
    from_users, (grad_tokens, output, pooled) = refs[:-3], refs[-3:]
    output[0] = (mid[...] + dot(active[...], down_w[...]) + down_b[...]).astype(BF16)
    even = lax.axis_index("seq") % 2 == 0
    first = jnp.where(even, outer[...], inner[0:HALO]).astype(F32)
    last = jnp.where(even, inner[0:HALO], outer[...]).astype(F32)
    for level in range(1, LOCAL + 1):
        at, width = HALO_AT[level]
        base, own = POOL_AT[level], level_rows(level)
        pooled[base : base + own] = jnp.zeros((own, pooled.shape[1]), F32)
        pooled[base : base + width] += first[at : at + width]
        pooled[base + own - width : base + own] += last[at : at + width]
    if len(from_users) > 1:
        pooled[POOLED:] = functools.reduce(jnp.add, [ref[...].astype(F32) for ref in from_users])
    else:
        for part in range(4):
            pooled[POOLED:, 128 * part : 128 * (part + 1)] = from_users[0][part].astype(F32)
    high, low = two_parts(pooled[...])
    pool = pool_matrix(levels)
    gap = jnp.zeros((ROWS - 32, first.shape[1]), F32)
    grad = grad_normed[...] + dot_rows(pool, high) + dot_rows(pool, low)
    grad = grad + jnp.concatenate([first[:16], gap, last[:16]], axis=0)
    normed, scale = normalize(tokens[0].astype(F32))
    grad_tokens[0] = grad_mid[...] + norm_back(grad * gain[...], normed, scale)


def collect_kernel(kind, *refs):
    blocks, refs, small = refs[:4], refs[4:-1], refs[-1]
    me = my_piece()
    squares = 4 if kind == 2 else 1
    grads, order = refs[:squares], refs[squares:]

    for core in range(2):
        odd = (me // 16 + core) % 2 == 1
        for plane in range(4):
            for depth in range(4):
                place = 4 * plane + depth
                place = jnp.where(odd, turned(place), place)
                piece = jnp.bitwise_xor(me, core * 16 + place)
                block = blocks[2 * core + plane % 2]

                def held(row, rows, block=block, plane=plane, depth=depth):
                    return block[plane // 2, depth, row : row + rows].astype(F32)

                lines = pl.ds(pl.multiple_of(piece * 16, 16), 16)
                if kind == 0:
                    (down,) = grads
                    rows = pl.ds(pl.multiple_of(piece * 64, 64), 64)
                    for part in range(down.shape[1] // 128):
                        down[rows, 128 * part : 128 * (part + 1)] = held(64 * part, 64)
                else:
                    base = 0
                    for grad in grads:
                        for part in range(grad.shape[1] // 128):
                            grad[lines, 128 * part : 128 * (part + 1)] = held(base, 16)
                            base += 16

                @pl.when(piece < 2)
                def _(held=held, lines=lines):
                    small[lines] = held(256, SMALL)

    at = 0
    for ref in order:
        ref[...] = small[at : at + ref.shape[0]]
        at += ref.shape[0]


class Fetched:
    def __init__(self, ref, copy):
        self.ref = ref
        self.copy = copy
        self.shape = ref.shape

    def wait(self):
        if self.copy is not None:
            self.copy.wait()
            self.copy = None

    def __getitem__(self, at):
        self.wait()
        return self.ref[at]


def call(
    kernel, inputs, outputs, scratch=(), smem=0, room=16, far_in=(), far_out=(), alias=None, pinned=()
):
    inputs = list(inputs)
    in_space = [pltpu.SMEM] * smem + [pltpu.VMEM] * (len(inputs) - smem)
    out_space = [pltpu.VMEM] * len(outputs)
    for at in far_in:
        in_space[at] = pl.ANY
    for at in pinned:
        inputs[at] = pltpu.with_memory_space_constraint(inputs[at], pltpu.HBM)
        in_space[at] = pltpu.HBM
    for at in far_out:
        out_space[at] = pl.ANY
    return pl.pallas_call(
        kernel,
        out_shape=[jax.ShapeDtypeStruct(s, d) for s, d in outputs],
        in_specs=[pl.BlockSpec(memory_space=s) for s in in_space],
        out_specs=[pl.BlockSpec(memory_space=s) for s in out_space],
        scratch_shapes=[pltpu.VMEM(*s) if isinstance(s, tuple) else s for s in scratch],
        input_output_aliases=alias or {},
        compiler_params=pltpu.CompilerParams(vmem_limit_bytes=room * 1024 * 1024),
        cost_estimate=pl.CostEstimate(flops=0, bytes_accessed=0, transcendentals=0),
    )(*inputs)


def swap(array, axis, distance):
    count = lax.axis_size(axis)
    return lax.ppermute(array, axis, [(i, i ^ distance) for i in range(count)])


def swap_outer(array, axis):
    count = lax.axis_size(axis)
    pairs = [(i, i + 1) for i in range(1, count - 1, 2)]
    return lax.ppermute(array, axis, pairs + [(j, i) for i, j in pairs])


def after(value, *others):
    return lax.optimization_barrier((value, others))[0]


def planes(array):
    return [swap(array, "seq", 2 * plane) for plane in (3, 1, 2)]


def hop(array, step):
    pairs = []
    for place in range(lax.axis_size("seq")):
        bit = 2 << (step if place % 2 == 0 else 1 - step)
        pairs.append((place, place ^ bit))
    return lax.ppermute(array, "seq", pairs)


def sum_of(*values):
    total = values[0].astype(F32)
    for value in values[1:]:
        total = total + value.astype(F32)
    return total.astype(BF16)


def halves_kernel(count, kept, *refs):
    came, (kept_out, *sends) = refs[:count], refs[count:]
    for slot in range(kept.shape[0]):
        first = 0
        for ref in came:
            last = first + ref.shape[-2]
            total = sum_of(kept[slot, ..., first:last, :], ref[slot])
            if slot % 2 == 0:
                kept_out[slot // 2, ..., first:last, :] = total
            else:
                row = 0
                for send in sends:
                    end = row + send.shape[-2]
                    low, high = max(first, row), min(last, end)
                    if low < high:
                        send[slot // 2, ..., low - row : high - row, :] = total[
                            ..., low - first : high - first, :
                        ]
                    row = end
            first = last


def add_halves(kept, *came, parts=1):
    half, rows = (kept.shape[0] // 2, *kept.shape[1:-2]), kept.shape[-2]
    bounds = row_bounds(rows, parts)
    sends = [((*half, last - first, 128), BF16) for first, last in zip(bounds, bounds[1:])]
    kernel = functools.partial(halves_kernel, len(came))
    kept, *sends = call(kernel, (kept, *came), [((*half, rows, 128), BF16), *sends], room=12)
    return (sends[0] if parts == 1 else sends), kept


def plane_kernel(extra, kept, came, sent_out, kept_out, *complete):
    rows = kept.shape[1] - extra
    for depth in range(4):
        total = sum_of(kept[depth], came[depth])
        (kept_out, sent_out)[depth % 2][depth // 2] = total[:rows]
        if extra:
            complete[0][depth] = total[rows:]


def add_plane(kept, came, extra):
    rows = kept.shape[1] - extra
    outputs = [((2, rows, 128), BF16)] * 2
    if extra:
        outputs.append(((4, extra, 128), BF16))
    return call(functools.partial(plane_kernel, extra), (kept, came), outputs, room=8)


def plane_direct_kernel(extra, kept, came, *outs):
    rows = kept.shape[1] - extra
    for depth in range(4):
        total = sum_of(kept[depth], came[depth])
        outs[depth][...] = total[:rows]
        if extra:
            outs[4][depth] = total[rows:]


def add_plane_direct(kept, came, extra):
    rows = kept.shape[1] - extra
    outputs = [((rows, 128), BF16)] * 4
    if extra:
        outputs.append(((4, extra, 128), BF16))
    outs = call(functools.partial(plane_direct_kernel, extra), (kept, came), outputs, room=8)
    return [*outs[:4], list(outs[4:])]


def column_kernel(whole, two, three, one, out):
    for depth, ref in enumerate((whole, one, two, three)):
        out[0, depth] = ref[...]


def column_of(whole, came):
    (column,) = call(column_kernel, (whole, *came), [((1, 4, *whole.shape), BF16)], room=8)
    return column


def whole_kernel(*refs):
    refs[-1][...] = sum_of(*[ref[...] for ref in refs[:-1]])


def add_whole(mine, *came):
    (whole,) = call(whole_kernel, (mine, *came), [(mine.shape, BF16)], room=8)
    distance = 8
    while distance < lax.axis_size("seq"):
        other = swap(whole, "seq", distance)
        (whole,) = call(whole_kernel, (whole, other), [(mine.shape, BF16)], room=8)
        distance *= 2
    return whole


def joined_kernel(mine, came, out):
    for slot in range(mine.shape[0]):
        out[2 * slot] = mine[slot]
        out[2 * slot + 1] = came[slot]


def join(mine, came):
    (out,) = call(joined_kernel, (mine, came), [((2 * mine.shape[0], *mine.shape[1:]), BF16)], room=8)
    return out


class Group:
    def __init__(self, keep, sends, parts=1):
        self.kept = slots(keep)
        self.parts = parts
        self.came = [slots(swap(send, "seq", 1)) for send in sends]
        self.stage = 0
        self.users = []

    def step(self, last, extra):
        stage, kept = self.stage, self.kept
        came = after(self.came, last)
        self.stage += 1
        if stage == 0:
            sent, self.kept = add_halves(kept, *came, parts=self.parts)
            self.came = hop(sent, 0) if self.parts == 1 else [hop(part, 0) for part in sent]
        elif stage == 1:
            sent, kept = add_halves(kept, *(came if self.parts > 1 else [came]))
            self.kept = kept[0]
            self.came = hop(sent[0], 1)
        elif stage == 2 and Z_DIRECT:
            *self.kept, self.users = add_plane_direct(kept, came, extra)
            self.came = [swap(self.kept[depth], "batch", depth) for depth in (2, 3, 1)]
            self.stage = 4
        elif stage == 4 and Z_DIRECT:
            self.kept = add_whole(kept[0], *came)
            self.came = [swap(self.kept, "batch", depth) for depth in (2, 3, 1)]
            self.stage = 6
        elif stage == 6 and Z_DIRECT:
            self.kept = column_of(kept, came)
            self.came = hop(self.kept, 1)
        elif stage == 2:
            sent, self.kept, *self.users = add_plane(kept, came, extra)
            self.came = swap(sent, "batch", 1)
        elif stage == 3:
            sent, kept = add_halves(kept, came)
            self.kept = kept[0]
            self.came = swap(sent[0], "batch", 2)
        elif stage == 4:
            self.kept = add_whole(kept, came)[None]
            self.came = swap(self.kept, "batch", 2)
        elif stage == 5:
            self.kept = join(kept, came)
            self.came = swap(self.kept, "batch", 1)
        elif stage == 6:
            self.kept = join(kept, came)[None]
            self.came = hop(self.kept, 1)
        elif stage == 7:
            self.kept = join(kept, came)
            self.came = hop(self.kept, 0)
        else:
            self.sums = [kept, came]
            self.sums += [swap(block, "seq", 1) for block in self.sums]
            return came
        return self.kept[0] if isinstance(self.kept, list) else self.kept


def slots(array):
    return array.reshape(-1, 4, *array.shape[1:])


def plane_of(column, came):
    return [column, came[1], came[2], came[0]]


def chip_kernel(inner, came, chip):
    chip[0:GATHER] = inner[HALO:]
    chip[GATHER:] = came[HALO:]


def share(inner, came):
    if not direct(lax.axis_size("seq")):
        return [lax.all_gather(inner[HALO:], "seq", axis=0, tiled=True)]
    (chip,) = call(chip_kernel, (inner, came), [((2 * GATHER, inner.shape[1]), BF16)], room=8)
    return plane_of(chip, planes(chip))


def on_device(
    tokens, cotangent, item_start, first_gain, first_shift, query_weight, query_bias, key_weight,
    value_weight, value_bias, out_weight, out_bias, second_gain, second_shift, up_weight, up_bias,
    down_weight, down_bias,
):
    width = tokens.shape[2]
    hidden = up_weight.shape[1]
    holders = lax.axis_size("seq")
    levels = (ROWS * holders // (4 * BLOCK)).bit_length() - 1
    far = 48 * (levels - LOCAL)
    lent = 2 * HALO + far

    cols = columns_of(levels)
    groups = (ROWS // SUB) * (HEADS // QUAD)
    bias_table = jnp.asarray(score_bias(levels))
    codes = jnp.asarray(column_codes(levels))

    def row(vector):
        return vector.reshape(1, -1)

    gain, shift = row(first_gain), row(first_shift)
    inner, outer = call(
        functools.partial(first_kernel, levels),
        (tokens,),
        [((HALO + GATHER, width), BF16), ((HALO, width), BF16)],
        room=8,
    )
    inner_came = swap(inner, "seq", 1)
    outer_came = swap_outer(outer, "seq")
    windows = share(inner, inner_came)
    carried = (
        tokens, gain, shift, query_weight, row(query_bias), key_weight, value_weight,
        row(value_bias), row(out_bias), row(second_gain), row(second_shift), row(up_bias),
        row(down_bias), bias_table, codes,
    )
    count = len(carried)
    *carried, normed_low, query, key, value, key_pool, value_pool = call(
        functools.partial(project_kernel, levels, count),
        carried,
        [(a.shape, a.dtype) for a in carried]
        + [((ROWS, width), BF16)] * 4
        + [((POOLED, width), BF16)] * 2,
        scratch=[pltpu.SemaphoreType.DMA((count,))],
        pinned=range(count),
        room=24,
    )
    (
        tokens, gain, shift, query_weight, _, key_weight, value_weight, value_bias, out_bias,
        second_gain, second_shift, up_bias, down_bias, bias_table, codes,
    ) = carried
    extra = extra_rows(holders)
    owner_shapes = [] if extra else [((holders * GATHER, width), BF16)]
    half = PIECES // 2
    copies = pltpu.SemaphoreType.DMA((1 + max(MID_PARTS, LATE_PARTS),))

    def piece_sums(parts, rows=GROUP_ROWS):
        bounds = row_bounds(rows, parts)
        sends = [((half, last - first, 128), BF16) for first, last in zip(bounds, bounds[1:])]
        return [((half, rows, 128), BF16)] + sends

    sums_scratch = ((PIECES, GROUP_ROWS, 128), BF16)
    small_scratch = ((2 * SMALL, 128), F32)
    (
        attended, weights, halo, key_halo, value_halo, mid, low_second, active, slope, keep, send,
        out_weight, up_weight, cotangent, down_weight,
    ) = call(
        functools.partial(middle_kernel, levels, holders, len(windows)),
        (
            item_start, tokens, query, key, value, key_pool, value_pool, inner_came, outer_came,
            gain, shift, key_weight, value_weight, value_bias, out_bias, second_gain, second_shift,
            up_bias, bias_table, codes, out_weight, up_weight, cotangent, down_weight, *windows,
        ),
        [
            ((ROWS, width), BF16),
            ((groups, QUAD * SUB, cols), BF16),
            ((lent, width), BF16),
            ((lent, width), BF16),
            ((lent, width), BF16),
            ((ROWS, width), F32),
            ((ROWS, width), BF16),
            ((ROWS, hidden), BF16),
            ((ROWS, hidden), F32),
        ]
        + piece_sums(1)
        + [(a.shape, a.dtype) for a in (out_weight, up_weight, cotangent, down_weight)],
        scratch=[
            ((cols, width), BF16),
            ((cols, width), BF16),
            ((ROWS, width), BF16),
            sums_scratch,
            small_scratch,
            copies,
            pltpu.SemaphoreType.DMA((4,)),
        ],
        smem=1,
        far_in=(20, 21, 22, 23),
        pinned=(20, 21, 22, 23),
        far_out=(9, 10),
        room=24,
    )
    lines = width // 128
    small = ((lines, 128), F32)
    square = ((width, width), F32)
    collected = {
        1: [((hidden, width), F32), small],
        2: [((width, hidden), F32), ((hidden // 128, 128), F32), small, small],
        3: [square] * 4 + [small] * 5,
    }
    sums = {1: Group(keep, [send])}
    done = {}
    last = ()
    for what in ORDER:
        if what == FEED:
            grad_mid, grad_attended, grad_out, out_b_sum, keep, *sends = call(
                feed_kernel,
                (
                    cotangent, after(mid, last), low_second, slope, second_gain, up_weight, down_weight,
                    out_weight, attended,
                ),
                [
                    ((ROWS, width), F32),
                    ((ROWS, width), BF16),
                    ((width, width), BF16),
                    ((1, width), F32),
                ]
                + piece_sums(MID_PARTS),
                scratch=[sums_scratch, small_scratch, copies],
                far_out=range(4, 5 + MID_PARTS),
                room=24,
            )
            sums[2] = Group(keep, sends)
            last = grad_attended
        elif what == BACK:
            grad_normed, inner, outer, keep, *sends = call(
                functools.partial(back_kernel, levels, holders),
                (
                    tokens, normed_low, after(query, last), key, value, key_pool, value_pool, halo, key_halo,
                    value_halo, weights, grad_attended, grad_out, out_b_sum, gain, shift, query_weight,
                    key_weight, value_weight,
                ),
                [
                    ((ROWS, width), F32),
                    ((HALO, width), BF16),
                    ((HALO, width), BF16),
                ]
                + piece_sums(LATE_PARTS, GROUP_ROWS + extra)
                + owner_shapes,
                scratch=[
                    ((cols, width), BF16),
                    ((cols, width), BF16),
                    ((ROWS, width), BF16),
                    ((ROWS, width), F32),
                    ((POOLED, width), F32),
                    ((lent, width), F32),
                    ((ROWS, width), F32),
                    ((POOLED, width), F32),
                    ((lent, width), F32),
                    ((PIECES, GROUP_ROWS + extra, 128), BF16),
                    small_scratch,
                    copies,
                    copies,
                ],
                far_out=range(3, 4 + LATE_PARTS),
                room=28,
            )
            sends, owners = sends[:LATE_PARTS], sends[LATE_PARTS:]
            sums[3] = Group(keep, sends, STEP_PARTS)
            inner_came = swap(inner, "seq", 1)
            outer_came = swap_outer(outer, "seq")
            last = grad_normed
        elif what == LAST:
            users = sums[3].users
            if not extra:
                rows = owners[0].reshape(holders, GATHER, width)
                users = list(lax.all_to_all(rows, "seq", split_axis=0, concat_axis=0, tiled=True))
            grad_tokens, output = call(
                functools.partial(last_kernel, levels),
                (
                    tokens, gain, grad_mid, after(grad_normed, last), inner_came, outer_came, mid,
                    active, down_weight, down_bias, *users,
                ),
                [((1, ROWS, width), F32), ((1, ROWS, width), BF16)],
                scratch=[((ROWS, width), F32)],
                room=12,
            )
            last = grad_tokens
        elif what == BORROWED:
            inner_came, outer_came = after((inner_came, outer_came), last)
            last = (inner_came, outer_came)
        elif sums[what].stage < 9:
            last = sums[what].step(last, extra if what == 3 else 0)
        else:
            done[what] = call(
                functools.partial(collect_kernel, what - 1),
                after(sums[what].sums, last),
                collected[what],
                scratch=[((PIECES * SMALL, 128), F32)],
                room=16,
            )
            last = done[what][-1]
    down, down_b = done[1]
    up, up_b, gain2, shift2 = done[2]
    out_w, query_w, key_w, value_w, query_b, value_b, out_b, gain1, shift1 = done[3]
    vectors = [query_b, value_b, out_b, up_b, down_b, gain1, shift1, gain2, shift2]
    return (output, grad_tokens, query_w, key_w, value_w, out_w, up, down) + tuple(
        vector.reshape(-1) for vector in vectors
    )


def solution(mesh):
    cut = P("batch", "seq", None)
    in_specs = (cut, cut, P("batch", None)) + (P(),) * 15
    out_specs = (cut, cut) + (P(),) * 15
    return jax.shard_map(
        on_device, mesh=mesh, in_specs=in_specs, out_specs=out_specs, check_vma=False
    )
```

```python
import functools
import math

import jax
import jax.numpy as jnp
import numpy as np
from jax import lax
from jax.experimental import pallas as pl
from jax.experimental.pallas import tpu as pltpu
from jax.sharding import PartitionSpec as P

HEADS = 8
BLOCK = 16
UNIT = 1024
ROWS = 256
SUB = 64
QUAD = 4
HALO = 112
LOCAL = 3
GATHER = 32
NEAR_COLS = 256
PIECES = 32
SMALL = 16

NORM_EPS = 1e-05
LOG_TWO = math.log(2.0)
NEVER = -1e30
F32 = jnp.float32
BF16 = jnp.bfloat16


def dot(left, right):
    return jnp.dot(left, right, preferred_element_type=F32)


def dot_rows(left, right):
    return lax.dot_general(left, right, (((0,), (0,)), ((), ())), preferred_element_type=F32)


def dot_cols(left, right):
    return lax.dot_general(left, right, (((1,), (1,)), ((), ())), preferred_element_type=F32)


def two_parts(values):
    high = values.astype(BF16)
    return high, (values - high.astype(F32)).astype(BF16)


def normalize(values):
    centred = values - jnp.mean(values, axis=-1, keepdims=True)
    spread = jnp.mean(centred * centred, axis=-1, keepdims=True)
    scale = lax.rsqrt(spread + NORM_EPS)
    return centred * scale, scale


def norm_back(grad, normed, scale):
    return scale * (
        grad
        - jnp.mean(grad, axis=-1, keepdims=True)
        - normed * jnp.mean(grad * normed, axis=-1, keepdims=True)
    )


def normal_parts(upper):
    below = 0.5 + 0.5 * lax.erf(upper * math.sqrt(0.5))
    return below, jnp.exp(-0.5 * upper * upper) * (1.0 / math.sqrt(2.0 * math.pi))


def level_rows(level):
    return ROWS >> level


def pool_matrix(levels, rows=ROWS):
    line = lax.broadcasted_iota(jnp.int32, (rows, ROWS), 0)
    token = lax.broadcasted_iota(jnp.int32, (rows, ROWS), 1)
    matrix = jnp.zeros((rows, ROWS), F32)
    at = 0
    for level in range(1, levels + 1):
        if at < rows:
            mine = lax.shift_right_arithmetic(token, jnp.int32(level)) == line - at
            matrix = jnp.where(mine, 1.0 / (1 << level), matrix)
        at += level_rows(level)
    return matrix.astype(BF16)


POOL_AT = {1: 0, 2: 128, 3: 192}
POOLED = 224
HALO_AT = {0: (0, 16), 1: (16, 32), 2: (48, 32), 3: (80, 32)}


def key_list(sub, levels):
    out = []

    def add(column, level, first, last):
        own = level_rows(level)
        base, width = HALO_AT[level]
        low = min(last, 0)
        if first < low:
            out.append((column, low - first, "halo", base + width + first, 1))
            column += low - first
            first = low
        mid = min(last, own)
        if first < mid:
            if level == 0:
                out.append((column, mid - first, "own", first, 0))
            else:
                out.append((column, mid - first, "pool", POOL_AT[level] + first, 0))
            column += mid - first
            first = mid
        if first < last:
            out.append((column, last - first, "halo", HALO + base + first - own, 2))

    start = SUB * sub
    add(0, 0, start - 16, start + SUB + 16)
    row = 32 * sub
    add(96, 1, row - 32, row)
    add(128, 1, row + 32, row + 64)
    row = 32 * (sub // 2)
    add(160, 2, row - 32, row - 16)
    third = row + 32 if sub % 2 == 0 else row - 16
    add(176, 2, third, third + 16)
    add(192, 2, row + 48, row + 64)
    add(208, 3, -32, -16)
    third = 32 if sub < 2 else -16
    add(224, 3, third, third + 16)
    add(240, 3, 48, 64)
    far = 48 * (levels - LOCAL)
    out.append((NEAR_COLS, far, "halo", 2 * HALO, 3))
    return out


def columns_of(levels):
    return -(-(NEAR_COLS + 48 * (levels - LOCAL)) // 128) * 128


def score_bias(levels):
    cols = columns_of(levels)
    bias = np.full((SUB, cols), NEVER, np.float32)
    block = np.arange(SUB) // BLOCK
    for col in range(96):
        bias[:, col] = np.where(np.abs(col // BLOCK - 1 - block) <= 1, 0.0, NEVER)
    bias[:, 96:160] = LOG_TWO
    bias[:32, 112:128] = NEVER
    bias[32:, 128:144] = NEVER
    bias[:, 160:208] = 2 * LOG_TWO
    bias[:, 208:256] = 3 * LOG_TWO
    for level in range(LOCAL + 1, levels + 1):
        at = NEAR_COLS + 48 * (level - LOCAL - 1)
        bias[:, at : at + 48] = level * LOG_TWO
    return bias


def column_codes(levels):
    codes = np.zeros((8, columns_of(levels)), np.int32)
    for sub in range(ROWS // SUB):
        for column, rows, _, _, code in key_list(sub, levels):
            if code == 3:
                codes[sub, column : column + rows] = 3 + np.arange(rows) // BLOCK
            else:
                codes[sub, column : column + rows] = code
    return codes


def gather_at(level):
    return sum(level_rows(other) for other in range(LOCAL + 1, level))


def item_bounds(starts, place):
    unit = place * ROWS // UNIT
    low = starts[0, unit]
    count = jnp.int32(0)
    for other in range(starts.shape[1]):
        count = count + jnp.where(starts[0, other] == low, 1, 0).astype(jnp.int32)
    return low, low + count * UNIT


def extra_rows(holders):
    return GATHER if direct(holders) else 0


def far_blocks(place, levels):
    out = []
    for level in range(LOCAL + 1, levels + 1):
        mine = place * ROWS // (BLOCK << level)
        parent = mine // 2
        odd = mine - 2 * parent
        third = jnp.where(odd == 1, 2 * parent - 1, 2 * parent + 2)
        out.append((level, (2 * parent - 2, third, 2 * parent + 3)))
    return out


def direct(holders):
    return holders == 8


def pick_matrix(place, levels, holders):
    rows = []
    column = lax.broadcasted_iota(jnp.int32, (48, holders * GATHER), 1)
    line = lax.broadcasted_iota(jnp.int32, (48, holders * GATHER), 0)
    for level, blocks in far_blocks(place, levels):
        part = line // BLOCK
        block = jnp.where(part == 0, blocks[0], jnp.where(part == 1, blocks[1], blocks[2]))
        row = block * BLOCK + (line - part * BLOCK)
        shift = 8 - level
        owner = lax.shift_right_arithmetic(row, jnp.int32(shift))
        inside = row - owner * (1 << shift)
        if direct(holders):
            owner = jnp.where(owner < 0, -1, jnp.bitwise_xor(owner, place))
        wanted = owner * GATHER + gather_at(level) + inside
        rows.append(jnp.where(column == wanted, 1.0, 0.0))
    return jnp.concatenate(rows, axis=0).astype(BF16)


def head_masks(quad_cols, rows):
    lane = lax.broadcasted_iota(jnp.int32, (rows, quad_cols), 1)
    width = quad_cols // QUAD
    return [(lane >= width * h) & (lane < width * (h + 1)) for h in range(QUAD)]


def stack_heads(block, masks):
    zero = jnp.zeros_like(block)
    return jnp.concatenate([jnp.where(mask, block, zero) for mask in masks], axis=0)


def unstack_heads(block, masks):
    total = None
    for h, mask in enumerate(masks):
        part = jnp.where(mask, block[SUB * h : SUB * (h + 1)], 0.0)
        total = part if total is None else total + part
    return total


def my_piece():
    return (
        (lax.axis_index("seq") % 2) * 16
        + ((lax.axis_index("seq") // 2) % 4) * 4
        + lax.axis_index("batch") % 4
    )


def first_kernel(levels, tokens, inner, outer):
    normed, _ = normalize(tokens[0].astype(F32))
    high, low = two_parts(normed)
    pool = pool_matrix(levels)
    pooled = (dot(pool, high) + dot(pool, low)).astype(BF16)
    even = lax.axis_index("seq") % 2 == 0

    def put(at, first, last):
        rows = first.shape[0]
        inner[at : at + rows] = jnp.where(even, last, first)
        outer[at : at + rows] = jnp.where(even, first, last)

    put(0, high[:16], high[ROWS - 16 :])
    for level in range(1, LOCAL + 1):
        at, width = HALO_AT[level]
        base, own = POOL_AT[level], level_rows(level)
        put(at, pooled[base : base + width], pooled[base + own - width : base + own])
    inner[HALO:] = pooled[POOLED:]


def project_kernel(levels, count, *refs):
    sources, refs = refs[:count], refs[count:]
    held, (normed_out, query_out, key_out, value_out, key_pool, value_pool, sem) = (
        refs[:count],
        refs[count:],
    )
    copies = [pltpu.make_async_copy(*pair, sem.at[n]) for n, pair in enumerate(zip(sources, held))]
    for copy in copies:
        copy.start()
    tokens, gain, shift, query_w, query_b, key_w, value_w, value_b = [
        Fetched(ref, copy) for ref, copy in zip(held[:8], copies[:8])
    ]
    normed, _ = normalize(tokens[0].astype(F32))
    rows = (normed * gain[...] + shift[...]).astype(BF16)
    normed_out[...] = rows
    pool = pool_matrix(levels, POOLED)
    query = (dot(rows, query_w[...]) + query_b[...]).astype(BF16)
    query_out[...] = query * jnp.asarray(0.125, BF16)
    key = dot(rows, key_w[...]).astype(BF16)
    key_out[...] = key
    key_pool[...] = dot(pool, key).astype(BF16)
    value = (dot(rows, value_w[...]) + value_b[...]).astype(BF16)
    value_out[...] = value
    value_pool[...] = dot(pool, value).astype(BF16)
    for copy in copies[8:]:
        copy.wait()


def fill_keys(sub, levels, target, own, pool, halo):
    cols = columns_of(levels)
    used = NEAR_COLS + 48 * (levels - LOCAL)
    sources = {"own": own, "pool": pool, "halo": halo}
    for column, rows, source, row, _ in key_list(sub, levels):
        target[column : column + rows] = sources[source][row : row + rows]
    if cols > used:
        target[used:] = jnp.zeros((cols - used, target.shape[1]), BF16)


def middle_kernel(
    levels, holders, parts,
    starts, tokens, query, key, value, key_pool, value_pool, inner, outer,
    gain, shift, key_w, value_w, value_b, out_b, gain2, shift2, up_b, bias_table, codes,
    out_source, up_source, cot_source, down_source, *refs,
):
    windows, refs = refs[:parts], refs[parts:]
    (
    attended_out, weights_out, halo_out, key_halo, value_halo, mid_out, second_out, active_out,
    slope_out, keep, send, out_held, up_held, cot_held, down_held,
    key_cat, value_cat, attended, sums, small, sem, sources_sem,
    ) = refs
    pairs = (
        (out_source, out_held), (up_source, up_held), (cot_source, cot_held),
        (down_source, down_held),
    )
    brought = []
    for number, pair in enumerate(pairs):
        copy = pltpu.make_async_copy(*pair, sources_sem.at[number])
        copy.start()
        brought.append(Fetched(pair[1], copy))
    out_w, up_w, cotangent, down_w = brought
    width = tokens.shape[2]
    place = lax.axis_index("seq")
    low, high = item_bounds(starts, place)
    far = 48 * (levels - LOCAL)

    even = place % 2 == 0
    halo_out[0:HALO] = jnp.where(even, outer[...], inner[0:HALO])
    halo_out[HALO : 2 * HALO] = jnp.where(even, inner[0:HALO], outer[...])
    window = jnp.concatenate([ref[...] for ref in windows], axis=0)
    halo_out[2 * HALO :] = dot(pick_matrix(place, levels, holders), window).astype(BF16)
    scaled = (halo_out[...].astype(F32) * gain[...]).astype(BF16)
    shift_high, shift_low = two_parts(jnp.broadcast_to(shift[...], (16, width)))
    key_shift = (dot(shift_high, key_w[...]) + dot(shift_low, key_w[...]))[0:1]
    value_shift = (dot(shift_high, value_w[...]) + dot(shift_low, value_w[...]))[0:1]
    key_halo[...] = (dot(scaled, key_w[...]) + key_shift).astype(BF16)
    value_halo[...] = (dot(scaled, value_w[...]) + (value_shift + value_b[...])).astype(BF16)

    code = codes[...]
    allowed = [
        jnp.where(place * ROWS > low, 0.0, NEVER).astype(F32),
        jnp.where(place * ROWS + ROWS < high, 0.0, NEVER).astype(F32),
    ]
    for level, blocks in far_blocks(place, levels):
        span = BLOCK << level
        for block in blocks:
            inside = (block * span >= low) & (block * span + span <= high)
            allowed.append(jnp.where(inside, 0.0, NEVER).astype(F32))
    column_bias = jnp.zeros(code.shape, F32)
    for number, value_of in enumerate(allowed):
        column_bias = jnp.where(code == number + 1, value_of, column_bias)

    quad_cols = width * QUAD // HEADS
    masks = head_masks(quad_cols, SUB)
    for sub in range(ROWS // SUB):
        fill_keys(sub, levels, key_cat, key, key_pool, key_halo)
        fill_keys(sub, levels, value_cat, value, value_pool, value_halo)
        bias = bias_table[...] + column_bias[sub : sub + 1]
        bias = jnp.concatenate([bias] * QUAD, axis=0)
        for quad in range(HEADS // QUAD):
            lanes = slice(quad * quad_cols, (quad + 1) * quad_cols)
            stacked = stack_heads(query[SUB * sub : SUB * (sub + 1), lanes], masks)
            score = dot_cols(stacked, key_cat[:, lanes]) + bias
            score = jnp.exp(score - jnp.max(score, axis=1, keepdims=True))
            weight = score * (1.0 / jnp.sum(score, axis=1, keepdims=True))
            weight = weight.astype(BF16)
            weights_out[sub * (HEADS // QUAD) + quad] = weight
            mixed = unstack_heads(dot(weight, value_cat[:, lanes]), masks)
            attended[SUB * sub : SUB * (sub + 1), lanes] = mixed.astype(BF16)

    attended_out[...] = attended[...]
    mid = tokens[0].astype(F32) + dot(attended[...], out_w[...]) + out_b[...]
    normed, scale = normalize(mid)
    low_second = (normed * gain2[...] + shift2[...]).astype(BF16)
    cot = cotangent[0]
    hidden = up_w.shape[1]
    mid_out[...] = mid
    second_out[...] = low_second
    for at in range(0, hidden, width):
        cols = slice(at, at + width)
        upper = dot(low_second, up_w[:, cols]) + up_b[:, cols]
        below, phi = normal_parts(upper)
        slope_out[:, cols] = below + upper * phi
        active = (upper * below).astype(BF16)
        active_out[:, cols] = active
        grad_down = dot_rows(active, cot).astype(BF16)
        for piece in range(at // 64, (at + width) // 64):
            row = 64 * piece - at
            for part in range(width // 128):
                sums[slot_of(piece), 64 * part : 64 * (part + 1)] = grad_down[
                    row : row + 64, 128 * part : 128 * (part + 1)
                ]
    small[...] = jnp.zeros_like(small)
    put_vector(small, 0, jnp.sum(cot.astype(F32), axis=0, keepdims=True))
    put_small(sums, 256, small)
    copies = hand_out(sums, keep, [send], sem)
    down_w.wait()
    for copy in copies:
        copy.wait()


def feed_kernel(
    cotangent, mid, low_second, slope, gain2, up_w, down_w, out_w, attended,
    grad_mid_out, grad_attended, grad_out, out_b_sum, keep, *refs,
):
    sends, (sums, small, sem) = refs[:-3], refs[-3:]
    cot = cotangent[0]
    hidden, width = down_w.shape
    grad_second = jnp.zeros((ROWS, width), F32)
    small[...] = jnp.zeros_like(small)
    for at in range(0, hidden, width):
        cols = slice(at, at + width)
        grad_upper = (dot_cols(cot, down_w[cols]) * slope[:, cols]).astype(BF16)
        put_vector(small, at // 128, jnp.sum(grad_upper.astype(F32), axis=0, keepdims=True))
        put_lines(sums, at // 8, dot_rows(low_second[...], grad_upper).astype(BF16))
        grad_second = grad_second + dot_cols(grad_upper, up_w[:, cols])
    normed, scale = normalize(mid[...])
    put_vector(small, 16, jnp.sum(grad_second * normed, axis=0, keepdims=True))
    put_vector(small, 20, jnp.sum(grad_second, axis=0, keepdims=True))
    put_small(sums, 256, small)
    copies = hand_out(sums, keep, sends, sem)
    grad_mid = cot.astype(F32) + norm_back(grad_second * gain2[...], normed, scale)
    grad_mid_out[...] = grad_mid
    branch = grad_mid.astype(BF16)
    grad_attended[...] = dot_cols(branch, out_w[...]).astype(BF16)
    grad_out[...] = dot_rows(attended[...], branch).astype(BF16)
    out_b_sum[...] = jnp.sum(branch.astype(F32), axis=0, keepdims=True)
    for copy in copies:
        copy.wait()


FEED, BACK, BORROWED, LAST = "feed", "back", "borrowed", "last"
ORDER = (FEED, 1, 2, BACK, 1, 2, 1, 3, 2, 1, BORROWED, 3, 2, 1, 3, 2, 1, 3, 2, 3, 1, 2, 3, LAST, 2, 1, 3, 3)
STEP_PARTS = 1
Z_DIRECT = True
GROUP_ROWS = 256 + SMALL
MID_PARTS, LATE_PARTS = 1, 3


def put_vector(small, row, vector):
    for part in range(vector.shape[1] // 128):
        small[row + part : row + part + 1] = vector[:, 128 * part : 128 * (part + 1)]


def turned(place):
    return (place & 4) * 2 + (place // 2 & 4) + (place & 3)


def slot_of(piece):
    mine, place = my_piece() % 16, piece % 16
    if piece // 16 == 1:
        mine, place = turned(mine), turned(place)
    return (piece // 16) * 16 + jnp.bitwise_xor(mine, place)


def put_lines(sums, base, grad):
    for piece in range(PIECES):
        slot = slot_of(piece)
        for part in range(grad.shape[1] // 128):
            row = base + 16 * part
            sums[slot, row : row + 16] = grad[
                16 * piece : 16 * (piece + 1), 128 * part : 128 * (part + 1)
            ]


def put_small(sums, row, small):
    for piece in range(PIECES):
        if piece < 2:
            part = small[SMALL * piece : SMALL * (piece + 1)].astype(BF16)
        else:
            part = jnp.zeros((SMALL, 128), BF16)
        sums[slot_of(piece), row : row + SMALL] = part


def row_bounds(rows, parts):
    return [16 * (rows // 16 * part // parts) for part in range(parts)] + [rows]


def hand_out(sums, keep, sends, sem, first=0, last=None):
    mine = my_piece() // 16
    half = PIECES // 2
    last = keep.shape[1] if last is None else last
    bounds = row_bounds(keep.shape[1], len(sends))
    copies = []
    for ref, core, low, high in [(keep, mine, 0, keep.shape[1])] + [
        (send, 1 - mine, low, high) for send, low, high in zip(sends, bounds, bounds[1:])
    ]:
        start, end = max(first, low), min(last, high)
        if start < end:
            copies.append(
                pltpu.make_async_copy(
                    sums.at[pl.ds(core * half, half), pl.ds(start, end - start)],
                    ref.at[:, pl.ds(start - low, end - start)],
                    sem.at[len(copies)],
                )
            )
    for copy in copies:
        copy.start()
    return copies


def back_kernel(
    levels, holders,
    tokens, normed_low, query, key, value, key_pool, value_pool, halo, key_halo, value_halo,
    weights, grad_attended, grad_out, out_b_sum, gain, shift, query_w, key_w, value_w,
    grad_normed_out, inner, outer, keep, *refs,
):
    sends, owners, refs = refs[:LATE_PARTS], refs[LATE_PARTS:-13], refs[-13:]
    (
    key_cat, value_cat, grad_query, key_own, key_pooled, key_lent, value_own, value_pooled,
    value_lent, sums, small, sem, rest_sem,
    ) = refs
    width = tokens.shape[2]
    place = lax.axis_index("seq")
    far = 48 * (levels - LOCAL)
    for ref in (key_own, key_pooled, key_lent, value_own, value_pooled, value_lent):
        ref[...] = jnp.zeros_like(ref)
    key_sums = {"own": key_own, "pool": key_pooled, "halo": key_lent}
    value_sums = {"own": value_own, "pool": value_pooled, "halo": value_lent}

    quad_cols = width * QUAD // HEADS
    masks = head_masks(quad_cols, SUB)
    for sub in range(ROWS // SUB):
        fill_keys(sub, levels, key_cat, key, key_pool, key_halo)
        fill_keys(sub, levels, value_cat, value, value_pool, value_halo)
        rows = slice(SUB * sub, SUB * (sub + 1))
        for quad in range(HEADS // QUAD):
            lanes = slice(quad * quad_cols, (quad + 1) * quad_cols)
            stacked = stack_heads(query[rows, lanes], masks)
            grads = stack_heads(grad_attended[rows, lanes], masks)
            weight = weights[sub * (HEADS // QUAD) + quad]
            prob = weight.astype(F32)
            dprob = dot_cols(grads, value_cat[:, lanes])
            delta = jnp.sum(prob * dprob, axis=1, keepdims=True)
            dscore = (prob * (dprob - delta)).astype(BF16)
            mixed = unstack_heads(dot(dscore, key_cat[:, lanes]), masks)
            grad_query[rows, lanes] = (mixed * 0.125).astype(BF16)
            grad_keys = dot_rows(dscore, stacked)
            grad_values = dot_rows(weight, grads)
            for column, count, source, row, _ in key_list(sub, levels):
                key_sums[source][row : row + count, lanes] += grad_keys[column : column + count]
                value_sums[source][row : row + count, lanes] += grad_values[
                    column : column + count
                ]

    low_query = grad_query[...]
    pool = pool_matrix(levels, POOLED)
    low_key = (key_own[...] + dot_rows(pool, key_pooled[...].astype(BF16))).astype(BF16)
    low_value = (value_own[...] + dot_rows(pool, value_pooled[...].astype(BF16))).astype(BF16)
    lent_key = key_lent[...].astype(BF16)
    lent_value = value_lent[...].astype(BF16)
    lent_normed = halo[...].astype(F32)
    lent_low = (lent_normed * gain[...] + shift[...]).astype(BF16)
    rows = normed_low[...]

    put_lines(sums, 0, grad_out[...])
    put_lines(sums, 64, dot_rows(rows, low_query).astype(BF16))
    grad_key = dot_rows(rows, low_key) + dot_rows(lent_low, lent_key)
    put_lines(sums, 128, grad_key.astype(BF16))
    grad_value = dot_rows(rows, low_value) + dot_rows(lent_low, lent_value)
    put_lines(sums, 192, grad_value.astype(BF16))
    copies = hand_out(sums, keep, sends, sem, last=256)
    small[...] = jnp.zeros_like(small)

    def total(values):
        return jnp.sum(values.astype(F32), axis=0, keepdims=True)

    normed, _ = normalize(tokens[0].astype(F32))
    grad_normed = (
        dot_cols(low_query, query_w[...])
        + dot_cols(low_key, key_w[...])
        + dot_cols(low_value, value_w[...])
    )
    lent_grad = dot_cols(lent_key, key_w[...]) + dot_cols(lent_value, value_w[...])
    grad_normed_out[...] = grad_normed
    put_vector(small, 0, total(low_query))
    put_vector(small, 4, total(low_value) + total(lent_value))
    put_vector(small, 8, out_b_sum[...])
    put_vector(small, 12, total(grad_normed * normed) + total(lent_grad * lent_normed))
    put_vector(small, 16, total(grad_normed) + total(lent_grad))
    lent_grad = lent_grad.astype(BF16)
    even = place % 2 == 0
    inner[...] = jnp.where(even, lent_grad[HALO : 2 * HALO], lent_grad[:HALO])
    outer[...] = jnp.where(even, lent_grad[:HALO], lent_grad[HALO : 2 * HALO])
    pick = pick_matrix(place, levels, holders)
    returned = dot_rows(pick, lent_grad[2 * HALO :]).astype(BF16)
    if owners:
        owners[0][...] = returned
    else:
        for plane in range(4):
            for other in range(2):
                core = (place + other) % 2
                at = jnp.where(core == 1, turned(4 * plane), 4 * plane)
                rows = returned[GATHER * (2 * plane + other) :][:GATHER]
                for part in range(4):
                    slot = core * 16 + at + part
                    sums[slot, GROUP_ROWS:] = rows[:, 128 * part : 128 * (part + 1)]
    put_small(sums, 256, small)
    copies += hand_out(sums, keep, sends, rest_sem, first=256)
    for copy in copies:
        copy.wait()


def last_kernel(
    levels, tokens, gain, grad_mid, grad_normed, inner, outer, mid, active, down_w, down_b, *refs
):
    from_users, (grad_tokens, output, pooled) = refs[:-3], refs[-3:]
    output[0] = (mid[...] + dot(active[...], down_w[...]) + down_b[...]).astype(BF16)
    even = lax.axis_index("seq") % 2 == 0
    first = jnp.where(even, outer[...], inner[0:HALO]).astype(F32)
    last = jnp.where(even, inner[0:HALO], outer[...]).astype(F32)
    for level in range(1, LOCAL + 1):
        at, width = HALO_AT[level]
        base, own = POOL_AT[level], level_rows(level)
        pooled[base : base + own] = jnp.zeros((own, pooled.shape[1]), F32)
        pooled[base : base + width] += first[at : at + width]
        pooled[base + own - width : base + own] += last[at : at + width]
    if len(from_users) > 1:
        pooled[POOLED:] = functools.reduce(jnp.add, [ref[...].astype(F32) for ref in from_users])
    else:
        for part in range(4):
            pooled[POOLED:, 128 * part : 128 * (part + 1)] = from_users[0][part].astype(F32)
    high, low = two_parts(pooled[...])
    pool = pool_matrix(levels)
    gap = jnp.zeros((ROWS - 32, first.shape[1]), F32)
    grad = grad_normed[...] + dot_rows(pool, high) + dot_rows(pool, low)
    grad = grad + jnp.concatenate([first[:16], gap, last[:16]], axis=0)
    normed, scale = normalize(tokens[0].astype(F32))
    grad_tokens[0] = grad_mid[...] + norm_back(grad * gain[...], normed, scale)


def collect_kernel(kind, *refs):
    blocks, refs, small = refs[:4], refs[4:-1], refs[-1]
    me = my_piece()
    squares = 4 if kind == 2 else 1
    grads, order = refs[:squares], refs[squares:]

    for core in range(2):
        odd = (me // 16 + core) % 2 == 1
        for plane in range(4):
            for depth in range(4):
                place = 4 * plane + depth
                place = jnp.where(odd, turned(place), place)
                piece = jnp.bitwise_xor(me, core * 16 + place)
                block = blocks[2 * core + plane % 2]

                def held(row, rows, block=block, plane=plane, depth=depth):
                    return block[plane // 2, depth, row : row + rows].astype(F32)

                lines = pl.ds(pl.multiple_of(piece * 16, 16), 16)
                if kind == 0:
                    (down,) = grads
                    rows = pl.ds(pl.multiple_of(piece * 64, 64), 64)
                    for part in range(down.shape[1] // 128):
                        down[rows, 128 * part : 128 * (part + 1)] = held(64 * part, 64)
                else:
                    base = 0
                    for grad in grads:
                        for part in range(grad.shape[1] // 128):
                            grad[lines, 128 * part : 128 * (part + 1)] = held(base, 16)
                            base += 16

                @pl.when(piece < 2)
                def _(held=held, lines=lines):
                    small[lines] = held(256, SMALL)

    at = 0
    for ref in order:
        ref[...] = small[at : at + ref.shape[0]]
        at += ref.shape[0]


class Fetched:
    def __init__(self, ref, copy):
        self.ref = ref
        self.copy = copy
        self.shape = ref.shape

    def wait(self):
        if self.copy is not None:
            self.copy.wait()
            self.copy = None

    def __getitem__(self, at):
        self.wait()
        return self.ref[at]


def call(
    kernel, inputs, outputs, scratch=(), smem=0, room=16, far_in=(), far_out=(), alias=None, pinned=()
):
    inputs = list(inputs)
    in_space = [pltpu.SMEM] * smem + [pltpu.VMEM] * (len(inputs) - smem)
    out_space = [pltpu.VMEM] * len(outputs)
    for at in far_in:
        in_space[at] = pl.ANY
    for at in pinned:
        inputs[at] = pltpu.with_memory_space_constraint(inputs[at], pltpu.HBM)
        in_space[at] = pltpu.HBM
    for at in far_out:
        out_space[at] = pl.ANY
    return pl.pallas_call(
        kernel,
        out_shape=[jax.ShapeDtypeStruct(s, d) for s, d in outputs],
        in_specs=[pl.BlockSpec(memory_space=s) for s in in_space],
        out_specs=[pl.BlockSpec(memory_space=s) for s in out_space],
        scratch_shapes=[pltpu.VMEM(*s) if isinstance(s, tuple) else s for s in scratch],
        input_output_aliases=alias or {},
        compiler_params=pltpu.CompilerParams(vmem_limit_bytes=room * 1024 * 1024),
        cost_estimate=pl.CostEstimate(flops=0, bytes_accessed=0, transcendentals=0),
    )(*inputs)


def swap(array, axis, distance):
    count = lax.axis_size(axis)
    return lax.ppermute(array, axis, [(i, i ^ distance) for i in range(count)])


def swap_outer(array, axis):
    count = lax.axis_size(axis)
    pairs = [(i, i + 1) for i in range(1, count - 1, 2)]
    return lax.ppermute(array, axis, pairs + [(j, i) for i, j in pairs])


def after(value, *others):
    return lax.optimization_barrier((value, others))[0]


def planes(array):
    return [swap(array, "seq", 2 * plane) for plane in (3, 1, 2)]


def hop(array, step):
    pairs = []
    for place in range(lax.axis_size("seq")):
        bit = 2 << (step if place % 2 == 0 else 1 - step)
        pairs.append((place, place ^ bit))
    return lax.ppermute(array, "seq", pairs)


def sum_of(*values):
    total = values[0].astype(F32)
    for value in values[1:]:
        total = total + value.astype(F32)
    return total.astype(BF16)


def halves_kernel(count, kept, *refs):
    came, (kept_out, *sends) = refs[:count], refs[count:]
    for slot in range(kept.shape[0]):
        first = 0
        for ref in came:
            last = first + ref.shape[-2]
            total = sum_of(kept[slot, ..., first:last, :], ref[slot])
            if slot % 2 == 0:
                kept_out[slot // 2, ..., first:last, :] = total
            else:
                row = 0
                for send in sends:
                    end = row + send.shape[-2]
                    low, high = max(first, row), min(last, end)
                    if low < high:
                        send[slot // 2, ..., low - row : high - row, :] = total[
                            ..., low - first : high - first, :
                        ]
                    row = end
            first = last


def add_halves(kept, *came, parts=1):
    half, rows = (kept.shape[0] // 2, *kept.shape[1:-2]), kept.shape[-2]
    bounds = row_bounds(rows, parts)
    sends = [((*half, last - first, 128), BF16) for first, last in zip(bounds, bounds[1:])]
    kernel = functools.partial(halves_kernel, len(came))
    kept, *sends = call(kernel, (kept, *came), [((*half, rows, 128), BF16), *sends], room=12)
    return (sends[0] if parts == 1 else sends), kept


def plane_kernel(extra, kept, came, sent_out, kept_out, *complete):
    rows = kept.shape[1] - extra
    for depth in range(4):
        total = sum_of(kept[depth], came[depth])
        (kept_out, sent_out)[depth % 2][depth // 2] = total[:rows]
        if extra:
            complete[0][depth] = total[rows:]


def add_plane(kept, came, extra):
    rows = kept.shape[1] - extra
    outputs = [((2, rows, 128), BF16)] * 2
    if extra:
        outputs.append(((4, extra, 128), BF16))
    return call(functools.partial(plane_kernel, extra), (kept, came), outputs, room=8)


def plane_direct_kernel(extra, kept, came, *outs):
    rows = kept.shape[1] - extra
    for depth in range(4):
        total = sum_of(kept[depth], came[depth])
        outs[depth][...] = total[:rows]
        if extra:
            outs[4][depth] = total[rows:]


def add_plane_direct(kept, came, extra):
    rows = kept.shape[1] - extra
    outputs = [((rows, 128), BF16)] * 4
    if extra:
        outputs.append(((4, extra, 128), BF16))
    outs = call(functools.partial(plane_direct_kernel, extra), (kept, came), outputs, room=8)
    return [*outs[:4], list(outs[4:])]


def column_kernel(whole, two, three, one, out):
    for depth, ref in enumerate((whole, one, two, three)):
        out[0, depth] = ref[...]


def column_of(whole, came):
    (column,) = call(column_kernel, (whole, *came), [((1, 4, *whole.shape), BF16)], room=8)
    return column


def whole_kernel(*refs):
    refs[-1][...] = sum_of(*[ref[...] for ref in refs[:-1]])


def add_whole(mine, *came):
    (whole,) = call(whole_kernel, (mine, *came), [(mine.shape, BF16)], room=8)
    distance = 8
    while distance < lax.axis_size("seq"):
        other = swap(whole, "seq", distance)
        (whole,) = call(whole_kernel, (whole, other), [(mine.shape, BF16)], room=8)
        distance *= 2
    return whole


def joined_kernel(mine, came, out):
    for slot in range(mine.shape[0]):
        out[2 * slot] = mine[slot]
        out[2 * slot + 1] = came[slot]


def join(mine, came):
    (out,) = call(joined_kernel, (mine, came), [((2 * mine.shape[0], *mine.shape[1:]), BF16)], room=8)
    return out


class Group:
    def __init__(self, keep, sends, parts=1):
        self.kept = slots(keep)
        self.parts = parts
        self.came = [slots(swap(send, "seq", 1)) for send in sends]
        self.stage = 0
        self.users = []

    def step(self, last, extra):
        stage, kept = self.stage, self.kept
        came = after(self.came, last)
        self.stage += 1
        if stage == 0:
            sent, self.kept = add_halves(kept, *came, parts=self.parts)
            self.came = hop(sent, 0) if self.parts == 1 else [hop(part, 0) for part in sent]
        elif stage == 1:
            sent, kept = add_halves(kept, *(came if self.parts > 1 else [came]))
            self.kept = kept[0]
            self.came = hop(sent[0], 1)
        elif stage == 2 and Z_DIRECT:
            *self.kept, self.users = add_plane_direct(kept, came, extra)
            self.came = [swap(self.kept[depth], "batch", depth) for depth in (2, 3, 1)]
            self.stage = 4
        elif stage == 4 and Z_DIRECT:
            self.kept = add_whole(kept[0], *came)
            self.came = [swap(self.kept, "batch", depth) for depth in (2, 3, 1)]
            self.stage = 6
        elif stage == 6 and Z_DIRECT:
            self.kept = column_of(kept, came)
            self.came = hop(self.kept, 1)
        elif stage == 2:
            sent, self.kept, *self.users = add_plane(kept, came, extra)
            self.came = swap(sent, "batch", 1)
        elif stage == 3:
            sent, kept = add_halves(kept, came)
            self.kept = kept[0]
            self.came = swap(sent[0], "batch", 2)
        elif stage == 4:
            self.kept = add_whole(kept, came)[None]
            self.came = swap(self.kept, "batch", 2)
        elif stage == 5:
            self.kept = join(kept, came)
            self.came = swap(self.kept, "batch", 1)
        elif stage == 6:
            self.kept = join(kept, came)[None]
            self.came = hop(self.kept, 1)
        elif stage == 7:
            self.kept = join(kept, came)
            self.came = hop(self.kept, 0)
        else:
            self.sums = [kept, came]
            self.sums += [swap(block, "seq", 1) for block in self.sums]
            return came
        return self.kept[0] if isinstance(self.kept, list) else self.kept


def slots(array):
    return array.reshape(-1, 4, *array.shape[1:])


def plane_of(column, came):
    return [column, came[1], came[2], came[0]]


def chip_kernel(inner, came, chip):
    chip[0:GATHER] = inner[HALO:]
    chip[GATHER:] = came[HALO:]


def share(inner, came):
    if not direct(lax.axis_size("seq")):
        return [lax.all_gather(inner[HALO:], "seq", axis=0, tiled=True)]
    (chip,) = call(chip_kernel, (inner, came), [((2 * GATHER, inner.shape[1]), BF16)], room=8)
    return plane_of(chip, planes(chip))


def on_device(
    tokens, cotangent, item_start, first_gain, first_shift, query_weight, query_bias, key_weight,
    value_weight, value_bias, out_weight, out_bias, second_gain, second_shift, up_weight, up_bias,
    down_weight, down_bias,
):
    width = tokens.shape[2]
    hidden = up_weight.shape[1]
    holders = lax.axis_size("seq")
    levels = (ROWS * holders // (4 * BLOCK)).bit_length() - 1
    far = 48 * (levels - LOCAL)
    lent = 2 * HALO + far

    cols = columns_of(levels)
    groups = (ROWS // SUB) * (HEADS // QUAD)
    bias_table = jnp.asarray(score_bias(levels))
    codes = jnp.asarray(column_codes(levels))

    def row(vector):
        return vector.reshape(1, -1)

    gain, shift = row(first_gain), row(first_shift)
    inner, outer = call(
        functools.partial(first_kernel, levels),
        (tokens,),
        [((HALO + GATHER, width), BF16), ((HALO, width), BF16)],
        room=8,
    )
    inner_came = swap(inner, "seq", 1)
    outer_came = swap_outer(outer, "seq")
    windows = share(inner, inner_came)
    carried = (
        tokens, gain, shift, query_weight, row(query_bias), key_weight, value_weight,
        row(value_bias), row(out_bias), row(second_gain), row(second_shift), row(up_bias),
        row(down_bias), bias_table, codes,
    )
    count = len(carried)
    *carried, normed_low, query, key, value, key_pool, value_pool = call(
        functools.partial(project_kernel, levels, count),
        carried,
        [(a.shape, a.dtype) for a in carried]
        + [((ROWS, width), BF16)] * 4
        + [((POOLED, width), BF16)] * 2,
        scratch=[pltpu.SemaphoreType.DMA((count,))],
        pinned=range(count),
        room=24,
    )
    (
        tokens, gain, shift, query_weight, _, key_weight, value_weight, value_bias, out_bias,
        second_gain, second_shift, up_bias, down_bias, bias_table, codes,
    ) = carried
    extra = extra_rows(holders)
    owner_shapes = [] if extra else [((holders * GATHER, width), BF16)]
    half = PIECES // 2
    copies = pltpu.SemaphoreType.DMA((1 + max(MID_PARTS, LATE_PARTS),))

    def piece_sums(parts, rows=GROUP_ROWS):
        bounds = row_bounds(rows, parts)
        sends = [((half, last - first, 128), BF16) for first, last in zip(bounds, bounds[1:])]
        return [((half, rows, 128), BF16)] + sends

    sums_scratch = ((PIECES, GROUP_ROWS, 128), BF16)
    small_scratch = ((2 * SMALL, 128), F32)
    (
        attended, weights, halo, key_halo, value_halo, mid, low_second, active, slope, keep, send,
        out_weight, up_weight, cotangent, down_weight,
    ) = call(
        functools.partial(middle_kernel, levels, holders, len(windows)),
        (
            item_start, tokens, query, key, value, key_pool, value_pool, inner_came, outer_came,
            gain, shift, key_weight, value_weight, value_bias, out_bias, second_gain, second_shift,
            up_bias, bias_table, codes, out_weight, up_weight, cotangent, down_weight, *windows,
        ),
        [
            ((ROWS, width), BF16),
            ((groups, QUAD * SUB, cols), BF16),
            ((lent, width), BF16),
            ((lent, width), BF16),
            ((lent, width), BF16),
            ((ROWS, width), F32),
            ((ROWS, width), BF16),
            ((ROWS, hidden), BF16),
            ((ROWS, hidden), F32),
        ]
        + piece_sums(1)
        + [(a.shape, a.dtype) for a in (out_weight, up_weight, cotangent, down_weight)],
        scratch=[
            ((cols, width), BF16),
            ((cols, width), BF16),
            ((ROWS, width), BF16),
            sums_scratch,
            small_scratch,
            copies,
            pltpu.SemaphoreType.DMA((4,)),
        ],
        smem=1,
        far_in=(20, 21, 22, 23),
        pinned=(20, 21, 22, 23),
        far_out=(9, 10),
        room=24,
    )
    lines = width // 128
    small = ((lines, 128), F32)
    square = ((width, width), F32)
    collected = {
        1: [((hidden, width), F32), small],
        2: [((width, hidden), F32), ((hidden // 128, 128), F32), small, small],
        3: [square] * 4 + [small] * 5,
    }
    sums = {1: Group(keep, [send])}
    done = {}
    last = ()
    for what in ORDER:
        if what == FEED:
            grad_mid, grad_attended, grad_out, out_b_sum, keep, *sends = call(
                feed_kernel,
                (
                    cotangent, after(mid, last), low_second, slope, second_gain, up_weight, down_weight,
                    out_weight, attended,
                ),
                [
                    ((ROWS, width), F32),
                    ((ROWS, width), BF16),
                    ((width, width), BF16),
                    ((1, width), F32),
                ]
                + piece_sums(MID_PARTS),
                scratch=[sums_scratch, small_scratch, copies],
                far_out=range(4, 5 + MID_PARTS),
                room=24,
            )
            sums[2] = Group(keep, sends)
            last = grad_attended
        elif what == BACK:
            grad_normed, inner, outer, keep, *sends = call(
                functools.partial(back_kernel, levels, holders),
                (
                    tokens, normed_low, after(query, last), key, value, key_pool, value_pool, halo, key_halo,
                    value_halo, weights, grad_attended, grad_out, out_b_sum, gain, shift, query_weight,
                    key_weight, value_weight,
                ),
                [
                    ((ROWS, width), F32),
                    ((HALO, width), BF16),
                    ((HALO, width), BF16),
                ]
                + piece_sums(LATE_PARTS, GROUP_ROWS + extra)
                + owner_shapes,
                scratch=[
                    ((cols, width), BF16),
                    ((cols, width), BF16),
                    ((ROWS, width), BF16),
                    ((ROWS, width), F32),
                    ((POOLED, width), F32),
                    ((lent, width), F32),
                    ((ROWS, width), F32),
                    ((POOLED, width), F32),
                    ((lent, width), F32),
                    ((PIECES, GROUP_ROWS + extra, 128), BF16),
                    small_scratch,
                    copies,
                    copies,
                ],
                far_out=range(3, 4 + LATE_PARTS),
                room=28,
            )
            sends, owners = sends[:LATE_PARTS], sends[LATE_PARTS:]
            sums[3] = Group(keep, sends, STEP_PARTS)
            inner_came = swap(inner, "seq", 1)
            outer_came = swap_outer(outer, "seq")
            last = grad_normed
        elif what == LAST:
            users = sums[3].users
            if not extra:
                rows = owners[0].reshape(holders, GATHER, width)
                users = list(lax.all_to_all(rows, "seq", split_axis=0, concat_axis=0, tiled=True))
            grad_tokens, output = call(
                functools.partial(last_kernel, levels),
                (
                    tokens, gain, grad_mid, after(grad_normed, last), inner_came, outer_came, mid,
                    active, down_weight, down_bias, *users,
                ),
                [((1, ROWS, width), F32), ((1, ROWS, width), BF16)],
                scratch=[((ROWS, width), F32)],
                room=12,
            )
            last = grad_tokens
        elif what == BORROWED:
            inner_came, outer_came = after((inner_came, outer_came), last)
            last = (inner_came, outer_came)
        elif sums[what].stage < 9:
            last = sums[what].step(last, extra if what == 3 else 0)
        else:
            done[what] = call(
                functools.partial(collect_kernel, what - 1),
                after(sums[what].sums, last),
                collected[what],
                scratch=[((PIECES * SMALL, 128), F32)],
                room=16,
            )
            last = done[what][-1]
    down, down_b = done[1]
    up, up_b, gain2, shift2 = done[2]
    out_w, query_w, key_w, value_w, query_b, value_b, out_b, gain1, shift1 = done[3]
    vectors = [query_b, value_b, out_b, up_b, down_b, gain1, shift1, gain2, shift2]
    return (output, grad_tokens, query_w, key_w, value_w, out_w, up, down) + tuple(
        vector.reshape(-1) for vector in vectors
    )


def solution(mesh):
    cut = P("batch", "seq", None)
    in_specs = (cut, cut, P("batch", None)) + (P(),) * 15
    out_specs = (cut, cut) + (P(),) * 15
    return jax.shard_map(
        on_device, mesh=mesh, in_specs=in_specs, out_specs=out_specs, check_vma=False
    )
```
